32 devices in a mesh: fsdp: 32 (over z, y, x, core).
Axes of the slice: x: 2, y: 2, z: 4, core: 2. Of those that a mesh axis runs over, the one named last changes fastest.
Arguments:
- tokens: bfloat16 [4096, 2048], P('fsdp'), may hold values from -6 to 6
- cotangent: bfloat16 [4096, 2048], P('fsdp'), may hold values from -6 to 6
- lengths: int32 [32, 4], P('fsdp'), may hold values from 1 to 64, 128 in all within a row
- routes: int32 [4096, 8], P('fsdp'), may hold values from 0 to 31, all different within a row; in each aligned block of 128 rows (0 to 127, 128 to 255, ...) at most 40 rows name the same one
- query_weight: bfloat16 [2048, 4096], P('fsdp'), may hold values from -0.125 to 0.125
- key_matrix: bfloat16 [2048, 512], P('fsdp'), may hold values from -0.125 to 0.125
- value_matrix: bfloat16 [2048, 512], P('fsdp'), may hold values from -0.125 to 0.125
- out_weight: bfloat16 [4096, 2048], P('fsdp'), may hold values from -0.375 to 0.375
- router_weight: bfloat16 [2048, 32], P('fsdp'), may hold values from -0.0625 to 0.0625
- expert_gate: bfloat16 [32, 2048, 768], P('fsdp'), may hold values from -0.125 to 0.125
- expert_up: bfloat16 [32, 2048, 768], P('fsdp'), may hold values from -0.125 to 0.125
- expert_down: bfloat16 [32, 768, 2048], P('fsdp'), may hold values from -0.875 to 0.875
- first_gain: float32 [2048], replicated, may hold values from 0.25 to 1.75
- second_gain: float32 [2048], replicated, may hold values from 0.25 to 1.75
- query_norm_gain: float32 [128], replicated, may hold values from 1 to 2
- key_gain: float32 [128], replicated, may hold values from 1 to 2
Outputs:
- output: bfloat16 [4096, 2048], P('fsdp')
- tokens_grad: float32 [4096, 2048], P('fsdp')
- query_grad: float32 [2048, 4096], P('fsdp')
- key_grad: float32 [2048, 512], P('fsdp')
- value_grad: float32 [2048, 512], P('fsdp')
- out_grad: float32 [4096, 2048], P('fsdp')
- router_grad: float32 [2048, 32], P('fsdp')
- gate_grad: float32 [32, 2048, 768], P('fsdp')
- up_grad: float32 [32, 2048, 768], P('fsdp')
- down_grad: float32 [32, 768, 2048], P('fsdp')
- first_gain_grad: float32 [2048], replicated
- second_gain_grad: float32 [2048], replicated
- query_gain_grad: float32 [128], replicated
- key_gain_grad: float32 [128], replicated
The draws below stay inside these ranges and needn't reach their ends.
Inputs may be any that keep to these rules, and one draw needn't show every extreme that they name: `routes`: in each aligned block of 128 rows (the rows of one device) no expert is named by more than 40 rows. Each row of 4 lengths sums to 128.
All inputs are finite; a program needn't handle non-finite values.
Results may differ from the reference program's by a relative error of at most 0.015.
The reference program's roundings to bfloat16 on the way count: a program that leaves them out, or rounds other values in their place, can miss the bound.
Values may be sent and summed in bfloat16 or wider, within the bound.
No kernel may reach another device: no remote copies, remote signals or barrier semaphores. Data moves between devices by JAX's collectives and lax.ppermute only.
A program may use at most 320 MiB of HBM per device.

```python
import functools
import math
import jax
import jax.numpy as jnp
import numpy as np
from jax import lax

MODEL_WIDTH = 2048
QUERY_HEADS = 32
KEY_VALUE_HEADS = 4
HEAD_SIZE = 128
FFE = 768
TOPK = 8
TOK_DEV = 128
SEQ_DEV = 4
EXPERTS = 32
SHARDS = 32
TOKENS = 4096
CAP = 40
N_FSDP = 32


def level_of(key, shape, cuts, low, top_value):
    loudness, own = 1.0, jax.random.fold_in(key, 6)
    for dim, shards_of in cuts:
        heights = jnp.exp(jax.random.uniform(jax.random.fold_in(own, dim), (shards_of,), jnp.float32, low / len(cuts), top_value / len(cuts)))
        loudness = loudness * jnp.repeat(heights, shape[dim] // shards_of).reshape([-1 if axis == dim else 1 for axis in range(len(shape))])
    return loudness


def length_profile(amount, total, most, slope):
    weights = [(1 << 20) // math.isqrt(grade ** slope) + 1 for grade in range(2, amount + 1)]
    spare, counts = total - most - (amount - 1), [1] * (amount - 1)
    while spare > 0:
        movable = [i for i in range(amount - 1) if counts[i] < most]
        mass, remaining = sum([weights[i] for i in movable]), spare
        for i in movable:
            more = min(most - counts[i], max(1, remaining * weights[i] // mass), spare)
            counts[i] = counts[i] + more
            spare = spare - more
    return np.array([most] + counts)


def ragged_sizes(stream_key, count, total, limit, lean):
    if count == 2:
        one = jax.random.randint(stream_key, (), max(1, total - limit), min(limit, total - 1) + 1)
        return jnp.stack([one, total - one])
    tallies = jnp.asarray(length_profile(count, total, limit, lean), jnp.int32)
    twos = (count - 1) // 2
    source_of, taker = tallies[1:1 + 2 * twos:2], tallies[2:2 + 2 * twos:2]
    room = jnp.minimum(source_of - 1, limit - taker)
    passed = jax.random.randint(jax.random.fold_in(stream_key, 1), (twos,), 0, 1 << 20) % (room + 1)
    tallies = tallies.at[1:1 + 2 * twos:2].set(source_of - passed).at[2:2 + 2 * twos:2].set(taker + passed)
    return tallies[jax.random.permutation(jax.random.fold_in(stream_key, 2), count)]


def deal_out(rng, own, number, rows, number_of, top, limit, skew):
    ranking = jax.random.permutation(rng, number_of)
    crowded, ordinary = portions_of(number_of, rows * top, limit, skew, True), portions_of(number_of, rows * top, limit, skew, False)
    places = jnp.arange(number_of)

    def named(sizes, rotation):
        used = int((sizes > 0).sum())
        fixed = max(1, used // 4)
        passed = fixed + (places - fixed + rotation * (used - fixed)) % max(1, number_of - fixed)
        return jnp.zeros((number_of,), jnp.int32).at[ranking[jnp.where(places < fixed, places, passed)]].set(jnp.asarray(sizes, jnp.int32))

    sizes = jnp.where(number % 4 == 0, named(crowded, number // 4), named(ordinary, number - number // 4 - 1))
    mixed = jax.random.permutation(jax.random.fold_in(own, 3), number_of)
    donor, receiver = mixed[0:number_of // 2 * 2:2], mixed[1:number_of // 2 * 2:2]
    room = jnp.minimum(sizes[donor] - 1, limit - sizes[receiver]) // 2
    room = jnp.where((donor == ranking[0]) | (receiver == ranking[0]) | (sizes[receiver] == 0), 0, jnp.maximum(room, 0))
    passed = jax.random.randint(jax.random.fold_in(own, 4), (number_of // 2,), 0, 1 << 20) % (room + 1)
    sizes = sizes.at[donor].add(-passed).at[receiver].add(passed)
    items = jnp.searchsorted(jnp.cumsum(sizes), jnp.arange(rows * top), side="right").astype(jnp.int32)
    listing = items.reshape(top, rows).T
    listing = listing[jax.random.permutation(jax.random.fold_in(own, 1), rows)]
    rotation = jax.random.randint(jax.random.fold_in(own, 2), (rows, 1), 0, top)
    return jnp.take_along_axis(listing, (jnp.arange(top)[None, :] + rotation) % top, axis=1)


def portions_of(amount, total, limit, slope, full):
    weights = [(1 << 20) // math.isqrt(standing ** slope) + 1 for standing in range(1, amount + 1)]
    largest = limit if full else min(limit, max(-(-total // amount), total * weights[0] // sum(weights)))
    least = 1 if total - largest >= amount - 1 else 0
    holding, rest = [largest] + [least] * (amount - 1), total - largest - least * (amount - 1)
    while rest > 0:
        candidates = [i for i in range(1, amount) if holding[i] < largest] or [i for i in range(1, amount) if holding[i] < limit]
        mass, remaining = sum([weights[i] for i in candidates]), rest
        for i in candidates:
            extra = min(limit - holding[i], max(1, remaining * weights[i] // mass), rest)
            holding[i] = holding[i] + extra
            rest = rest - extra
    return np.array(holding)


def noise(stream_key, shape, deviation, bound, split=(), kind=jnp.bfloat16):
    factor_of = level_of(stream_key, shape, split, -0.22, 0.18) if split else 1.0
    values = jax.random.normal(stream_key, shape, jnp.float32) * deviation * factor_of
    return jnp.minimum(jnp.maximum(values, -bound), bound).astype(kind)


def setup_inputs(seed: int = 0) -> dict:
    arg_keys = jax.random.split(jax.random.key(seed), 17)
    tokens = noise(arg_keys[0], (TOKENS, MODEL_WIDTH), 1.0, 6.0, ((0, 32),))
    cotangent = noise(arg_keys[1], (TOKENS, MODEL_WIDTH), 1.0, 6.0, ((0, 32),))
    lengths = jax.vmap(lambda own: ragged_sizes(own, SEQ_DEV, TOK_DEV, TOK_DEV // 2, 2))(jax.random.split(arg_keys[2], SHARDS)).reshape((SHARDS, SEQ_DEV)).astype(jnp.int32)
    routes_keys = jax.random.split(jax.random.fold_in(arg_keys[3], 1), TOKENS // TOK_DEV)
    routes_turns = jax.random.permutation(jax.random.fold_in(arg_keys[3], 3), TOKENS // TOK_DEV)
    routes = jax.vmap(lambda own, number: deal_out(jax.random.fold_in(arg_keys[3], 2), own, number, TOK_DEV, EXPERTS, TOPK, CAP, 2))(routes_keys, routes_turns).reshape((TOKENS, TOPK))
    query_weight = noise(arg_keys[4], (MODEL_WIDTH, QUERY_HEADS * HEAD_SIZE), MODEL_WIDTH ** -0.5, 0.125, ((0, 32),))
    key_matrix = noise(arg_keys[5], (MODEL_WIDTH, KEY_VALUE_HEADS * HEAD_SIZE), MODEL_WIDTH ** -0.5, 0.125, ((0, 32),))
    value_matrix = noise(arg_keys[6], (MODEL_WIDTH, KEY_VALUE_HEADS * HEAD_SIZE), MODEL_WIDTH ** -0.5, 0.125, ((0, 32),))
    out_weight = noise(arg_keys[7], (QUERY_HEADS * HEAD_SIZE, MODEL_WIDTH), (QUERY_HEADS * HEAD_SIZE // 16) ** -0.5, 0.375, ((0, 32),))
    router_weight = noise(arg_keys[8], (MODEL_WIDTH, EXPERTS), (4 * MODEL_WIDTH) ** -0.5, 0.0625, ((0, 32),))
    expert_gate = noise(arg_keys[9], (EXPERTS, MODEL_WIDTH, FFE), MODEL_WIDTH ** -0.5, 0.125, ((0, 32),))
    expert_up = noise(arg_keys[10], (EXPERTS, MODEL_WIDTH, FFE), MODEL_WIDTH ** -0.5, 0.125, ((0, 32),))
    expert_down = noise(arg_keys[11], (EXPERTS, FFE, MODEL_WIDTH), (FFE // 16) ** -0.5, 0.875, ((0, 32),))
    first_gain = jnp.clip(1.0 + 0.15 * jax.random.normal(arg_keys[12], (MODEL_WIDTH,), jnp.float32), 0.25, 1.75)
    second_gain = jnp.clip(1.0 + 0.15 * jax.random.normal(arg_keys[13], (MODEL_WIDTH,), jnp.float32), 0.25, 1.75)
    query_norm_gain = jnp.clip(jnp.exp(jax.random.uniform(arg_keys[14], (HEAD_SIZE,), jnp.float32, math.log(1.0), math.log(2.0))), 1.0, 2.0)
    key_gain = jnp.clip(jnp.exp(jax.random.uniform(arg_keys[15], (HEAD_SIZE,), jnp.float32, math.log(1.0), math.log(2.0))), 1.0, 2.0)
    return dict(tokens=tokens, cotangent=cotangent, lengths=lengths, routes=routes, query_weight=query_weight, key_matrix=key_matrix, value_matrix=value_matrix, out_weight=out_weight, router_weight=router_weight, expert_gate=expert_gate, expert_up=expert_up, expert_down=expert_down, first_gain=first_gain, second_gain=second_gain, query_norm_gain=query_norm_gain, key_gain=key_gain)


EPS = 1e-06
THETA = 1000000.0
NEGATIVE = -1e+30
HIGH = lax.Precision.HIGHEST

@jax.custom_vjp
def lower_precision(v):
    return lax.optimization_barrier(v.astype(jnp.bfloat16)).astype(jnp.float32)

@jax.custom_vjp
def lower_precision_backward(v):
    return v

def low_keep(v):
    return (lower_precision(v), None)

def low_pass(kept, grad):
    return (grad,)

def back_keep(v):
    return (v, None)

def back_low(kept, grad):
    return (lower_precision(grad),)
lower_precision.defvjp(low_keep, low_pass)
lower_precision_backward.defvjp(back_keep, back_low)

def product_highest(left, right):
    return jnp.dot(left, right, precision=HIGH, preferred_element_type=jnp.float32)

def root_mean_square_norm(value_rows, gain):
    return value_rows * lax.rsqrt(lax.optimization_barrier(jnp.mean(value_rows * value_rows, axis=-1, keepdims=True)) + EPS) * gain

def sequence_layout(lengths, count_total):
    ends = jnp.cumsum(lengths).astype(jnp.int32)
    starts = (ends - lengths).astype(jnp.int32)
    places = jnp.arange(count_total, dtype=jnp.int32)
    member = ((places[:, None] >= starts[None, :]) & (places[:, None] < ends[None, :])).astype(jnp.int32)
    labels = jnp.arange(lengths.shape[0], dtype=jnp.int32)
    segment = lax.optimization_barrier(jnp.sum(member * labels[None, :], axis=1)).astype(jnp.int32)
    offset = lax.optimization_barrier(jnp.sum(member * starts[None, :], axis=1)).astype(jnp.int32)
    return (segment, (places - offset).astype(jnp.int32))

def rotary_tables(position, width):
    half = width // 2
    inverse = jnp.power(THETA, -(jnp.arange(half, dtype=jnp.float32) * 2.0) / width)
    angle = position.astype(jnp.float32)[:, None] * inverse[None, :]
    angle = jnp.concatenate([angle, angle], axis=1)
    return (jnp.cos(angle), jnp.sin(angle))

def rotary_apply(value_rows, cosine_table, sine_table):
    half = value_rows.shape[-1] // 2
    turned = jnp.concatenate([-value_rows[..., half:], value_rows[..., :half]], axis=-1)
    return value_rows * cosine_table[:, None, :] + turned * sine_table[:, None, :]

def route_gates(logits, picks):
    peak = lax.optimization_barrier(jnp.max(logits, axis=-1, keepdims=True))
    exponent = jnp.exp(logits - peak)
    shares = exponent / lax.optimization_barrier(jnp.sum(exponent, axis=-1, keepdims=True))
    chosen = lax.optimization_barrier(jnp.sum(shares[:, None, :] * picks, axis=-1))
    return chosen / lax.optimization_barrier(jnp.sum(chosen, axis=-1, keepdims=True))

def attend_block(normalized_input, lengths, query_weight, key_matrix, value_matrix, query_norm_gain, key_gain):
    count_total = normalized_input.shape[0]
    head_group = QUERY_HEADS // KEY_VALUE_HEADS
    segment, position = sequence_layout(lengths, count_total)
    cosine_table, sine_table = rotary_tables(position, HEAD_SIZE)
    query_rows = lower_precision_backward(product_highest(normalized_input, query_weight)).reshape(count_total, QUERY_HEADS, HEAD_SIZE)
    key_rows = lower_precision_backward(product_highest(normalized_input, key_matrix)).reshape(count_total, KEY_VALUE_HEADS, HEAD_SIZE)
    value_rows = lower_precision(lower_precision_backward(product_highest(normalized_input, value_matrix))).reshape(count_total, KEY_VALUE_HEADS, HEAD_SIZE)
    query_rows = lower_precision(rotary_apply(root_mean_square_norm(query_rows, query_norm_gain), cosine_table, sine_table)).reshape(count_total, KEY_VALUE_HEADS, head_group, HEAD_SIZE)
    key_rows = lower_precision(rotary_apply(root_mean_square_norm(key_rows, key_gain), cosine_table, sine_table))
    places = jnp.arange(count_total, dtype=jnp.int32)
    allowed = (segment[:, None] == segment[None, :]) & (places[None, :] <= places[:, None])
    scores = lower_precision_backward(jnp.einsum('ikgc,jkc->kgij', query_rows, key_rows, precision=HIGH) * HEAD_SIZE ** (-0.5))
    scores = jnp.where(allowed, scores, NEGATIVE)
    peak = lax.optimization_barrier(jnp.max(scores, axis=-1, keepdims=True))
    exponent = jnp.exp(scores - peak)
    shares = lower_precision(exponent / lax.optimization_barrier(jnp.sum(exponent, axis=-1, keepdims=True)))
    context = jnp.einsum('kgij,jkc->ikgc', shares, value_rows, precision=HIGH)
    return lower_precision(lower_precision_backward(context.reshape(count_total, QUERY_HEADS * HEAD_SIZE)))

def expert_rows(pieces, padded_second, padded_gates):
    entries, gate_weight, up_weight, down_weight = pieces
    rows = lower_precision_backward(padded_second[entries // TOPK])
    gate_part = lower_precision_backward(product_highest(rows, gate_weight))
    up_part = lower_precision_backward(product_highest(rows, up_weight))
    units = lower_precision(gate_part * jax.nn.sigmoid(gate_part) * up_part)
    result = lower_precision(lower_precision_backward(product_highest(units, down_weight)))
    return result * padded_gates[entries][:, None]

def slot_table(routes):
    expert_ids = routes.reshape(N_FSDP, TOK_DEV * TOPK)
    hits = (expert_ids[:, :, None] == jnp.arange(EXPERTS, dtype=jnp.int32)[None, None, :]).astype(jnp.int32)
    before = jnp.cumsum(hits, axis=1) - hits
    rank = lax.optimization_barrier(jnp.sum(before * hits, axis=2)).astype(jnp.int32)
    source = jnp.arange(N_FSDP, dtype=jnp.int32)[:, None]
    place = (expert_ids * (N_FSDP * CAP) + source * CAP + rank).astype(jnp.int32)
    entries = jnp.full((EXPERTS * N_FSDP * CAP,), TOKENS * TOPK, jnp.int32)
    entries = entries.at[place.reshape(-1)].set(jnp.arange(TOKENS * TOPK, dtype=jnp.int32))
    return entries.reshape(EXPERTS, N_FSDP * CAP)

def reference(tokens, cotangent, lengths, routes, query_weight, key_matrix, value_matrix, out_weight, router_weight, expert_gate, expert_up, expert_down, first_gain, second_gain, query_norm_gain, key_gain):
    entries = slot_table(routes)
    picks = (routes[:, :, None] == jnp.arange(EXPERTS, dtype=jnp.int32)[None, None, :]).astype(jnp.float32)

    def forward(inputs, query_weight, key_matrix, value_matrix, out_weight, router_weight, expert_gate, expert_up, expert_down, first_gain, second_gain, query_norm_gain, key_gain):
        normalized_input = lower_precision(root_mean_square_norm(inputs, first_gain))

        def one_block(pieces):
            return attend_block(pieces[0], pieces[1], query_weight, key_matrix, value_matrix, query_norm_gain, key_gain)
        context = lax.map(jax.checkpoint(one_block), (normalized_input.reshape(N_FSDP, TOK_DEV, MODEL_WIDTH), lengths))
        context = context.reshape(TOKENS, QUERY_HEADS * HEAD_SIZE)
        hidden = inputs + lower_precision_backward(product_highest(context, out_weight))
        second = lower_precision(root_mean_square_norm(hidden, second_gain))
        logits = lower_precision_backward(product_highest(second, router_weight))
        gates = route_gates(logits, picks)
        padded_second = jnp.concatenate([second, jnp.zeros((1, MODEL_WIDTH), jnp.float32)], axis=0)
        padded_gates = jnp.concatenate([gates.reshape(-1), jnp.zeros((1,), jnp.float32)], axis=0)
        expert_fn = functools.partial(expert_rows, padded_second=padded_second, padded_gates=padded_gates)
        weighted = lax.map(jax.checkpoint(expert_fn), (entries, expert_gate, expert_up, expert_down))
        mixture = jnp.zeros((TOKENS + 1, MODEL_WIDTH), jnp.float32).at[(entries // TOPK).reshape(-1)].add(weighted.reshape(-1, MODEL_WIDTH))
        return hidden + mixture[:TOKENS]
    floats = [array.astype(jnp.float32) for array in (tokens, query_weight, key_matrix, value_matrix, out_weight, router_weight, expert_gate, expert_up, expert_down, first_gain, second_gain, query_norm_gain, key_gain)]
    result, pullback = jax.vjp(forward, *floats)
    grads = pullback(cotangent.astype(jnp.float32))
    return (result.astype(jnp.bfloat16), grads[0], grads[1], grads[2], grads[3], grads[4], grads[5], grads[6], grads[7], grads[8], grads[9], grads[10], grads[11], grads[12])
```

```python
import functools

import jax
import jax.numpy as jnp
from jax import lax
from jax.sharding import PartitionSpec as P

EPS = 1e-06
THETA = 1000000.0
NEGATIVE = -1e30
CORES = 2
LANES = 128
CONTRACT_ROWS = (((0,), (0,)), ((), ()))
CONTRACT_LAST = (((1,), (1,)), ((), ()))


def root_mean_square_norm(value_rows, gain):
    return (
        value_rows
        * lax.rsqrt(jnp.mean(value_rows * value_rows, axis=-1, keepdims=True) + EPS)
        * gain
    )


def sequence_layout(lengths, count_total):
    ends = jnp.cumsum(lengths)
    starts = ends - lengths
    places = jnp.arange(count_total, dtype=jnp.int32)
    member = ((places[:, None] >= starts[None, :]) & (places[:, None] < ends[None, :])).astype(
        jnp.int32
    )
    labels = jnp.arange(lengths.shape[0], dtype=jnp.int32)
    segment = jnp.sum(member * labels[None, :], axis=1)
    offset = jnp.sum(member * starts[None, :], axis=1)
    return (segment, places - offset)


def rotary_tables(position, width):
    half = width // 2
    inverse = jnp.power(THETA, -(jnp.arange(half, dtype=jnp.float32) * 2.0) / width)
    angle = position.astype(jnp.float32)[:, None] * inverse[None, :]
    angle = jnp.concatenate([angle, angle], axis=1)
    return (jnp.cos(angle), jnp.sin(angle))


def rotary_apply(value_rows, cosine_table, sine_table):
    half = value_rows.shape[-1] // 2
    turned = jnp.concatenate([-value_rows[..., half:], value_rows[..., :half]], axis=-1)
    return value_rows * cosine_table[:, None, :] + turned * sine_table[:, None, :]


def prepare(projected_query, projected_key, query_norm_gain, key_gain, cosine_table, sine_table):
    count_total = projected_query.shape[0]
    width = query_norm_gain.shape[0]
    query_rows = rotary_apply(
        root_mean_square_norm(projected_query.reshape(count_total, -1, width), query_norm_gain),
        cosine_table,
        sine_table,
    )
    key_rows = rotary_apply(
        root_mean_square_norm(projected_key.reshape(count_total, -1, width), key_gain),
        cosine_table,
        sine_table,
    )
    return (query_rows, key_rows)


def round_up(number, step):
    return -(-number // step) * step


def body(
    tokens,
    cotangent,
    lengths,
    routes,
    query_weight,
    key_matrix,
    value_matrix,
    out_weight,
    router_weight,
    expert_gate,
    expert_up,
    expert_down,
    first_gain,
    second_gain,
    query_norm_gain,
    key_gain,
):
    f32, bf16 = jnp.float32, jnp.bfloat16
    count, model = tokens.shape
    width = query_norm_gain.shape[0]
    heads = query_weight.shape[1] // width
    kv_heads = key_matrix.shape[1] // width
    head_group = heads // kv_heads
    choose = routes.shape[1]
    shards = lax.axis_size("fsdp")
    experts = shards * expert_gate.shape[0]
    capacity = max(2, count * choose * 5 // (4 * experts))
    scale = width ** (-0.5)

    chips = kv_heads
    plane = chips * CORES
    outer = shards // plane
    span = outer // chips
    me = lax.axis_index("fsdp")
    my_core = me % CORES
    my_outer = me // plane
    four = [
        [o * plane + m * CORES + c for m in range(chips)]
        for o in range(outer)
        for c in range(CORES)
    ]
    eight = [[o * plane + j for j in range(plane)] for o in range(outer)]

    def swap_core(value):
        return lax.ppermute(value, "fsdp", [(i, i ^ 1) for i in range(shards)])

    def swap_chip(value, r):
        return lax.ppermute(value, "fsdp", [(i, i ^ (r * CORES)) for i in range(shards)])

    def shift_outer(value, s):
        return lax.ppermute(
            value,
            "fsdp",
            [(i, ((i // plane + s) % outer) * plane + i % plane) for i in range(shards)],
        )

    def exchange(value, groups):
        return lax.all_to_all(
            value, "fsdp", split_axis=0, concat_axis=0, tiled=True, axis_index_groups=groups
        )

    def gather_chips(value):
        return [value] + [swap_chip(value, r) for r in range(1, chips)]

    def gather_outer(value):
        return [value] + [shift_outer(value, s) for s in range(1, outer)]

    def ring_outer(value):
        pieces = [value]
        for _ in range(1, outer):
            pieces.append(shift_outer(pieces[-1], 1))
        return pieces

    def scatter_outer(value):
        total = lax.dynamic_index_in_dim(value, my_outer, 0, keepdims=False).astype(f32)
        for s in range(1, outer):
            part = lax.dynamic_index_in_dim(value, (my_outer + s) % outer, 0, keepdims=False)
            total = total + shift_outer(part, s).astype(f32)
        return total

    def sum_everywhere(value):
        value = value + swap_core(value)
        value = sum([swap_chip(value, r) for r in range(1, chips)], value)
        return sum([shift_outer(value, s) for s in range(1, outer)], value)

    depth = query_weight.shape[0]
    group_columns = head_group * width
    columns = group_columns + 2 * width
    cut = jnp.concatenate(
        [
            query_weight.reshape(depth, chips, group_columns),
            key_matrix.reshape(depth, chips, width),
            value_matrix.reshape(depth, chips, width),
        ],
        axis=2,
    ).transpose(1, 0, 2)
    cut = exchange(cut, four)
    full_front = jnp.zeros((outer, chips, CORES, depth, columns), bf16)
    for s, piece in enumerate(gather_outer(cut)):
        place = (my_outer - s) % outer
        other = swap_core(piece)
        full_front = lax.dynamic_update_slice(
            full_front, piece[None, :, None], (place, 0, my_core, 0, 0)
        )
        full_front = lax.dynamic_update_slice(
            full_front, other[None, :, None], (place, 0, 1 - my_core, 0, 0)
        )
    full_front = full_front.reshape(model, columns)

    rows_out = out_weight.shape[0]
    stacked = jnp.zeros((outer, rows_out, model), bf16)
    for s, piece in enumerate(gather_outer(out_weight)):
        stacked = lax.dynamic_update_slice(stacked, piece[None], ((my_outer - s) % outer, 0, 0))
    mine = exchange(stacked.reshape(chips, span * rows_out, model), four)
    mine = mine.reshape(chips, span, rows_out, model)
    other = swap_core(mine)
    full_out = jnp.where(
        my_core == 0, jnp.stack([mine, other], axis=1), jnp.stack([other, mine], axis=1)
    )
    full_out = full_out.transpose(2, 0, 1, 3, 4).reshape(group_columns, model)
    full_router = lax.all_gather(router_weight, "fsdp", axis=0, tiled=True)

    mask = jnp.sum(
        (routes[:, :, None] == jnp.arange(experts, dtype=jnp.int32)[None, None, :]).astype(f32),
        axis=1,
    )
    mask_width = round_up(experts, LANES)
    cotangent_wide = jnp.concatenate(
        [cotangent, jnp.pad(mask.astype(bf16), ((0, 0), (0, mask_width - experts)))], axis=1
    )
    earlier = jnp.tril(jnp.ones((count, count), bf16), -1)
    picks, cotangent_rows = [], []
    for piece in gather_outer(cotangent_wide):
        piece_mask = piece[:, model : model + experts]
        rank = jnp.dot(earlier, piece_mask, preferred_element_type=f32)
        local_mask = lax.dynamic_slice_in_dim(piece_mask, my_outer * plane, plane, axis=1)
        local_rank = lax.dynamic_slice_in_dim(rank, my_outer * plane, plane, axis=1)
        pick = (
            (local_rank.T[:, None, :] == jnp.arange(capacity, dtype=f32)[None, :, None])
            & (local_mask.T[:, None, :] > 0)
        ).astype(bf16)
        pick = pick.reshape(plane * capacity, count)
        picks.append(pick)
        sent = jnp.dot(pick, piece[:, :model], preferred_element_type=f32).astype(bf16)
        sent = exchange(sent.reshape(plane, capacity, model), eight)
        cotangent_rows.append(sent.reshape(plane * capacity, model))

    inputs = tokens.astype(f32)
    token_parts = gather_chips(tokens)
    length_parts = gather_chips(lengths)
    normed_low = jnp.concatenate(
        [root_mean_square_norm(part.astype(f32), first_gain).astype(bf16) for part in token_parts],
        axis=0,
    )
    together = chips * count
    projected = jnp.dot(normed_low, full_front, preferred_element_type=f32)
    value_low = projected[:, group_columns + width :].astype(bf16).reshape(chips, count, width)
    layouts = [sequence_layout(part[0], count) for part in length_parts]
    segment = jnp.stack([layout[0] for layout in layouts])
    position = jnp.concatenate([layout[1] for layout in layouts])
    cosine_table, sine_table = rotary_tables(position, width)
    rotated, prepare_back = jax.vjp(
        functools.partial(prepare, cosine_table=cosine_table, sine_table=sine_table),
        projected[:, :group_columns],
        projected[:, group_columns : group_columns + width],
        query_norm_gain,
        key_gain,
    )
    query_low = rotated[0].astype(bf16).reshape(chips, count, head_group, width)
    key_low = rotated[1].astype(bf16).reshape(chips, count, width)
    places = jnp.arange(count, dtype=jnp.int32)
    allowed = (segment[:, :, None] == segment[:, None, :]) & (
        places[None, None, :] <= places[None, :, None]
    )
    allowed = allowed[:, None]

    def score_table():
        raw = jnp.einsum("bigc,bjc->bgij", query_low, key_low, preferred_element_type=f32) * scale
        return jnp.where(allowed, raw, NEGATIVE)

    scores = score_table()
    peak = jnp.max(scores, axis=-1, keepdims=True)
    log_total = peak + jnp.log(jnp.sum(jnp.exp(scores - peak), axis=-1, keepdims=True))
    shares_low = jnp.exp(scores - log_total).astype(bf16)
    context_low = (
        jnp.einsum("bgij,bjc->bigc", shares_low, value_low, preferred_element_type=f32)
        .reshape(together, group_columns)
        .astype(bf16)
    )
    attended = jnp.dot(context_low, full_out, preferred_element_type=f32)
    attended = attended.reshape(chips, count, model)
    hidden = inputs + attended[0]
    for r in range(1, chips):
        hidden = hidden + swap_chip(attended[r].astype(bf16), r).astype(f32)

    second_low = root_mean_square_norm(hidden, second_gain).astype(bf16)
    logits = jnp.dot(second_low, full_router, preferred_element_type=f32)
    exponent = jnp.exp(logits - jnp.max(logits, axis=-1, keepdims=True))
    prob = exponent / jnp.sum(exponent, axis=-1, keepdims=True)
    chosen = prob * mask
    chosen_sum = jnp.sum(chosen, axis=-1, keepdims=True)
    gates = chosen / chosen_sum

    def two_parts(value):
        high = value.astype(bf16)
        low = (value - high.astype(f32)).astype(bf16)
        return high, low

    pair_width = round_up(2 * experts, LANES)
    pair_pad = jnp.zeros((count, pair_width - 2 * experts), bf16)
    second_wide = jnp.concatenate([second_low, *two_parts(gates), pair_pad], axis=1)

    slots = plane * capacity
    gate_weight, up_weight, down_weight = expert_gate[0], expert_up[0], expert_down[0]
    pair_column = jnp.arange(pair_width, dtype=jnp.int32)[None, :]
    high_column = (pair_column == me).astype(f32)
    low_column = (pair_column == me + experts).astype(f32)
    received, units_list, gate_grads, up_grads = [], [], [], []
    moved_sum, grad_sum = None, None
    for s, piece in enumerate(ring_outer(second_wide)):
        sent = jnp.dot(picks[s], piece, preferred_element_type=f32).astype(bf16)
        wide = exchange(sent.reshape(plane, capacity, -1), eight).reshape(slots, -1)
        rows = wide[:, :model]
        row_gate = jnp.sum(
            wide[:, model:].astype(f32) * (high_column + low_column), axis=1, keepdims=True
        )
        gate_part = jnp.dot(rows, gate_weight, preferred_element_type=f32)
        up_part = jnp.dot(rows, up_weight, preferred_element_type=f32)
        grad_units_raw = lax.dot_general(
            cotangent_rows[s], down_weight, CONTRACT_LAST, preferred_element_type=f32
        )
        sig = jax.nn.sigmoid(gate_part)
        silu = gate_part * sig
        units = silu * up_part
        gate_change = jnp.sum(units * grad_units_raw, axis=1, keepdims=True)
        gated_units = (row_gate * units).astype(bf16)
        grad_units = row_gate * grad_units_raw
        grad_gate_low = (grad_units * up_part * sig * (1.0 + gate_part * (1.0 - sig))).astype(bf16)
        grad_up_low = (grad_units * silu).astype(bf16)
        grad_rows = lax.dot_general(
            grad_gate_low, gate_weight, CONTRACT_LAST, preferred_element_type=f32
        ) + lax.dot_general(grad_up_low, up_weight, CONTRACT_LAST, preferred_element_type=f32)
        change_high, change_low = two_parts(gate_change)
        change_wide = change_high.astype(f32) * high_column + change_low.astype(f32) * low_column
        back = jnp.concatenate([grad_rows.astype(bf16), change_wide.astype(bf16)], axis=1)
        back = exchange(back.reshape(plane, capacity, -1), eight).reshape(slots, -1)
        back = lax.dot_general(picks[s], back, CONTRACT_ROWS, preferred_element_type=f32)
        moved = jnp.dot(gated_units, down_weight, preferred_element_type=f32).astype(bf16)
        moved = exchange(moved.reshape(plane, capacity, -1), eight).reshape(slots, -1)
        moved = lax.dot_general(picks[s], moved, CONTRACT_ROWS, preferred_element_type=f32)
        if s == 0:
            grad_sum, moved_sum = back, moved
        else:
            grad_sum = grad_sum + shift_outer(back.astype(bf16), -s).astype(f32)
            moved_sum = moved_sum + shift_outer(moved.astype(bf16), -s).astype(f32)
        received.append(rows)
        units_list.append(gated_units)
        gate_grads.append(grad_gate_low)
        up_grads.append(grad_up_low)
    output = (hidden + moved_sum).astype(bf16)
    all_rows = jnp.concatenate(received, axis=0)
    all_cotangent = jnp.concatenate(cotangent_rows, axis=0)
    gate_grad = lax.dot_general(
        all_rows, jnp.concatenate(gate_grads, axis=0), CONTRACT_ROWS, preferred_element_type=f32
    )[None]
    up_grad = lax.dot_general(
        all_rows, jnp.concatenate(up_grads, axis=0), CONTRACT_ROWS, preferred_element_type=f32
    )[None]
    down_grad = lax.dot_general(
        jnp.concatenate(units_list, axis=0),
        all_cotangent,
        CONTRACT_ROWS,
        preferred_element_type=f32,
    )[None]

    pairs = grad_sum[:, model : model + 2 * experts]
    grad_gates = pairs[:, :experts] + pairs[:, experts:]
    grad_chosen = (
        mask * (grad_gates - jnp.sum(gates * grad_gates, axis=-1, keepdims=True)) / chosen_sum
    )
    grad_logits_low = (
        prob * (grad_chosen - jnp.sum(prob * grad_chosen, axis=-1, keepdims=True))
    ).astype(bf16)
    grad_second = grad_sum[:, :model] + lax.dot_general(
        grad_logits_low, full_router, CONTRACT_LAST, preferred_element_type=f32
    )
    router_grad = lax.psum_scatter(
        lax.dot_general(second_low, grad_logits_low, CONTRACT_ROWS, preferred_element_type=f32),
        "fsdp",
        scatter_dimension=0,
        tiled=True,
    )
    _, second_back = jax.vjp(root_mean_square_norm, hidden, second_gain)
    grad_hidden_part, second_gain_term = second_back(grad_second)
    grad_hidden = cotangent.astype(f32) + grad_hidden_part
    grad_attn_low = jnp.concatenate(gather_chips(grad_hidden.astype(bf16)), axis=0)

    grad_context_low = (
        lax.dot_general(grad_attn_low, full_out, CONTRACT_LAST, preferred_element_type=f32)
        .astype(bf16)
        .reshape(chips, count, head_group, width)
    )
    out_part = lax.dot_general(
        context_low, grad_attn_low, CONTRACT_ROWS, preferred_element_type=f32
    ).astype(bf16)
    out_part = out_part.reshape(span, chips, CORES, rows_out, model)
    out_keep = lax.dynamic_index_in_dim(out_part, my_core, 2, keepdims=False)
    out_send = lax.dynamic_index_in_dim(out_part, 1 - my_core, 2, keepdims=False)
    out_half = (out_keep.astype(f32) + swap_core(out_send).astype(f32)).astype(bf16)
    out_half = exchange(out_half.transpose(1, 0, 2, 3), four)
    out_grad = scatter_outer(out_half.reshape(outer, rows_out, model))

    shares = jnp.exp(score_table() - log_total)
    grad_shares = jnp.einsum(
        "bigc,bjc->bgij", grad_context_low, value_low, preferred_element_type=f32
    )
    grad_scores_low = (
        shares * (grad_shares - jnp.sum(shares * grad_shares, axis=-1, keepdims=True))
    ).astype(bf16)
    grad_rot_query = (
        jnp.einsum("bgij,bjc->bigc", grad_scores_low, key_low, preferred_element_type=f32) * scale
    ).reshape(together, head_group, width)
    grad_rot_key = (
        jnp.einsum("bgij,bigc->bjc", grad_scores_low, query_low, preferred_element_type=f32)
        * scale
    ).reshape(together, 1, width)
    grad_value_low = (
        jnp.einsum("bgij,bigc->bjc", shares_low, grad_context_low, preferred_element_type=f32)
        .astype(bf16)
        .reshape(together, width)
    )
    grad_proj_query, grad_proj_key, query_gain_term, key_gain_term = prepare_back(
        (grad_rot_query, grad_rot_key)
    )
    grad_front_low = jnp.concatenate(
        [grad_proj_query.astype(bf16), grad_proj_key.astype(bf16), grad_value_low], axis=1
    )
    front_part = lax.dot_general(
        normed_low, grad_front_low, CONTRACT_ROWS, preferred_element_type=f32
    ).astype(bf16)
    front_part = front_part.reshape(outer, chips, CORES, depth, columns)
    front_keep = lax.dynamic_index_in_dim(front_part, my_core, 2, keepdims=False)
    front_send = lax.dynamic_index_in_dim(front_part, 1 - my_core, 2, keepdims=False)
    front_half = (front_keep.astype(f32) + swap_core(front_send).astype(f32)).astype(bf16)
    front = exchange(scatter_outer(front_half).astype(bf16), four).astype(f32)
    query_grad = front[:, :, :group_columns].transpose(1, 0, 2).reshape(depth, -1)
    key_grad = (
        front[:, :, group_columns : group_columns + width].transpose(1, 0, 2).reshape(depth, -1)
    )
    value_grad = front[:, :, group_columns + width :].transpose(1, 0, 2).reshape(depth, -1)

    grad_normed_part = lax.dot_general(
        grad_front_low, full_front, CONTRACT_LAST, preferred_element_type=f32
    ).reshape(chips, count, model)
    grad_normed = grad_normed_part[0]
    for r in range(1, chips):
        grad_normed = grad_normed + swap_chip(grad_normed_part[r].astype(bf16), r).astype(f32)
    _, first_back = jax.vjp(root_mean_square_norm, inputs, first_gain)
    grad_input_part, first_gain_term = first_back(grad_normed)
    tokens_grad = grad_hidden + grad_input_part
    gain_sums = sum_everywhere(
        jnp.concatenate(
            [first_gain_term, second_gain_term, query_gain_term, key_gain_term]
        ).reshape(-1, LANES)
    ).reshape(-1)
    return (
        output,
        tokens_grad,
        query_grad,
        key_grad,
        value_grad,
        out_grad,
        router_grad,
        gate_grad,
        up_grad,
        down_grad,
        gain_sums[:model],
        gain_sums[model : 2 * model],
        gain_sums[2 * model : 2 * model + width],
        gain_sums[2 * model + width :],
    )


def solution(mesh):
    rows = P("fsdp", None)
    blocks = P("fsdp", None, None)
    placed = (rows,) * 9 + (blocks,) * 3 + (P(),) * 4
    return jax.shard_map(
        body,
        mesh=mesh,
        in_specs=placed,
        out_specs=(rows,) * 7 + (blocks,) * 3 + (P(),) * 4,
        check_vma=False,
    )
```

```python
import functools

import jax
import jax.numpy as jnp
from jax import lax
from jax.experimental import pallas as pl
from jax.experimental.pallas import tpu as pltpu
from jax.sharding import PartitionSpec as P

EPS = 1e-06
THETA = 1000000.0
NEGATIVE = -1e30
CORES = 2
LANES = 128
FLOPS_A_MICRO = 1_000_000_000
BYTES_A_MICRO = 2_000_000
VMEM_BYTES = 32 * 1024 * 1024
MORE_BYTES = 50 * 1024 * 1024
CONTRACT_ROWS = (((0,), (0,)), ((), ()))
CONTRACT_LAST = (((1,), (1,)), ((), ()))


def root_mean_square_norm(value_rows, gain):
    return (
        value_rows
        * lax.rsqrt(jnp.mean(value_rows * value_rows, axis=-1, keepdims=True) + EPS)
        * gain
    )


def sequence_layout(lengths, count_total):
    ends = jnp.cumsum(lengths)
    starts = ends - lengths
    places = jnp.arange(count_total, dtype=jnp.int32)
    member = ((places[:, None] >= starts[None, :]) & (places[:, None] < ends[None, :])).astype(
        jnp.int32
    )
    labels = jnp.arange(lengths.shape[0], dtype=jnp.int32)
    segment = jnp.sum(member * labels[None, :], axis=1)
    offset = jnp.sum(member * starts[None, :], axis=1)
    return (segment, places - offset)


def rotary_tables(position, width):
    half = width // 2
    inverse = jnp.power(THETA, -(jnp.arange(half, dtype=jnp.float32) * 2.0) / width)
    angle = position.astype(jnp.float32)[:, None] * inverse[None, :]
    angle = jnp.concatenate([angle, angle], axis=1)
    return (jnp.cos(angle), jnp.sin(angle))


def call(kernel, outs, vmem=VMEM_BYTES, micros=0, **specs):
    if micros:
        specs["cost_estimate"] = pl.CostEstimate(
            flops=micros * FLOPS_A_MICRO, bytes_accessed=micros * BYTES_A_MICRO, transcendentals=0
        )
    return pl.pallas_call(
        kernel,
        out_shape=outs,
        compiler_params=pltpu.CompilerParams(vmem_limit_bytes=vmem),
        **specs,
    )


def turned_sine(sine_table):
    half = sine_table.shape[1] // 2
    return jnp.concatenate([-sine_table[:, :half], sine_table[:, half:]], axis=1)


def head_rotated(value, gain, cosine, sine):
    normal = (
        value * lax.rsqrt(jnp.mean(value * value, axis=-1, keepdims=True) + EPS) * gain
    )
    return normal * cosine + pltpu.roll(normal, value.shape[1] // 2, 1) * sine


def head_shares(query, key, allowed, scale):
    scores = lax.dot_general(query, key, CONTRACT_LAST, preferred_element_type=jnp.float32)
    scores = jnp.where(allowed, scores * scale, NEGATIVE)
    exponent = jnp.exp(scores - jnp.max(scores, axis=-1, keepdims=True))
    return exponent / jnp.sum(exponent, axis=-1, keepdims=True)


def norm_kernel(outer, my_outer, *refs):
    *parts, gain, order, out, normed = refs
    count = parts[0].shape[0]
    span = order.shape[0]
    half = span // CORES
    for b, part in enumerate(parts):
        normed[b * count : (b + 1) * count, :] = root_mean_square_norm(
            part[...].astype(jnp.float32), gain[...]
        ).astype(jnp.bfloat16)
    for s in range(outer):
        start = lax.rem(my_outer[0] + (outer - s), outer) * span
        block = normed[:, pl.ds(pl.multiple_of(start, LANES), span)]
        block = jnp.dot(block, order[...], preferred_element_type=jnp.float32)
        block = block.astype(jnp.bfloat16)
        for k in range(CORES):
            first = (k * outer + s) * half
            out[:, first : first + half] = block[:, k * half : (k + 1) * half]


def project_kernel(normed, *refs):
    *pieces, out = refs
    rows = pieces[0].shape[0]
    total = jnp.zeros(out.shape, jnp.float32)
    for i, piece in enumerate(pieces):
        total += jnp.dot(
            normed[:, i * rows : (i + 1) * rows], piece[...], preferred_element_type=jnp.float32
        )
    out[...] = total


def project_back_kernel(my_outer, grad, own, other, order, out):
    f32, bf16 = jnp.float32, jnp.bfloat16
    block = jnp.concatenate(
        [
            lax.dot_general(grad[...], part[0], CONTRACT_LAST, preferred_element_type=f32)
            for part in (own, other)
        ],
        axis=1,
    ).astype(bf16)
    out[...] = lax.dot_general(
        block, order[...], CONTRACT_LAST, preferred_element_type=f32
    ).astype(bf16)


def tokens_back_kernel(tokens, own, *refs):
    *others, hidden_grad, gain, tokens_grad, gain_grad = refs
    f32 = jnp.float32
    grad = own[...].astype(f32)
    for other in others:
        grad = grad + other[...].astype(f32)
    value = tokens[...].astype(f32)
    root = lax.rsqrt(jnp.mean(value * value, axis=-1, keepdims=True) + EPS)
    normal = value * root
    gain_grad[...] = jnp.sum(grad * normal, axis=0, keepdims=True)
    grad = grad * gain[...]
    tokens_grad[...] = hidden_grad[...] + root * (
        grad - normal * jnp.mean(normal * grad, axis=-1, keepdims=True)
    )


def attend_kernel(scale, front, cosine, sine, allowed, query_gain, key_gain, order, *outs):
    query_out, key_out, value_out, context_out, context = outs
    width = cosine.shape[1]
    heads = query_out.shape[1] // width
    bf16 = jnp.bfloat16
    cos, sin = cosine[...], sine[...]
    open_places = allowed[...] > 0.0
    key = head_rotated(
        front[:, heads * width : (heads + 1) * width], key_gain[...], cos, sin
    ).astype(bf16)
    value = front[:, (heads + 1) * width :].astype(bf16)
    key_out[...] = key
    value_out[...] = value
    for h in range(heads):
        part = slice(h * width, (h + 1) * width)
        query = head_rotated(front[:, part], query_gain[...], cos, sin).astype(bf16)
        query_out[:, part] = query
        shares = head_shares(query, key, open_places, scale).astype(bf16)
        context[:, part] = jnp.dot(
            shares, value, preferred_element_type=jnp.float32
        ).astype(bf16)
    context_out[...] = jnp.dot(
        context[...], order[...], preferred_element_type=jnp.float32
    ).astype(bf16)


def head_back(grad, value, gain, cosine, sine):
    grad = grad * cosine + pltpu.roll(grad * sine, value.shape[1] // 2, 1)
    root = lax.rsqrt(jnp.mean(value * value, axis=-1, keepdims=True) + EPS)
    normal = value * root
    gain_grad = jnp.sum(grad * normal, axis=0, keepdims=True)
    grad = grad * gain
    grad = root * (grad - normal * jnp.mean(normal * grad, axis=-1, keepdims=True))
    return grad, gain_grad


def attend_back_kernel(
    scale, front, query_in, key_in, value_in, grad_own, grad_other, cosine, sine, allowed, *rest
):
    query_gain, key_gain, order, front_grad, gain_grads, context_grad = rest
    half = grad_own.shape[1]
    context_grad[...] = (
        lax.dot_general(
            grad_own[...], order[:, :half], CONTRACT_LAST, preferred_element_type=jnp.float32
        )
        + lax.dot_general(
            grad_other[...], order[:, half:], CONTRACT_LAST, preferred_element_type=jnp.float32
        )
    ).astype(jnp.bfloat16)
    width = cosine.shape[1]
    heads = query_in.shape[1] // width
    f32, bf16 = jnp.float32, jnp.bfloat16
    cos, sin = cosine[...], sine[...]
    open_places = allowed[...] > 0.0
    key, value = key_in[...], value_in[...]
    key_total = jnp.zeros(key.shape, f32)
    value_total = jnp.zeros(key.shape, f32)
    gain_total = jnp.zeros((1, width), f32)
    for h in range(heads):
        part = slice(h * width, (h + 1) * width)
        query, grad = query_in[:, part], context_grad[:, part]
        shares = head_shares(query, key, open_places, scale)
        grad_shares = lax.dot_general(grad, value, CONTRACT_LAST, preferred_element_type=f32)
        grad_scores = (
            shares * (grad_shares - jnp.sum(shares * grad_shares, axis=-1, keepdims=True))
        ).astype(bf16)
        value_total += lax.dot_general(
            shares.astype(bf16), grad, CONTRACT_ROWS, preferred_element_type=f32
        )
        key_total += lax.dot_general(
            grad_scores, query, CONTRACT_ROWS, preferred_element_type=f32
        )
        grad_query = jnp.dot(grad_scores, key, preferred_element_type=f32) * scale
        grad_query, gain_grad = head_back(grad_query, front[:, part], query_gain[...], cos, sin)
        front_grad[:, part] = grad_query.astype(bf16)
        gain_total += gain_grad
    part = slice(heads * width, (heads + 1) * width)
    grad_key, key_gain_grad = head_back(
        key_total * scale, front[:, part], key_gain[...], cos, sin
    )
    front_grad[:, part] = grad_key.astype(bf16)
    front_grad[:, (heads + 1) * width :] = value_total.astype(bf16)

    @pl.when(pl.program_id(0) == 0)
    def _():
        gain_grads[...] = jnp.zeros(gain_grads.shape, f32)

    gain_grads[0:1, :] += gain_total
    gain_grads[1:2, :] += key_gain_grad


def router_kernel(experts, *refs):
    tokens, own, *others, gain, router, mask, hidden_out, wide_out, prob_out, gates_out = refs
    f32, bf16 = jnp.float32, jnp.bfloat16
    model = tokens.shape[1]
    lanes = mask.shape[1]
    hidden = tokens[...].astype(f32) + own[...]
    for other in others:
        hidden = hidden + other[...].astype(f32)
    hidden_out[...] = hidden
    second = root_mean_square_norm(hidden, gain[...]).astype(bf16)
    wide_out[:, :model] = second
    logits = jnp.dot(second, router[...], preferred_element_type=f32)
    column = lax.broadcasted_iota(jnp.int32, logits.shape, 1)
    logits = jnp.where(column < experts, logits, NEGATIVE)
    exponent = jnp.exp(logits - jnp.max(logits, axis=-1, keepdims=True))
    prob = exponent / jnp.sum(exponent, axis=-1, keepdims=True)
    chosen = prob * mask[...]
    gates = chosen / jnp.sum(chosen, axis=-1, keepdims=True)
    prob_out[...] = prob
    gates_out[...] = gates
    high = gates.astype(bf16).astype(f32)
    low = gates - high
    if 2 * experts <= lanes:
        wide_out[:, model:] = (high + pltpu.roll(low, experts, 1)).astype(bf16)
    else:
        wide_out[:, model : model + lanes] = high.astype(bf16)
        wide_out[:, model + lanes :] = low.astype(bf16)


def router_back_kernel(experts, *refs):
    own, near, came, cotangent, hidden, gain, router, mask, prob, gates, *outs = refs
    hidden_grad, attn_grad, logits_grad, gain_grad = outs
    f32, bf16 = jnp.float32, jnp.bfloat16
    model = cotangent.shape[1]
    lanes = mask.shape[1]
    pairs = own[:, model:] + near[:, model:].astype(f32) + came[:, model:].astype(f32)
    if 2 * experts <= lanes:
        grad_gates = pairs + pltpu.roll(pairs, lanes - experts, 1)
    else:
        grad_gates = pairs[:, :lanes] + pairs[:, lanes:]
    chosen_sum = jnp.sum(prob[...] * mask[...], axis=-1, keepdims=True)
    grad_gates = jnp.where(mask[...] > 0.0, grad_gates, 0.0)
    grad_chosen = (
        mask[...]
        * (grad_gates - jnp.sum(gates[...] * grad_gates, axis=-1, keepdims=True))
        / chosen_sum
    )
    grad_logits = (
        prob[...] * (grad_chosen - jnp.sum(prob[...] * grad_chosen, axis=-1, keepdims=True))
    ).astype(bf16)
    logits_grad[...] = grad_logits
    grad = (
        own[:, :model]
        + near[:, :model].astype(f32)
        + came[:, :model].astype(f32)
        + lax.dot_general(grad_logits, router[...], CONTRACT_LAST, preferred_element_type=f32)
    )
    value = hidden[...]
    root = lax.rsqrt(jnp.mean(value * value, axis=-1, keepdims=True) + EPS)
    normal = value * root
    gain_grad[...] = jnp.sum(grad * normal, axis=0, keepdims=True)
    grad = grad * gain[...]
    grad = cotangent[...].astype(f32) + root * (
        grad - normal * jnp.mean(normal * grad, axis=-1, keepdims=True)
    )
    hidden_grad[...] = grad
    attn_grad[...] = grad.astype(bf16)


def pick_kernel(capacity, own, partner, near, earlier, *outs):
    *parts, picks = outs
    f32, bf16 = jnp.float32, jnp.bfloat16
    rows, model = parts[0].shape
    count = own.shape[0]
    masks = [
        lax.dot_general(near[...], side[:, model:], CONTRACT_LAST, preferred_element_type=f32)
        for side in (own, partner)
    ]
    ranks = [jnp.dot(m.astype(bf16), earlier[...], preferred_element_type=f32) for m in masks]
    mask = jnp.concatenate(masks, axis=1)
    rank = jnp.concatenate([ranks[0], ranks[1] + capacity], axis=1)
    place = lax.broadcasted_iota(jnp.int32, (rows, CORES * count), 0).astype(f32)
    for r in range(len(parts)):
        hit = (place == rank[r : r + 1, :]) & (mask[r : r + 1, :] > 0.5)
        picks[r * rows : (r + 1) * rows, :] = jnp.where(hit, 1.0, 0.0).astype(bf16)
    both = jnp.concatenate([own[:, :model], partner[:, :model]], axis=0)
    chosen = jnp.dot(picks[...], both, preferred_element_type=f32).astype(bf16)
    for r, part in enumerate(parts):
        part[...] = chosen[r * rows : (r + 1) * rows, :]


def send_kernel(picks, own, partner, *parts):
    rows = parts[0].shape[0]
    both = jnp.concatenate([own[...], partner[...]], axis=0)
    chosen = jnp.dot(picks[...], both, preferred_element_type=jnp.float32).astype(jnp.bfloat16)
    for r, part in enumerate(parts):
        part[...] = chosen[r * rows : (r + 1) * rows, :]


def settle_kernel(picks, *refs):
    *parts, own, partner = refs
    count = own.shape[0]
    rows = jnp.concatenate([part[...] for part in parts], axis=0)
    total = lax.dot_general(
        picks[...], rows, CONTRACT_ROWS, preferred_element_type=jnp.float32
    )
    own[...] = total[:count, :]
    partner[...] = total[count:, :].astype(jnp.bfloat16)


def move_kernel(units, weight, *parts):
    rows = parts[0].shape[0]
    moved = jnp.dot(units[...], weight[...], preferred_element_type=jnp.float32)
    for r, part in enumerate(parts):
        part[...] = moved[r * rows : (r + 1) * rows, :].astype(jnp.bfloat16)


def expert_kernel(chips, experts, me, *refs):
    f32, bf16 = jnp.float32, jnp.bfloat16
    came, given = refs[:chips], refs[chips : 2 * chips]
    gate_weight, up_weight, down_weight = refs[2 * chips : 2 * chips + 3]
    back = refs[2 * chips + 3 : 3 * chips + 3]
    units_out, gate_out, up_out, rows, grads, row_gate, change, total = refs[3 * chips + 3 :]
    size, model = came[0].shape[0], rows.shape[1]
    step = pl.program_id(0)
    column = lax.broadcasted_iota(jnp.int32, (size, came[0].shape[1] - model), 1)
    high_column, low_column = column == me[0], column == me[0] + experts

    @pl.when(step == 0)
    def _():
        for r in range(chips):
            part = slice(r * size, (r + 1) * size)
            rows[part, :] = came[r][:, :model]
            grads[part, :] = given[r][...]
            side = jnp.where(high_column | low_column, came[r][:, model:].astype(f32), 0.0)
            row_gate[part, :] = jnp.sum(side, axis=1, keepdims=True)
        change[...] = jnp.zeros(change.shape, f32)
        total[...] = jnp.zeros(total.shape, f32)

    gate_part = jnp.dot(rows[...], gate_weight[...], preferred_element_type=f32)
    up_part = jnp.dot(rows[...], up_weight[...], preferred_element_type=f32)
    raw = lax.dot_general(
        grads[...], down_weight[...], CONTRACT_LAST, preferred_element_type=f32
    )
    sig = 1.0 / (1.0 + jnp.exp(-gate_part))
    silu = gate_part * sig
    units = silu * up_part
    change[...] += jnp.sum(units * raw, axis=1, keepdims=True)
    units_out[...] = (row_gate[...] * units).astype(bf16)
    grad_units = row_gate[...] * raw
    gate_grad = (grad_units * up_part * sig * (1.0 + gate_part * (1.0 - sig))).astype(bf16)
    up_grad = (grad_units * silu).astype(bf16)
    gate_out[...] = gate_grad
    up_out[...] = up_grad
    total[...] += lax.dot_general(
        gate_grad, gate_weight[...], CONTRACT_LAST, preferred_element_type=f32
    ) + lax.dot_general(up_grad, up_weight[...], CONTRACT_LAST, preferred_element_type=f32)

    @pl.when(step == pl.num_programs(0) - 1)
    def _():
        for r in range(chips):
            part = slice(r * size, (r + 1) * size)
            back[r][:, :model] = total[part, :].astype(bf16)
            high = change[part, :].astype(bf16).astype(f32)
            low = change[part, :] - high
            back[r][:, model:] = (
                jnp.where(high_column, high, 0.0) + jnp.where(low_column, low, 0.0)
            ).astype(bf16)


def expert_grad_kernel(outer, chips, *refs):
    f32 = jnp.float32
    parts = outer * chips
    rows, grads = refs[:parts], refs[parts : 2 * parts]
    units, gates, ups = (
        refs[2 * parts + i * outer : 2 * parts + (i + 1) * outer] for i in range(3)
    )
    gate_out, up_out, down_out, left, right, all_units, all_gates, all_ups = refs[
        2 * parts + 3 * outer :
    ]
    size = rows[0].shape[0]
    for i in range(parts):
        part = slice(i * size, (i + 1) * size)
        left[part, :] = rows[i][...]
        right[part, :] = grads[i][...]
    size = units[0].shape[0]

    @pl.when(pl.program_id(0) == 0)
    def _():
        for s in range(outer):
            part = slice(s * size, (s + 1) * size)
            all_units[part, :] = units[s][...]
            all_gates[part, :] = gates[s][...]
            all_ups[part, :] = ups[s][...]

    def product(a, b):
        return lax.dot_general(a[...], b[...], CONTRACT_ROWS, preferred_element_type=f32)

    gate_out[...] = product(left, all_gates)
    up_out[...] = product(left, all_ups)
    down_out[...] = product(all_units, right)


def round_up(number, step):
    return -(-number // step) * step


def after(value, *others):
    return lax.optimization_barrier((value, *others))[0]


def body(
    tokens,
    cotangent,
    lengths,
    routes,
    query_weight,
    key_matrix,
    value_matrix,
    out_weight,
    router_weight,
    expert_gate,
    expert_up,
    expert_down,
    first_gain,
    second_gain,
    query_norm_gain,
    key_gain,
):
    f32, bf16, i32 = jnp.float32, jnp.bfloat16, jnp.int32
    shape = jax.ShapeDtypeStruct
    fence = lax.optimization_barrier
    count, model = tokens.shape
    width = query_norm_gain.shape[0]
    heads = query_weight.shape[1] // width
    kv_heads = key_matrix.shape[1] // width
    head_group = heads // kv_heads
    choose = routes.shape[1]
    shards = lax.axis_size("fsdp")
    experts = shards * expert_gate.shape[0]
    capacity = max(2, count * choose * 5 // (4 * experts))
    scale = width ** (-0.5)

    chips = kv_heads
    plane = chips * CORES
    outer = shards // plane
    span = outer // chips
    me = lax.axis_index("fsdp")
    my_core = me % CORES
    my_chip = (me // CORES) % chips
    my_outer = me // plane
    me_scalar = me.reshape(1)
    outer_scalar = my_outer.reshape(1)
    smem = pl.BlockSpec(memory_space=pltpu.SMEM)
    vmem = pl.BlockSpec(memory_space=pltpu.VMEM)

    def swap_core(value):
        return lax.ppermute(value, "fsdp", [(i, i ^ 1) for i in range(shards)])

    def swap_chip(value, r):
        if r == 0:
            return value
        return lax.ppermute(value, "fsdp", [(i, i ^ (r * CORES)) for i in range(shards)])

    def shift_outer(value, s=1):
        if s == 0:
            return value
        return lax.ppermute(
            value,
            "fsdp",
            [(i, ((i // plane + s) % outer) * plane + i % plane) for i in range(shards)],
        )

    def gather_chips(value):
        return [swap_chip(value, r) for r in range(chips)]

    def spread(parts):
        return [swap_chip(part, r) for r, part in enumerate(parts)]

    def ring_reduce(part):
        total = part(1)
        for s in range(2, outer):
            total = shift_outer(total.astype(bf16)).astype(f32) + part(s)
        return part(0), shift_outer(total.astype(bf16))

    def scatter_outer(take):
        total = take(my_outer)
        for s in range(1, outer):
            total = total + shift_outer(take((my_outer + s) % outer), s)
        return total

    def by_chip(parts):
        parts = jnp.stack(parts)
        return [
            lax.dynamic_index_in_dim(parts, my_chip ^ m, 0, keepdims=False) for m in range(chips)
        ]

    depth = query_weight.shape[0]
    group_columns = head_group * width
    half_columns = group_columns // CORES
    columns = group_columns + 2 * width
    rows_out = out_weight.shape[0]

    def arrival_order(length, block, inner):
        place = jnp.arange(length, dtype=i32)
        went_to = (
            (
                ((place // block % CORES) ^ my_core) * chips
                + ((place // (block * CORES) % chips) ^ my_chip)
            )
            * inner
            + place // (block * plane)
        ) * block + place % block
        return (went_to[:, None] == place[None, :]).astype(bf16)

    front_order = arrival_order(plane * depth, depth, 1)
    out_order = arrival_order(group_columns, rows_out, span)

    lanes = round_up(experts, LANES)
    pair_width = round_up(2 * experts, LANES)
    mask = jnp.sum(
        (routes[:, :, None] == jnp.arange(lanes, dtype=i32)[None, None, :]).astype(f32), axis=1
    )
    near = jnp.arange(2 * chips, dtype=i32)
    near = jnp.where(
        near < chips, my_outer * plane + (my_chip ^ near) * CORES + my_core, -1
    )
    near = (near[:, None] == jnp.arange(lanes, dtype=i32)[None, :]).astype(bf16)
    earlier = jnp.triu(jnp.ones((count, count), bf16), 1)
    part_rows = round_up(CORES * capacity, 16)
    slots = chips * part_rows

    def dispatch_first(piece, partner):
        *parts, picks = call(
            functools.partial(pick_kernel, capacity),
            [shape((part_rows, model), bf16)] * chips + [shape((slots, CORES * count), bf16)],
        )(piece, partner, near, earlier)
        return parts, picks

    def dispatch(picks, piece, partner):
        return call(send_kernel, [shape((part_rows, piece.shape[1]), bf16)] * chips)(
            picks, piece, partner
        )

    def settle(picks, parts):
        columns_of = parts[0].shape[1]
        return call(
            settle_kernel, (shape((count, columns_of), f32), shape((count, columns_of), bf16))
        )(picks, *parts)

    cut = []
    for r in range(chips):
        target = my_chip ^ r
        part = [
            lax.dynamic_slice_in_dim(query_weight, target * group_columns, group_columns, 1),
            lax.dynamic_slice_in_dim(key_matrix, target * width, width, 1),
            lax.dynamic_slice_in_dim(value_matrix, target * width, width, 1),
        ]
        cut.append(swap_chip(jnp.concatenate(part, axis=1), r))
    cut = jnp.concatenate(cut, axis=0)
    front_pieces, front_others = [cut], []
    out_pieces = [out_weight, shift_outer(out_weight)]
    cotangent_wide = jnp.concatenate([cotangent, mask.astype(bf16)], axis=1)
    cotangent_pieces, cotangent_parts, picks = [cotangent_wide], [], []

    def send_cotangent(piece, partner):
        parts, pick = dispatch_first(piece, partner)
        cotangent_parts.append(spread(parts))
        picks.append(pick)

    router_parts = router_weight.reshape(1, depth * experts)
    for t in range(2, outer + 1):
        (
            front_pieces[-1],
            out_pieces[-1],
            tokens,
            lengths,
            router_parts,
            cotangent_pieces[0],
        ) = fence(
            (
                front_pieces[-1],
                out_pieces[-1],
                tokens,
                lengths,
                router_parts,
                cotangent_pieces[0],
            )
        )
        front_pieces.append(shift_outer(front_pieces[-1]))
        front_others.append(swap_core(front_pieces[-2]))
        if t < outer:
            out_pieces.append(shift_outer(out_pieces[-1]))
        if t == 2:
            token_parts = gather_chips(tokens)
            length_parts = gather_chips(lengths)
            router_parts = jnp.concatenate([router_parts, swap_core(router_parts)], axis=0)
            cotangent_partner = swap_core(cotangent_pieces[0])
        if t == 3:
            router_parts = jnp.concatenate(gather_chips(router_parts), axis=0)
            send_cotangent(cotangent_pieces[0], cotangent_partner)
    cotangent_pieces.append(shift_outer(cotangent_pieces[0]))
    stacked = jnp.stack(out_pieces)
    out_own = []
    for r in range(chips):
        part = [
            lax.dynamic_index_in_dim(
                stacked,
                (my_outer + outer - ((my_chip ^ r) * span + u)) % outer,
                0,
                keepdims=False,
            )
            for u in range(span)
        ]
        out_own.append(swap_chip(jnp.concatenate(part, axis=0), r))

    together = chips * count
    first_gain_row, second_gain_row = first_gain[None, :], second_gain[None, :]
    query_gain_row, key_gain_row = query_norm_gain[None, :], key_gain[None, :]
    normed_low = call(
        functools.partial(norm_kernel, outer),
        shape((together, model), bf16),
        in_specs=[smem] + [vmem] * (chips + 2),
        scratch_shapes=[pltpu.VMEM((together, model), bf16)],
    )(outer_scalar, *token_parts, first_gain_row, front_order)
    layouts = [sequence_layout(part[0], count) for part in length_parts]
    segment = jnp.stack([layout[0] for layout in layouts])
    position = jnp.concatenate([layout[1] for layout in layouts])
    cosine_table, sine_table = rotary_tables(position, width)
    sine_table = turned_sine(sine_table)
    places = jnp.arange(count, dtype=i32)
    allowed = (segment[:, :, None] == segment[:, None, :]) & (
        places[None, None, :] <= places[None, :, None]
    )
    allowed = allowed.astype(f32).reshape(together, count)
    (
        front_pieces[-1],
        cotangent_pieces[-1],
        router_parts,
        out_own,
        normed_low,
        cosine_table,
        sine_table,
        allowed,
        out_order,
        cotangent_parts[0],
    ) = fence(
        (
            front_pieces[-1],
            cotangent_pieces[-1],
            router_parts,
            out_own,
            normed_low,
            cosine_table,
            sine_table,
            allowed,
            out_order,
            cotangent_parts[0],
        )
    )
    front_others.append(swap_core(front_pieces[-1]))
    router_parts = jnp.concatenate([shift_outer(router_parts, s) for s in range(outer)], axis=0)
    out_own = jnp.concatenate(out_own, axis=0)
    out_other = swap_core(out_own)
    cotangent_partner = swap_core(cotangent_pieces[1])
    for s in range(2, outer - 1):
        cotangent_pieces.append(shift_outer(cotangent_pieces[-1]))
    tile = 2 * width
    projected = call(
        project_kernel,
        shape((together, columns), f32),
        grid=(columns // tile,),
        in_specs=[pl.BlockSpec((together, model), lambda n: (0, 0))]
        + [pl.BlockSpec((chips * depth, tile), lambda n: (0, n))] * (CORES * outer),
        out_specs=pl.BlockSpec((together, tile), lambda n: (0, n)),
    )(normed_low, *front_pieces, *front_others)

    def blocks(columns_of):
        return pl.BlockSpec((count, columns_of), lambda b: (b, 0))

    once = pl.BlockSpec((1, width), lambda b: (0, 0))
    order_once = pl.BlockSpec((group_columns, group_columns), lambda b: (0, 0))
    query_low, key_low, value_low, context_low = call(
        functools.partial(attend_kernel, scale),
        (
            shape((together, group_columns), bf16),
            shape((together, width), bf16),
            shape((together, width), bf16),
            shape((together, group_columns), bf16),
        ),
        micros=13,
        grid=(chips,),
        in_specs=[
            blocks(columns),
            blocks(width),
            blocks(width),
            blocks(count),
            once,
            once,
            order_once,
        ],
        out_specs=[blocks(group_columns), blocks(width), blocks(width), blocks(group_columns)],
        scratch_shapes=[pltpu.VMEM((count, group_columns), bf16)],
    )(projected, cosine_table, sine_table, allowed, query_gain_row, key_gain_row, out_order)
    send_cotangent(after(cotangent_pieces[1], context_low), cotangent_partner)
    device = jnp.arange(shards, dtype=i32)
    came_from = ((my_outer - device // plane) % outer) * plane + (
        (device % plane) ^ (me % plane)
    )
    full_router = jnp.dot(
        (came_from[:, None] == device[None, :]).astype(bf16),
        router_parts,
        preferred_element_type=f32,
    )
    full_router = full_router.astype(bf16).reshape(model, experts)
    router_wide = jnp.pad(full_router, ((0, 0), (0, lanes - experts)))

    context_low, out_own, out_other, cotangent_pieces[-1], router_wide = fence(
        (context_low, out_own, out_other, cotangent_pieces[-1], router_wide)
    )
    context_own, context_other = context_low[:, :half_columns], context_low[:, half_columns:]

    def attended(first, last):
        return jnp.dot(
            context_own[first:last], out_own, preferred_element_type=f32
        ) + jnp.dot(context_other[first:last], out_other, preferred_element_type=f32)

    away = attended(count, together).astype(bf16)
    arrived = [swap_chip(away[(r - 1) * count : r * count], r) for r in range(1, chips)]
    home = attended(0, count)
    cotangent_pieces.append(shift_outer(cotangent_pieces[-1]))
    for s in range(2, outer - 1):
        send_cotangent(after(cotangent_pieces[s], away), swap_core(cotangent_pieces[s]))
    arrived, home, cotangent_pieces[-1], cotangent_parts = fence(
        (arrived, home, cotangent_pieces[-1], cotangent_parts)
    )
    send_cotangent(cotangent_pieces[-1], swap_core(cotangent_pieces[-1]))
    hidden, second_wide, prob, gates = call(
        functools.partial(router_kernel, experts),
        (
            shape((count, model), f32),
            shape((count, model + pair_width), bf16),
            shape((count, lanes), f32),
            shape((count, lanes), f32),
        ),
    )(tokens, home, *arrived, second_gain_row, router_wide, mask)

    gate_weight, up_weight, down_weight = expert_gate[0], expert_up[0], expert_down[0]
    hidden_units = gate_weight.shape[1]
    unit_tile = 2 * LANES

    def expert(came, given):
        part = pl.BlockSpec((part_rows, model + pair_width), lambda f: (0, 0))
        units = pl.BlockSpec((slots, unit_tile), lambda f: (0, f))
        outs = call(
            functools.partial(expert_kernel, chips, experts),
            [shape((part_rows, model + pair_width), bf16)] * chips
            + [shape((slots, hidden_units), bf16)] * 3,
            vmem=MORE_BYTES,
            micros=13,
            grid=(hidden_units // unit_tile,),
            in_specs=[smem]
            + [part] * chips
            + [pl.BlockSpec((part_rows, model), lambda f: (0, 0))] * chips
            + [pl.BlockSpec((model, unit_tile), lambda f: (0, f))] * 2
            + [pl.BlockSpec((unit_tile, model), lambda f: (f, 0))],
            out_specs=[part] * chips + [units] * 3,
            scratch_shapes=[
                pltpu.VMEM((slots, model), bf16),
                pltpu.VMEM((slots, model), bf16),
                pltpu.VMEM((slots, 1), f32),
                pltpu.VMEM((slots, 1), f32),
                pltpu.VMEM((slots, model), f32),
            ],
        )(me_scalar, *came, *given, gate_weight, up_weight, down_weight)
        return outs[:chips], (came, given, *outs[chips:])

    second_pieces = [second_wide]
    for s in range(1, outer):
        second_pieces.append(shift_outer(second_pieces[-1]))
    backs, kept = [], []
    sent = dispatch(picks[0], second_pieces[0], swap_core(second_pieces[0]))
    for s in range(outer):
        came = spread(sent)
        if s + 1 < outer:
            piece = second_pieces[s + 1]
            partner = swap_core(piece)
            if s:
                piece = after(piece, *backs[s - 1])
            sent = dispatch(picks[s + 1], piece, partner)
            came, sent, cotangent_parts = fence((came, sent, cotangent_parts))
        back, keep = expert(came, cotangent_parts[s])
        backs.append(back)
        kept.append(keep)

    returned, latest = {}, ()
    for s in [*range(1, outer), 0]:
        parts = spread(fence((backs[s], latest))[0])
        latest = tuple(parts[1:])
        own, partner = settle(picks[s], parts)
        returned[s] = (own, swap_core(partner))
    grad_own, grad_came = ring_reduce(
        lambda s: returned[s][0] + returned[s][1].astype(f32) if s else returned[0]
    )

    def move(s, *others):
        return call(move_kernel, [shape((part_rows, model), bf16)] * chips)(
            after(kept[s][2], *others), down_weight
        )

    moved = {s: spread(move(s, *latest)) for s in range(1, outer - 1)}

    grad_hidden, grad_hidden_low, grad_logits_low, second_gain_term = call(
        functools.partial(router_back_kernel, experts),
        (
            shape((count, model), f32),
            shape((count, model), bf16),
            shape((count, lanes), bf16),
            shape((1, model), f32),
        ),
    )(
        *grad_own,
        grad_came,
        cotangent,
        hidden,
        second_gain_row,
        router_wide,
        mask,
        prob,
        gates,
    )
    grad_attn_parts = gather_chips(grad_hidden_low)
    kept_late = [fence((keep, grad_hidden_low))[0] for keep in kept]
    total_slots = outer * slots
    row_tile = pl.BlockSpec((part_rows, unit_tile), lambda i: (0, i))
    unit_once = pl.BlockSpec((slots, hidden_units), lambda i: (0, 0))
    gate_grad, up_grad, down_grad = call(
        functools.partial(expert_grad_kernel, outer, chips),
        (
            shape((model, hidden_units), f32),
            shape((model, hidden_units), f32),
            shape((hidden_units, model), f32),
        ),
        vmem=MORE_BYTES,
        micros=18,
        grid=(model // unit_tile,),
        in_specs=[row_tile] * (2 * outer * chips) + [unit_once] * (3 * outer),
        out_specs=[
            pl.BlockSpec((unit_tile, hidden_units), lambda i: (i, 0)),
            pl.BlockSpec((unit_tile, hidden_units), lambda i: (i, 0)),
            pl.BlockSpec((hidden_units, unit_tile), lambda i: (0, i)),
        ],
        scratch_shapes=[pltpu.VMEM((total_slots, unit_tile), bf16)] * 2
        + [pltpu.VMEM((total_slots, hidden_units), bf16)] * 3,
    )(
        *[part for i in range(2) for keep in kept_late for part in keep[i]],
        *[keep[i] for i in range(2, 5) for keep in kept_late],
    )


    def settled(s, parts):
        own, partner = settle(picks[s], parts)
        return own + swap_core(partner).astype(f32)

    moved_step = shift_outer(settled(1, after(moved[1], gate_grad)).astype(bf16))
    (
        grad_attn_parts,
        gate_grad,
        up_grad,
        down_grad,
        moved,
    ) = fence((grad_attn_parts, gate_grad, up_grad, down_grad, moved))

    grad_attn_low = jnp.concatenate(grad_attn_parts, axis=0)
    out_send, out_keep = (
        lax.dot_general(
            context, grad_attn_low, CONTRACT_ROWS, preferred_element_type=f32
        ).astype(bf16)
        for context in (context_other, context_own)
    )
    out_swapped = swap_core(out_send)
    grad_context_own, grad_context_other = (
        lax.dot_general(
            grad_attn_low, weight, CONTRACT_LAST, preferred_element_type=f32
        ).astype(bf16)
        for weight in (out_own, out_other)
    )
    out_half = (out_keep.astype(f32) + out_swapped.astype(f32)).astype(bf16)
    out_half = out_half.reshape(chips, span * rows_out, model)
    out_came = [swap_chip(out_half[r], r) for r in range(chips)]
    grad_context_own = after(grad_context_own, out_half)
    for s in range(2, outer - 1):
        moved_step = shift_outer((moved_step.astype(f32) + settled(s, moved[s])).astype(bf16))
    moved_last = spread(move(outer - 1, grad_context_other))
    grad_front_low, gain_terms = call(
        functools.partial(attend_back_kernel, scale),
        (shape((together, columns), bf16), shape((2, width), f32)),
        micros=18,
        grid=(chips,),
        in_specs=[
            blocks(columns),
            blocks(group_columns),
            blocks(width),
            blocks(width),
            blocks(half_columns),
            blocks(half_columns),
            blocks(width),
            blocks(width),
            blocks(count),
            once,
            once,
            order_once,
        ],
        out_specs=[blocks(columns), pl.BlockSpec((2, width), lambda b: (0, 0))],
        scratch_shapes=[pltpu.VMEM((count, group_columns), bf16)],
    )(
        projected,
        query_low,
        key_low,
        value_low,
        grad_context_own,
        grad_context_other,
        cosine_table,
        sine_table,
        allowed,
        query_gain_row,
        key_gain_row,
        out_order,
    )

    grad_front_low, gain_terms, out_came, moved_last, moved_step = fence(
        (grad_front_low, gain_terms, out_came, moved_last, moved_step)
    )

    half_model = model // CORES
    front_send, front_keep = (
        lax.dot_general(
            normed_low[:, k * half_model : (k + 1) * half_model],
            grad_front_low,
            CONTRACT_ROWS,
            preferred_element_type=f32,
        ).astype(bf16)
        for k in (1, 0)
    )
    front_half = (front_keep.astype(f32) + swap_core(front_send).astype(f32)).astype(bf16)
    front_half = front_half.reshape(outer, chips * depth, columns)
    moved_step = shift_outer(
        (moved_step.astype(f32) + settled(outer - 1, moved_last)).astype(bf16)
    )
    out_whole = jnp.stack(out_came).reshape(outer, rows_out, model)
    router_part = lax.dot_general(
        after(grad_logits_low, front_send)[:, :experts],
        second_wide[:, :model],
        CONTRACT_ROWS,
        preferred_element_type=f32,
    )
    router_part = scatter_outer(
        lambda o: lax.dynamic_slice_in_dim(router_part, o * (plane * depth), plane * depth, 1)
    )

    def out_slice(s):
        target = (my_outer - s) % outer
        return lax.dynamic_index_in_dim(
            out_whole, ((target // span) ^ my_chip) * span + target % span, 0, keepdims=False
        )

    def next_step(step, part):
        return shift_outer((step.astype(f32) + part.astype(f32)).astype(bf16))

    out_first = out_slice(1)
    front_half, grad_front_late, out_first = fence((front_half, grad_front_low, out_first))
    front_step, out_step = shift_outer(front_half[1]), shift_outer(out_first)
    piece_block = pl.BlockSpec((1, chips * depth, columns), lambda s, o: (s, 0, 0))
    grad_normed = pl.pallas_call(
        project_back_kernel,
        out_shape=shape((together, model), bf16),
        grid_spec=pltpu.PrefetchScalarGridSpec(
            num_scalar_prefetch=1,
            grid=(outer,),
            in_specs=[
                pl.BlockSpec((together, columns), lambda s, o: (0, 0)),
                piece_block,
                piece_block,
                pl.BlockSpec((plane * depth, plane * depth), lambda s, o: (0, 0)),
            ],
            out_specs=pl.BlockSpec(
                (together, plane * depth), lambda s, o: (0, lax.rem(o[0] + outer - s, outer))
            ),
        ),
        compiler_params=pltpu.CompilerParams(vmem_limit_bytes=VMEM_BYTES),
    )(
        outer_scalar,
        grad_front_late,
        jnp.stack(front_pieces),
        jnp.stack(front_others),
        front_order,
    )
    came = [swap_chip(grad_normed[r * count : (r + 1) * count], r) for r in range(1, chips)]
    grad_home = grad_normed[:count]
    front_step, out_step, came, grad_home, moved_step, router_part = fence(
        (front_step, out_step, came, grad_home, moved_step, router_part)
    )
    for s in range(2, outer):
        front_step = next_step(front_step, front_half[s])
        out_step = next_step(out_step, out_slice(s))
        if s == 2:
            moved_home = spread(move(0, moved_step))
            tokens_grad, first_gain_term = call(
                tokens_back_kernel,
                (shape((count, model), f32), shape((1, model), f32)),
            )(tokens, grad_home, *came, grad_hidden, first_gain_row)
            gain_sums = jnp.concatenate(
                [first_gain_term.reshape(-1), second_gain_term.reshape(-1), gain_terms.reshape(-1)]
            ).reshape(-1, LANES)
            gain_sums = gain_sums + swap_core(gain_sums)
            router_part = sum(
                [
                    swap_chip(
                        lax.dynamic_slice_in_dim(
                            router_part, (my_chip ^ r) * (CORES * depth), CORES * depth, 1
                        ),
                        r,
                    )
                    for r in range(chips)
                ]
            )
            front_step, out_step, moved_home, gain_sums, tokens_grad, router_part = fence(
                (front_step, out_step, moved_home, gain_sums, tokens_grad, router_part)
            )
            router_grad = (
                lax.dynamic_slice_in_dim(router_part, my_core * depth, depth, 1)
                + swap_core(lax.dynamic_slice_in_dim(router_part, (1 - my_core) * depth, depth, 1))
            ).T
            gain_sums = sum([swap_chip(gain_sums, r) for r in range(1, chips)], gain_sums)
            output = (hidden + settled(0, moved_home) + moved_step.astype(f32)).astype(bf16)
        else:
            front_step, out_step = fence((front_step, out_step))
    gain_sums, output, front_step, out_step = fence((gain_sums, output, front_step, out_step))
    gain_sums = sum([shift_outer(gain_sums, s) for s in range(1, outer)], gain_sums).reshape(-1)
    front = (front_step.astype(f32) + front_half[0].astype(f32)).astype(bf16)
    front = front.reshape(chips, depth, columns)
    front = by_chip([swap_chip(front[r], r) for r in range(chips)])
    out_grad = out_step.astype(f32) + out_slice(0).astype(f32)

    def lay_out(first, last):
        return jnp.concatenate([part[:, first:last] for part in front], axis=1).astype(f32)

    query_grad = lay_out(0, group_columns)
    key_grad = lay_out(group_columns, group_columns + width)
    value_grad = lay_out(group_columns + width, columns)
    return (
        output,
        tokens_grad,
        query_grad,
        key_grad,
        value_grad,
        out_grad,
        router_grad,
        gate_grad[None],
        up_grad[None],
        down_grad[None],
        gain_sums[:model],
        gain_sums[model : 2 * model],
        gain_sums[2 * model : 2 * model + width],
        gain_sums[2 * model + width :],
    )


def solution(mesh):
    rows = P("fsdp", None)
    blocks = P("fsdp", None, None)
    placed = (rows,) * 9 + (blocks,) * 3 + (P(),) * 4
    return jax.shard_map(
        body,
        mesh=mesh,
        in_specs=placed,
        out_specs=(rows,) * 7 + (blocks,) * 3 + (P(),) * 4,
        check_vma=False,
    )
```

```python
import functools

import jax
import jax.numpy as jnp
from jax import lax
from jax.experimental import pallas as pl
from jax.experimental.pallas import tpu as pltpu
from jax.sharding import PartitionSpec as P

EPS = 1e-06
THETA = 1000000.0
NEGATIVE = -1e30
CORES = 2
LANES = 128
MEBIBYTE = 1024 * 1024
FLOPS_A_MICRO = 1_000_000_000
BYTES_A_MICRO = 2_000_000
CONTRACT_ROWS = (((0,), (0,)), ((), ()))
CONTRACT_LAST = (((1,), (1,)), ((), ()))


def root_mean_square_norm(value_rows, gain):
    return (
        value_rows
        * lax.rsqrt(jnp.mean(value_rows * value_rows, axis=-1, keepdims=True) + EPS)
        * gain
    )


def sequence_layout(lengths, count_total):
    ends = jnp.cumsum(lengths)
    starts = ends - lengths
    places = jnp.arange(count_total, dtype=jnp.int32)
    member = ((places[:, None] >= starts[None, :]) & (places[:, None] < ends[None, :])).astype(
        jnp.int32
    )
    labels = jnp.arange(lengths.shape[0], dtype=jnp.int32)
    segment = jnp.sum(member * labels[None, :], axis=1)
    offset = jnp.sum(member * starts[None, :], axis=1)
    return (segment, places - offset)


def rotary_tables(position, width):
    half = width // 2
    inverse = jnp.power(THETA, -(jnp.arange(half, dtype=jnp.float32) * 2.0) / width)
    angle = position.astype(jnp.float32)[:, None] * inverse[None, :]
    angle = jnp.concatenate([angle, angle], axis=1)
    return (jnp.cos(angle), jnp.sin(angle))


def call(kernel, outs, mebibytes=32, micros=0, **specs):
    if micros:
        specs["cost_estimate"] = pl.CostEstimate(
            flops=micros * FLOPS_A_MICRO, bytes_accessed=micros * BYTES_A_MICRO, transcendentals=0
        )
    return pl.pallas_call(
        kernel,
        out_shape=outs,
        compiler_params=pltpu.CompilerParams(vmem_limit_bytes=mebibytes * MEBIBYTE),
        **specs,
    )


def turned_sine(sine_table):
    half = sine_table.shape[1] // 2
    return jnp.concatenate([-sine_table[:, :half], sine_table[:, half:]], axis=1)


def head_rotated(value, gain, cosine, sine):
    normal = (
        value * lax.rsqrt(jnp.mean(value * value, axis=-1, keepdims=True) + EPS) * gain
    )
    return normal * cosine + pltpu.roll(normal, value.shape[1] // 2, 1) * sine


def head_shares(query, key, allowed, scale):
    scores = lax.dot_general(query, key, CONTRACT_LAST, preferred_element_type=jnp.float32)
    scores = jnp.where(allowed, scores * scale, NEGATIVE)
    exponent = jnp.exp(scores - jnp.max(scores, axis=-1, keepdims=True))
    return exponent / jnp.sum(exponent, axis=-1, keepdims=True)


def norm_kernel(outer, my_outer, *refs):
    *parts, gain, order, out, normed = refs
    count = parts[0].shape[0]
    span = order.shape[0]
    half = span // CORES
    for b, part in enumerate(parts):
        normed[b * count : (b + 1) * count, :] = root_mean_square_norm(
            part[...].astype(jnp.float32), gain[...]
        ).astype(jnp.bfloat16)
    for s in range(outer):
        start = lax.rem(my_outer[0] + (outer - s), outer) * span
        block = normed[:, pl.ds(pl.multiple_of(start, LANES), span)]
        block = jnp.dot(block, order[...], preferred_element_type=jnp.float32)
        block = block.astype(jnp.bfloat16)
        for k in range(CORES):
            first = (k * outer + s) * half
            out[:, first : first + half] = block[:, k * half : (k + 1) * half]


def project_kernel(normed, *refs):
    *pieces, out = refs
    rows = pieces[0].shape[0]
    total = jnp.zeros(out.shape, jnp.float32)
    for i, piece in enumerate(pieces):
        total += jnp.dot(
            normed[:, i * rows : (i + 1) * rows], piece[...], preferred_element_type=jnp.float32
        )
    out[...] = total


def project_back_kernel(outer, my_outer, grad, *refs):
    *pieces, order, out = refs
    f32, bf16 = jnp.float32, jnp.bfloat16
    for s in range(outer):

        @pl.when(pl.program_id(0) == s)
        def _(s=s):
            block = jnp.concatenate(
                [
                    lax.dot_general(
                        grad[...], part[...], CONTRACT_LAST, preferred_element_type=f32
                    )
                    for part in pieces[s::outer]
                ],
                axis=1,
            ).astype(bf16)
            out[...] = lax.dot_general(
                block, order[...], CONTRACT_LAST, preferred_element_type=f32
            ).astype(bf16)


def router_order_kernel(outer, experts, my_outer, *refs):
    *pieces, order, out = refs
    span = order.shape[0]
    column = lax.broadcasted_iota(jnp.int32, (span, out.shape[1]), 1)
    for s in range(outer):
        block = jnp.concatenate([part[...] for part in pieces[s::outer]], axis=0)
        block = jnp.dot(order[...], block, preferred_element_type=jnp.float32)
        start = pl.multiple_of(lax.rem(my_outer[0] + (outer - s), outer) * span, LANES)
        out[pl.ds(start, span), :] = jnp.where(column < experts, block, 0.0).astype(jnp.bfloat16)


def gain_back_kernel(grad, *refs):
    *parts, gain_grad = refs
    count = parts[0].shape[0]
    total = jnp.zeros(gain_grad.shape, jnp.float32)
    for b, part in enumerate(parts):
        value = part[...].astype(jnp.float32)
        root = lax.rsqrt(jnp.mean(value * value, axis=-1, keepdims=True) + EPS)
        rows = grad[b * count : (b + 1) * count, :].astype(jnp.float32)
        total += jnp.sum(rows * value * root, axis=0, keepdims=True)
    gain_grad[...] = total


def tokens_back_kernel(tokens, own, *refs):
    *others, hidden_grad, gain, tokens_grad = refs
    f32 = jnp.float32
    grad = own[...].astype(f32)
    for other in others:
        grad = grad + other[...].astype(f32)
    value = tokens[...].astype(f32)
    root = lax.rsqrt(jnp.mean(value * value, axis=-1, keepdims=True) + EPS)
    normal = value * root
    grad = grad * gain[...]
    tokens_grad[...] = hidden_grad[...] + root * (
        grad - normal * jnp.mean(normal * grad, axis=-1, keepdims=True)
    )


def attend_kernel(scale, front, cosine, sine, allowed, query_gain, key_gain, order, *outs):
    query_out, key_out, value_out, context_out, context = outs
    width = cosine.shape[1]
    heads = query_out.shape[1] // width
    bf16 = jnp.bfloat16
    cos, sin = cosine[...], sine[...]
    open_places = allowed[...] > 0.0
    key = head_rotated(
        front[:, heads * width : (heads + 1) * width], key_gain[...], cos, sin
    ).astype(bf16)
    value = front[:, (heads + 1) * width :].astype(bf16)
    key_out[...] = key
    value_out[...] = value
    for h in range(heads):
        part = slice(h * width, (h + 1) * width)
        query = head_rotated(front[:, part], query_gain[...], cos, sin).astype(bf16)
        query_out[:, part] = query
        shares = head_shares(query, key, open_places, scale).astype(bf16)
        context[:, part] = jnp.dot(
            shares, value, preferred_element_type=jnp.float32
        ).astype(bf16)
    context_out[...] = jnp.dot(
        context[...], order[...], preferred_element_type=jnp.float32
    ).astype(bf16)


def head_back(grad, value, gain, cosine, sine):
    grad = grad * cosine + pltpu.roll(grad * sine, value.shape[1] // 2, 1)
    root = lax.rsqrt(jnp.mean(value * value, axis=-1, keepdims=True) + EPS)
    normal = value * root
    gain_grad = jnp.sum(grad * normal, axis=0, keepdims=True)
    grad = grad * gain
    grad = root * (grad - normal * jnp.mean(normal * grad, axis=-1, keepdims=True))
    return grad, gain_grad


def attend_back_kernel(
    scale, front, query_in, key_in, value_in, grad_own, grad_other, cosine, sine, allowed, *rest
):
    query_gain, key_gain, order, front_grad, gain_grads, context_grad = rest
    half = grad_own.shape[1]
    context_grad[...] = (
        lax.dot_general(
            grad_own[...], order[:, :half], CONTRACT_LAST, preferred_element_type=jnp.float32
        )
        + lax.dot_general(
            grad_other[...], order[:, half:], CONTRACT_LAST, preferred_element_type=jnp.float32
        )
    ).astype(jnp.bfloat16)
    width = cosine.shape[1]
    heads = query_in.shape[1] // width
    f32, bf16 = jnp.float32, jnp.bfloat16
    cos, sin = cosine[...], sine[...]
    open_places = allowed[...] > 0.0
    key, value = key_in[...], value_in[...]
    key_total = jnp.zeros(key.shape, f32)
    value_total = jnp.zeros(key.shape, f32)
    gain_total = jnp.zeros((1, width), f32)
    for h in range(heads):
        part = slice(h * width, (h + 1) * width)
        query, grad = query_in[:, part], context_grad[:, part]
        shares = head_shares(query, key, open_places, scale)
        grad_shares = lax.dot_general(grad, value, CONTRACT_LAST, preferred_element_type=f32)
        grad_scores = (
            shares * (grad_shares - jnp.sum(shares * grad_shares, axis=-1, keepdims=True))
        ).astype(bf16)
        value_total += lax.dot_general(
            shares.astype(bf16), grad, CONTRACT_ROWS, preferred_element_type=f32
        )
        key_total += lax.dot_general(
            grad_scores, query, CONTRACT_ROWS, preferred_element_type=f32
        )
        grad_query = jnp.dot(grad_scores, key, preferred_element_type=f32) * scale
        grad_query, gain_grad = head_back(grad_query, front[:, part], query_gain[...], cos, sin)
        front_grad[:, part] = grad_query.astype(bf16)
        gain_total += gain_grad
    part = slice(heads * width, (heads + 1) * width)
    grad_key, key_gain_grad = head_back(
        key_total * scale, front[:, part], key_gain[...], cos, sin
    )
    front_grad[:, part] = grad_key.astype(bf16)
    front_grad[:, (heads + 1) * width :] = value_total.astype(bf16)

    @pl.when(pl.program_id(0) == 0)
    def _():
        gain_grads[...] = jnp.zeros(gain_grads.shape, f32)

    gain_grads[0:1, :] += gain_total
    gain_grads[1:2, :] += key_gain_grad


def router_kernel(experts, *refs):
    tokens, own, *others, gain, router, mask, hidden_out, wide_out, prob_out, gates_out = refs
    f32, bf16 = jnp.float32, jnp.bfloat16
    model = tokens.shape[1]
    lanes = mask.shape[1]
    hidden = tokens[...].astype(f32) + own[...]
    for other in others:
        hidden = hidden + other[...].astype(f32)
    hidden_out[...] = hidden
    second = root_mean_square_norm(hidden, gain[...]).astype(bf16)
    wide_out[:, :model] = second
    logits = jnp.dot(second, router[...], preferred_element_type=f32)
    column = lax.broadcasted_iota(jnp.int32, logits.shape, 1)
    logits = jnp.where(column < experts, logits, NEGATIVE)
    exponent = jnp.exp(logits - jnp.max(logits, axis=-1, keepdims=True))
    prob = exponent / jnp.sum(exponent, axis=-1, keepdims=True)
    chosen = prob * mask[...]
    gates = chosen / jnp.sum(chosen, axis=-1, keepdims=True)
    prob_out[...] = prob
    gates_out[...] = gates
    high = gates.astype(bf16).astype(f32)
    low = gates - high
    if 2 * experts <= lanes:
        wide_out[:, model:] = (high + pltpu.roll(low, experts, 1)).astype(bf16)
    else:
        wide_out[:, model : model + lanes] = high.astype(bf16)
        wide_out[:, model + lanes :] = low.astype(bf16)


def router_back_kernel(experts, *refs):
    own, near, came, cotangent, hidden, gain, router, mask, prob, gates, *outs = refs
    hidden_grad, attn_grad, logits_grad, gain_grad = outs
    f32, bf16 = jnp.float32, jnp.bfloat16
    model = cotangent.shape[1]
    lanes = mask.shape[1]
    pairs = own[:, model:] + near[:, model:].astype(f32) + came[:, model:].astype(f32)
    if 2 * experts <= lanes:
        grad_gates = pairs + pltpu.roll(pairs, lanes - experts, 1)
    else:
        grad_gates = pairs[:, :lanes] + pairs[:, lanes:]
    chosen_sum = jnp.sum(prob[...] * mask[...], axis=-1, keepdims=True)
    grad_gates = jnp.where(mask[...] > 0.0, grad_gates, 0.0)
    grad_chosen = (
        mask[...]
        * (grad_gates - jnp.sum(gates[...] * grad_gates, axis=-1, keepdims=True))
        / chosen_sum
    )
    grad_logits = (
        prob[...] * (grad_chosen - jnp.sum(prob[...] * grad_chosen, axis=-1, keepdims=True))
    ).astype(bf16)
    logits_grad[...] = grad_logits
    grad = (
        own[:, :model]
        + near[:, :model].astype(f32)
        + came[:, :model].astype(f32)
        + lax.dot_general(grad_logits, router[...], CONTRACT_LAST, preferred_element_type=f32)
    )
    value = hidden[...]
    root = lax.rsqrt(jnp.mean(value * value, axis=-1, keepdims=True) + EPS)
    normal = value * root
    gain_grad[...] = jnp.sum(grad * normal, axis=0, keepdims=True)
    grad = grad * gain[...]
    grad = cotangent[...].astype(f32) + root * (
        grad - normal * jnp.mean(normal * grad, axis=-1, keepdims=True)
    )
    hidden_grad[...] = grad
    attn_grad[...] = grad.astype(bf16)


def pick_kernel(capacity, own, partner, near, earlier, *outs):
    *parts, picks = outs
    f32, bf16 = jnp.float32, jnp.bfloat16
    rows, model = parts[0].shape
    count = own.shape[0]
    masks = [
        lax.dot_general(near[...], side[:, model:], CONTRACT_LAST, preferred_element_type=f32)
        for side in (own, partner)
    ]
    ranks = [jnp.dot(m.astype(bf16), earlier[...], preferred_element_type=f32) for m in masks]
    mask = jnp.concatenate(masks, axis=1)
    rank = jnp.concatenate([ranks[0], ranks[1] + capacity], axis=1)
    place = lax.broadcasted_iota(jnp.int32, (rows, CORES * count), 0).astype(f32)
    for r in range(len(parts)):
        hit = (place == rank[r : r + 1, :]) & (mask[r : r + 1, :] > 0.5)
        picks[r * rows : (r + 1) * rows, :] = jnp.where(hit, 1.0, 0.0).astype(bf16)
    both = jnp.concatenate([own[:, :model], partner[:, :model]], axis=0)
    chosen = jnp.dot(picks[...], both, preferred_element_type=f32).astype(bf16)
    for r, part in enumerate(parts):
        part[...] = chosen[r * rows : (r + 1) * rows, :]


def send_kernel(picks, own, partner, *parts):
    rows = parts[0].shape[0]
    both = jnp.concatenate([own[...], partner[...]], axis=0)
    chosen = jnp.dot(picks[...], both, preferred_element_type=jnp.float32).astype(jnp.bfloat16)
    for r, part in enumerate(parts):
        part[...] = chosen[r * rows : (r + 1) * rows, :]


def settle_kernel(picks, *refs):
    *parts, own, partner = refs
    count = own.shape[0]
    rows = jnp.concatenate([part[...] for part in parts], axis=0)
    total = lax.dot_general(
        picks[...], rows, CONTRACT_ROWS, preferred_element_type=jnp.float32
    )
    own[...] = total[:count, :]
    partner[...] = total[count:, :].astype(jnp.bfloat16)


def move_kernel(units, weight, *parts):
    rows = parts[0].shape[0]
    moved = jnp.dot(units[...], weight[...], preferred_element_type=jnp.float32)
    for r, part in enumerate(parts):
        part[...] = moved[r * rows : (r + 1) * rows, :].astype(jnp.bfloat16)


def expert_kernel(chips, experts, me, *refs):
    f32, bf16 = jnp.float32, jnp.bfloat16
    came, given = refs[:chips], refs[chips : 2 * chips]
    gate_weight, up_weight, down_weight = refs[2 * chips : 2 * chips + 3]
    back = refs[2 * chips + 3 : 3 * chips + 3]
    units_out, gate_out, up_out, rows, grads, row_gate, change, total = refs[3 * chips + 3 :]
    size, model = came[0].shape[0], rows.shape[1]
    step = pl.program_id(0)
    column = lax.broadcasted_iota(jnp.int32, (size, came[0].shape[1] - model), 1)
    high_column, low_column = column == me[0], column == me[0] + experts

    @pl.when(step == 0)
    def _():
        for r in range(chips):
            part = slice(r * size, (r + 1) * size)
            rows[part, :] = came[r][:, :model]
            grads[part, :] = given[r][...]
            side = jnp.where(high_column | low_column, came[r][:, model:].astype(f32), 0.0)
            row_gate[part, :] = jnp.sum(side, axis=1, keepdims=True)
        change[...] = jnp.zeros(change.shape, f32)
        total[...] = jnp.zeros(total.shape, f32)

    gate_part = jnp.dot(rows[...], gate_weight[...], preferred_element_type=f32)
    up_part = jnp.dot(rows[...], up_weight[...], preferred_element_type=f32)
    raw = lax.dot_general(
        grads[...], down_weight[...], CONTRACT_LAST, preferred_element_type=f32
    )
    sig = 1.0 / (1.0 + jnp.exp(-gate_part))
    silu = gate_part * sig
    units = silu * up_part
    change[...] += jnp.sum(units * raw, axis=1, keepdims=True)
    units_out[...] = (row_gate[...] * units).astype(bf16)
    grad_units = row_gate[...] * raw
    gate_grad = (grad_units * up_part * sig * (1.0 + gate_part * (1.0 - sig))).astype(bf16)
    up_grad = (grad_units * silu).astype(bf16)
    gate_out[...] = gate_grad
    up_out[...] = up_grad
    total[...] += lax.dot_general(
        gate_grad, gate_weight[...], CONTRACT_LAST, preferred_element_type=f32
    ) + lax.dot_general(up_grad, up_weight[...], CONTRACT_LAST, preferred_element_type=f32)

    @pl.when(step == pl.num_programs(0) - 1)
    def _():
        for r in range(chips):
            part = slice(r * size, (r + 1) * size)
            back[r][:, :model] = total[part, :].astype(bf16)
            high = change[part, :].astype(bf16).astype(f32)
            low = change[part, :] - high
            back[r][:, model:] = (
                jnp.where(high_column, high, 0.0) + jnp.where(low_column, low, 0.0)
            ).astype(bf16)


def expert_grad_kernel(outer, chips, *refs):
    f32 = jnp.float32
    parts = outer * chips
    rows, grads = refs[:parts], refs[parts : 2 * parts]
    units, gates, ups = (
        refs[2 * parts + i * outer : 2 * parts + (i + 1) * outer] for i in range(3)
    )
    gate_out, up_out, down_out, left, right, all_units, all_gates, all_ups = refs[
        2 * parts + 3 * outer :
    ]
    size = rows[0].shape[0]
    for i in range(parts):
        part = slice(i * size, (i + 1) * size)
        left[part, :] = rows[i][...]
        right[part, :] = grads[i][...]
    size = units[0].shape[0]

    @pl.when(pl.program_id(0) == 0)
    def _():
        for s in range(outer):
            part = slice(s * size, (s + 1) * size)
            all_units[part, :] = units[s][...]
            all_gates[part, :] = gates[s][...]
            all_ups[part, :] = ups[s][...]

    def product(a, b):
        return lax.dot_general(a[...], b[...], CONTRACT_ROWS, preferred_element_type=f32)

    gate_out[...] = product(left, all_gates)
    up_out[...] = product(left, all_ups)
    down_out[...] = product(all_units, right)


def round_up(number, step):
    return -(-number // step) * step


def after(value, *others):
    return lax.optimization_barrier((value, *others))[0]


def body(
    tokens,
    cotangent,
    lengths,
    routes,
    query_weight,
    key_matrix,
    value_matrix,
    out_weight,
    router_weight,
    expert_gate,
    expert_up,
    expert_down,
    first_gain,
    second_gain,
    query_norm_gain,
    key_gain,
):
    f32, bf16, i32 = jnp.float32, jnp.bfloat16, jnp.int32
    shape = jax.ShapeDtypeStruct
    fence = lax.optimization_barrier
    count, model = tokens.shape
    width = query_norm_gain.shape[0]
    heads = query_weight.shape[1] // width
    kv_heads = key_matrix.shape[1] // width
    head_group = heads // kv_heads
    choose = routes.shape[1]
    shards = lax.axis_size("fsdp")
    experts = shards * expert_gate.shape[0]
    capacity = max(2, count * choose * 5 // (4 * experts))
    scale = width ** (-0.5)

    chips = kv_heads
    plane = chips * CORES
    outer = shards // plane
    span = outer // chips
    me = lax.axis_index("fsdp")
    my_core = me % CORES
    my_chip = (me // CORES) % chips
    my_outer = me // plane
    me_scalar = me.reshape(1)
    outer_scalar = my_outer.reshape(1)
    smem = pl.BlockSpec(memory_space=pltpu.SMEM)
    vmem = pl.BlockSpec(memory_space=pltpu.VMEM)

    def swap_core(value):
        return lax.ppermute(value, "fsdp", [(i, i ^ 1) for i in range(shards)])

    def swap_chip(value, r):
        if r == 0:
            return value
        return lax.ppermute(value, "fsdp", [(i, i ^ (r * CORES)) for i in range(shards)])

    def shift_outer(value, s=1):
        if s == 0:
            return value
        return lax.ppermute(
            value,
            "fsdp",
            [(i, ((i // plane + s) % outer) * plane + i % plane) for i in range(shards)],
        )

    def gather_chips(value):
        return [swap_chip(value, r) for r in range(chips)]

    def spread(parts):
        return [swap_chip(part, r) for r, part in enumerate(parts)]

    def scatter_outer(take):
        total = take(my_outer)
        for s in range(1, outer):
            total = total + shift_outer(take((my_outer + s) % outer), s)
        return total

    def by_chip(parts):
        parts = jnp.stack(parts)
        return [
            lax.dynamic_index_in_dim(parts, my_chip ^ m, 0, keepdims=False) for m in range(chips)
        ]

    depth = query_weight.shape[0]
    group_columns = head_group * width
    half_columns = group_columns // CORES
    columns = group_columns + 2 * width
    rows_out = out_weight.shape[0]

    lanes = round_up(experts, LANES)
    pair_width = round_up(2 * experts, LANES)
    part_rows = round_up(CORES * capacity, 16)
    slots = chips * part_rows

    def dispatch_first(piece, partner):
        *parts, picks = call(
            functools.partial(pick_kernel, capacity),
            [shape((part_rows, model), bf16)] * chips + [shape((slots, CORES * count), bf16)],
            mebibytes=16,
        )(piece, partner, near, earlier)
        return parts, picks

    def dispatch(picks, piece, partner):
        outs = [shape((part_rows, piece.shape[1]), bf16)] * chips
        return call(send_kernel, outs, mebibytes=16)(picks, piece, partner)

    def settle(picks, parts):
        columns_of = parts[0].shape[1]
        return call(
            settle_kernel,
            (shape((count, columns_of), f32), shape((count, columns_of), bf16)),
            mebibytes=16,
        )(picks, *parts)

    together = chips * count
    first_gain_row, second_gain_row = first_gain[None, :], second_gain[None, :]
    query_gain_row, key_gain_row = query_norm_gain[None, :], key_gain[None, :]

    def norm(token_parts):
        return call(
            functools.partial(norm_kernel, outer),
            shape((together, model), bf16),
            in_specs=[smem] + [vmem] * (chips + 2),
            scratch_shapes=[pltpu.VMEM((together, model), bf16)],
        )(outer_scalar, *token_parts, first_gain_row, front_order)

    def positions(length_parts):
        layouts = [sequence_layout(part[0], count) for part in length_parts]
        segment = jnp.stack([layout[0] for layout in layouts])
        position = jnp.concatenate([layout[1] for layout in layouts])
        cosine_table, sine_table = rotary_tables(position, width)
        sine_table = turned_sine(sine_table)
        places = jnp.arange(count, dtype=i32)
        allowed = (segment[:, :, None] == segment[:, None, :]) & (
            places[None, None, :] <= places[None, :, None]
        )
        return cosine_table, sine_table, allowed.astype(f32).reshape(together, count)

    sequences = lengths.shape[1]
    side_width = round_up(experts + sequences, LANES)
    side = jnp.pad(router_weight, ((0, 0), (0, side_width - experts))) + jnp.pad(
        lengths.astype(bf16), ((0, depth - 1), (experts, side_width - experts - sequences))
    )
    cut = []
    for r in range(chips):
        target = my_chip ^ r
        part = [
            lax.dynamic_slice_in_dim(query_weight, target * group_columns, group_columns, 1),
            lax.dynamic_slice_in_dim(key_matrix, target * width, width, 1),
            lax.dynamic_slice_in_dim(value_matrix, target * width, width, 1),
            side,
        ]
        cut.append(swap_chip(jnp.concatenate(part, axis=1), r))
    out_pieces = [out_weight, shift_outer(out_weight)]
    front_pieces, front_others = [], []
    state = fence((cut, out_pieces, routes, tokens, cotangent))
    cut, out_pieces, routes, tokens, cotangent = state
    length_parts = [
        part[:1, columns + experts : columns + experts + sequences].astype(i32) for part in cut
    ]
    cut = jnp.concatenate(cut, axis=0)
    me = after(me, cut)
    my_core, my_chip, my_outer = me % CORES, (me // CORES) % chips, me // plane

    def arrival_order(length, block, inner):
        place = jnp.arange(length, dtype=i32)
        went_to = (
            (
                ((place // block % CORES) ^ my_core) * chips
                + ((place // (block * CORES) % chips) ^ my_chip)
            )
            * inner
            + place // (block * plane)
        ) * block + place % block
        return (went_to[:, None] == place[None, :]).astype(bf16)

    front_order = arrival_order(plane * depth, depth, 1)
    out_order = arrival_order(group_columns, rows_out, span)

    mask = jnp.sum(
        (routes[:, :, None] == jnp.arange(lanes, dtype=i32)[None, None, :]).astype(f32), axis=1
    )
    near = jnp.arange(2 * chips, dtype=i32)
    near = jnp.where(
        near < chips, my_outer * plane + (my_chip ^ near) * CORES + my_core, -1
    )
    near = (near[:, None] == jnp.arange(lanes, dtype=i32)[None, :]).astype(bf16)
    earlier = jnp.triu(jnp.ones((count, count), bf16), 1)
    cotangent_wide = jnp.concatenate([cotangent, mask.astype(bf16)], axis=1)
    cotangent_pieces, cotangent_parts, picks = [cotangent_wide], [], []
    cotangent_partners = []

    def send_cotangent(s):
        parts, pick = dispatch_first(cotangent_pieces[s], cotangent_partners[s])
        cotangent_parts.append(spread(parts))
        picks.append(pick)

    front_pieces.append(cut)
    for t in range(2, outer + 1):
        front_pieces.append(shift_outer(front_pieces[-1]))
        if t < outer:
            out_pieces.append(shift_outer(out_pieces[-1]))
        front_others.append(swap_core(front_pieces[-2]))
        if t == 2:
            token_parts = gather_chips(tokens)
            cotangent_partners.append(swap_core(cotangent_pieces[0]))
            state = (token_parts, cotangent_partners, positions(length_parts))
            state = fence((state, front_pieces, front_others, out_pieces))
            (token_parts, cotangent_partners, tables), *state = state
            cosine_table, sine_table, allowed = tables
        elif t == 3:
            send_cotangent(0)
            normed_low = norm(token_parts)
            state = (cotangent_parts, picks, normed_low)
            state = fence((state, front_pieces, front_others, out_pieces))
            (cotangent_parts, picks, normed_low), *state = state
        elif t < outer:
            state = fence((front_pieces, front_others, out_pieces))
        else:
            cotangent_pieces.append(shift_outer(cotangent_pieces[0]))
            stacked = jnp.stack(out_pieces)
            out_own = []
            for r in range(chips):
                part = [
                    lax.dynamic_index_in_dim(
                        stacked,
                        (my_outer + outer - ((my_chip ^ r) * span + u)) % outer,
                        0,
                        keepdims=False,
                    )
                    for u in range(span)
                ]
                out_own.append(swap_chip(jnp.concatenate(part, axis=0), r))
            state = fence((front_pieces, front_others, out_pieces))
        front_pieces, front_others, out_pieces = state
    cotangent_pieces, out_own = fence((cotangent_pieces, out_own))

    front_others.append(swap_core(front_pieces[-1]))
    cotangent_partners.append(swap_core(cotangent_pieces[1]))
    out_own = jnp.concatenate(out_own, axis=0)
    front_others, cotangent_partners, out_own = fence((front_others, cotangent_partners, out_own))
    out_other = swap_core(out_own)
    for s in range(2, outer - 1):
        cotangent_pieces.append(shift_outer(cotangent_pieces[-1]))
    tile = 2 * width
    projected = call(
        project_kernel,
        shape((together, columns), f32),
        grid=(columns // tile,),
        in_specs=[pl.BlockSpec((together, model), lambda n: (0, 0))]
        + [pl.BlockSpec((chips * depth, tile), lambda n: (0, n))] * (CORES * outer),
        out_specs=pl.BlockSpec((together, tile), lambda n: (0, n)),
    )(normed_low, *front_pieces, *front_others)

    cotangent_pieces[1] = after(cotangent_pieces[1], projected)
    send_cotangent(1)

    def blocks(columns_of):
        return pl.BlockSpec((count, columns_of), lambda b: (b, 0))

    once = pl.BlockSpec((1, width), lambda b: (0, 0))
    order_once = pl.BlockSpec((group_columns, group_columns), lambda b: (0, 0))
    query_low, key_low, value_low, context_low = call(
        functools.partial(attend_kernel, scale),
        (
            shape((together, group_columns), bf16),
            shape((together, width), bf16),
            shape((together, width), bf16),
            shape((together, group_columns), bf16),
        ),
        grid=(chips,),
        in_specs=[
            blocks(columns),
            blocks(width),
            blocks(width),
            blocks(count),
            once,
            once,
            order_once,
        ],
        out_specs=[blocks(group_columns), blocks(width), blocks(width), blocks(group_columns)],
        scratch_shapes=[pltpu.VMEM((count, group_columns), bf16)],
    )(projected, cosine_table, sine_table, allowed, query_gain_row, key_gain_row, out_order)
    state = (context_low, out_other, cotangent_pieces, cotangent_parts, picks)
    state = fence((state, query_low, key_low, value_low, projected))
    (context_low, out_other, cotangent_pieces, cotangent_parts, picks), *state = state
    query_low, key_low, value_low, projected = state
    context_own, context_other = context_low[:, :half_columns], context_low[:, half_columns:]

    def attended(first, last):
        return jnp.dot(
            context_own[first:last], out_own, preferred_element_type=f32
        ) + jnp.dot(context_other[first:last], out_other, preferred_element_type=f32)

    away = attended(count, together).astype(bf16)
    arrived = [swap_chip(away[(r - 1) * count : r * count], r) for r in range(1, chips)]
    home = attended(0, count)
    cotangent_pieces.append(shift_outer(cotangent_pieces[-1]))
    cotangent_partners.append(swap_core(cotangent_pieces[2]))
    router_block = pl.BlockSpec((chips * depth, lanes), lambda n: (0, columns // lanes))
    order_block = pl.BlockSpec((plane * depth, plane * depth), lambda n: (0, 0))
    router_wide = call(
        functools.partial(router_order_kernel, outer, experts),
        shape((model, lanes), bf16),
        grid=(1,),
        in_specs=[smem, *[router_block] * (CORES * outer), order_block],
        out_specs=pl.BlockSpec((model, lanes), lambda n: (0, 0)),
    )(outer_scalar, *front_pieces, *front_others, after(front_order, away))
    arrived, home, cotangent_pieces, cotangent_partners, router_wide = fence(
        (arrived, home, cotangent_pieces, cotangent_partners, router_wide)
    )
    hidden, second_wide, prob, gates = call(
        functools.partial(router_kernel, experts),
        (
            shape((count, model), f32),
            shape((count, model + pair_width), bf16),
            shape((count, lanes), f32),
            shape((count, lanes), f32),
        ),
    )(tokens, home, *arrived, second_gain_row, router_wide, mask)

    gate_weight, up_weight, down_weight = expert_gate[0], expert_up[0], expert_down[0]
    hidden_units = gate_weight.shape[1]
    unit_tile = 2 * LANES

    def expert(came, given):
        part = pl.BlockSpec((part_rows, model + pair_width), lambda f: (0, 0))
        units = pl.BlockSpec((slots, unit_tile), lambda f: (0, f))
        outs = call(
            functools.partial(expert_kernel, chips, experts),
            [shape((part_rows, model + pair_width), bf16)] * chips
            + [shape((slots, hidden_units), bf16)] * 3,
            micros=11,
            grid=(hidden_units // unit_tile,),
            in_specs=[smem]
            + [part] * chips
            + [pl.BlockSpec((part_rows, model), lambda f: (0, 0))] * chips
            + [pl.BlockSpec((model, unit_tile), lambda f: (0, f))] * 2
            + [pl.BlockSpec((unit_tile, model), lambda f: (f, 0))],
            out_specs=[part] * chips + [units] * 3,
            scratch_shapes=[
                pltpu.VMEM((slots, model), bf16),
                pltpu.VMEM((slots, model), bf16),
                pltpu.VMEM((slots, 1), f32),
                pltpu.VMEM((slots, 1), f32),
                pltpu.VMEM((slots, model), f32),
            ],
        )(me_scalar, *came, *given, gate_weight, up_weight, down_weight)
        return outs[:chips], (came, given, *outs[chips:])

    def move(s):
        return call(move_kernel, [shape((part_rows, model), bf16)] * chips, mebibytes=16)(
            kept[s][2], down_weight
        )

    second_pieces, second_partners = [second_wide], []
    came, backs, kept, returned, settled_own, settled_partner = {}, {}, {}, {}, {}, {}
    moved, moving, moved_own, moved_partner = {}, [], {}, {}
    grad_step = None
    for t in range(outer + 5):
        if 0 <= t - 1 < outer:
            sent = dispatch(picks[t - 1], second_pieces[t - 1], second_partners[t - 1])
            came[t - 1] = spread(sent)
        if 2 <= t + 2 < outer:
            send_cotangent(t + 2)
        if t + 3 < outer:
            cotangent_partners.append(swap_core(cotangent_pieces[t + 3]))
        if t + 1 < outer:
            second_pieces.append(shift_outer(second_pieces[t]))
        if t < outer:
            second_partners.append(swap_core(second_pieces[t]))
        if t - 5 >= 1:
            total = settled_own[t - 5] + settled_partner[t - 5].astype(f32)
            if grad_step is not None:
                total = total + grad_step.astype(f32)
            grad_step = shift_outer(total.astype(bf16))
        if 0 <= t - 4 < outer:
            settled_own[t - 4], partner = settle(picks[t - 4], returned[t - 4])
            settled_partner[t - 4] = swap_core(partner)
        if 0 <= t - 3 < outer:
            returned[t - 3] = spread(backs[t - 3])
        if t == outer + 2:
            moving = [move(i) for i in range(outer)]
        if t >= outer + 3:
            moved[t - outer - 2] = spread(moving[t - outer - 2])
        if t == outer + 4:
            moved_own[1], partner = settle(picks[1], moved[1])
            moved_partner[1] = swap_core(partner)
        if 0 <= t - 2 < outer:
            backs[t - 2], kept[t - 2] = expert(came[t - 2], cotangent_parts[t - 2])
        state = (second_pieces, second_partners, cotangent_partners, cotangent_parts, picks)
        state = (state, came, backs, returned, settled_own, settled_partner)
        state = fence((state, moved, moving, moved_own, moved_partner, grad_step, kept))
        state, moved, moving, moved_own, moved_partner, grad_step, kept = state
        state, came, backs, returned, settled_own, settled_partner = state
        second_pieces, second_partners, cotangent_partners, cotangent_parts, picks = state

    grad_hidden, grad_hidden_low, grad_logits_low, second_gain_term = call(
        functools.partial(router_back_kernel, experts),
        (
            shape((count, model), f32),
            shape((count, model), bf16),
            shape((count, lanes), bf16),
            shape((1, model), f32),
        ),
        mebibytes=60,
    )(
        settled_own[0],
        settled_partner[0],
        grad_step,
        cotangent,
        hidden,
        second_gain_row,
        router_wide,
        mask,
        prob,
        gates,
    )
    grad_attn_low = jnp.concatenate(gather_chips(grad_hidden_low), axis=0)
    moved_step = shift_outer((moved_own[1] + moved_partner[1].astype(f32)).astype(bf16))
    moved_own[2], partner = settle(picks[2], moved[2])
    moved_partner[2] = swap_core(partner)
    kept_late = [fence((kept[s], grad_hidden_low))[0] for s in range(outer)]
    total_slots = outer * slots
    row_tile = pl.BlockSpec((part_rows, unit_tile), lambda i: (0, i))
    unit_once = pl.BlockSpec((slots, hidden_units), lambda i: (0, 0))
    gate_grad, up_grad, down_grad = call(
        functools.partial(expert_grad_kernel, outer, chips),
        (
            shape((model, hidden_units), f32),
            shape((model, hidden_units), f32),
            shape((hidden_units, model), f32),
        ),
        mebibytes=50,
        micros=20,
        grid=(model // unit_tile,),
        in_specs=[row_tile] * (2 * outer * chips) + [unit_once] * (3 * outer),
        out_specs=[
            pl.BlockSpec((unit_tile, hidden_units), lambda i: (i, 0)),
            pl.BlockSpec((unit_tile, hidden_units), lambda i: (i, 0)),
            pl.BlockSpec((hidden_units, unit_tile), lambda i: (0, i)),
        ],
        scratch_shapes=[pltpu.VMEM((total_slots, unit_tile), bf16)] * 2
        + [pltpu.VMEM((total_slots, hidden_units), bf16)] * 3,
    )(
        *[part for i in range(2) for keep in kept_late for part in keep[i]],
        *[keep[i] for i in range(2, 5) for keep in kept_late],
    )


    router_part = lax.dot_general(
        grad_logits_low[:, :experts],
        second_wide[:, :model],
        CONTRACT_ROWS,
        preferred_element_type=f32,
    )
    router_part = scatter_outer(
        lambda o: lax.dynamic_slice_in_dim(router_part, o * (plane * depth), plane * depth, 1)
    )
    state = (grad_attn_low, gate_grad, up_grad, down_grad, moved_step, moved_own, moved_partner)
    state, router_part = fence((state, router_part))
    grad_attn_low, gate_grad, up_grad, down_grad, moved_step, moved_own, moved_partner = state

    def next_step(step, *parts):
        total = step.astype(f32)
        for part in parts:
            total = total + part.astype(f32)
        return shift_outer(total.astype(bf16))

    out_send, out_keep = (
        lax.dot_general(
            context, grad_attn_low, CONTRACT_ROWS, preferred_element_type=f32
        ).astype(bf16)
        for context in (context_other, context_own)
    )
    out_swapped = swap_core(out_send)
    grad_context_own, grad_context_other = (
        lax.dot_general(
            grad_attn_low, weight, CONTRACT_LAST, preferred_element_type=f32
        ).astype(bf16)
        for weight in (out_own, out_other)
    )
    out_keep, out_swapped, grad_context_own, grad_context_other = fence(
        (out_keep, out_swapped, grad_context_own, grad_context_other)
    )
    out_half = (out_keep.astype(f32) + out_swapped.astype(f32)).astype(bf16)
    out_half = out_half.reshape(chips, span * rows_out, model)
    out_came = [swap_chip(out_half[r], r) for r in range(chips)]
    moved_step = next_step(moved_step, moved_own[2], moved_partner[2])
    grad_front_low, gain_terms = call(
        functools.partial(attend_back_kernel, scale),
        (shape((together, columns), bf16), shape((2, width), f32)),
        micros=18,
        grid=(chips,),
        in_specs=[
            blocks(columns),
            blocks(group_columns),
            blocks(width),
            blocks(width),
            blocks(half_columns),
            blocks(half_columns),
            blocks(width),
            blocks(width),
            blocks(count),
            once,
            once,
            order_once,
        ],
        out_specs=[blocks(columns), pl.BlockSpec((2, width), lambda b: (0, 0))],
        scratch_shapes=[pltpu.VMEM((count, group_columns), bf16)],
    )(
        projected,
        query_low,
        key_low,
        value_low,
        grad_context_own,
        grad_context_other,
        cosine_table,
        sine_table,
        allowed,
        query_gain_row,
        key_gain_row,
        out_order,
    )

    grad_front_low, gain_terms, out_came, moved_step, router_part = fence(
        (grad_front_low, gain_terms, out_came, moved_step, router_part)
    )

    half_model = model // CORES
    front_send, front_keep = (
        lax.dot_general(
            normed_low[:, k * half_model : (k + 1) * half_model],
            grad_front_low,
            CONTRACT_ROWS,
            preferred_element_type=f32,
        ).astype(bf16)
        for k in (1, 0)
    )
    front_swapped = swap_core(front_send)
    out_parts = [
        part[u * rows_out : (u + 1) * rows_out] for part in out_came for u in range(span)
    ]

    def out_slice(s):
        target = (my_outer - s) % outer
        place = ((target // span) ^ my_chip) * span + target % span
        chosen = out_parts[0]
        for i in range(1, outer):
            chosen = jnp.where(place == i, out_parts[i], chosen)
        return chosen

    out_step = shift_outer(out_slice(1))
    for s in range(3, outer):
        moved[s] = spread(moving[s])
    state = (front_keep, front_swapped, out_step, moved, router_part)
    front_keep, front_swapped, out_step, moved, router_part = fence(state)
    front_half = (front_keep.astype(f32) + front_swapped.astype(f32)).astype(bf16)
    front_half = front_half.reshape(outer, chips * depth, columns)
    front_step = shift_outer(front_half[1])
    out_step = next_step(out_step, out_slice(2))
    piece_block = pl.BlockSpec((chips * depth, columns), lambda s, o: (0, 0))
    grad_normed = pl.pallas_call(
        functools.partial(project_back_kernel, outer),
        out_shape=shape((together, model), bf16),
        grid_spec=pltpu.PrefetchScalarGridSpec(
            num_scalar_prefetch=1,
            grid=(outer,),
            in_specs=[
                pl.BlockSpec((together, columns), lambda s, o: (0, 0)),
                *[piece_block] * (CORES * outer),
                pl.BlockSpec((plane * depth, plane * depth), lambda s, o: (0, 0)),
            ],
            out_specs=pl.BlockSpec(
                (together, plane * depth), lambda s, o: (0, lax.rem(o[0] + outer - s, outer))
            ),
        ),
        compiler_params=pltpu.CompilerParams(vmem_limit_bytes=32 * MEBIBYTE),
    )(
        outer_scalar,
        after(grad_front_low, front_half),
        *front_pieces,
        *front_others,
        front_order,
    )
    for s in range(3, outer):
        moved_own[s], partner = settle(picks[s], moved[s])
        moved_partner[s] = swap_core(partner)
    router_part = sum(
        [
            swap_chip(
                lax.dynamic_slice_in_dim(
                    router_part, (my_chip ^ r) * (CORES * depth), CORES * depth, 1
                ),
                r,
            )
            for r in range(chips)
        ]
    )
    state = (front_half, front_step, out_step, grad_normed, moved_own, moved_partner)
    state, router_part = fence((state, router_part))
    front_half, front_step, out_step, grad_normed, moved_own, moved_partner = state
    front_step = next_step(front_step, front_half[2])
    for s in range(3, outer):
        out_step = next_step(out_step, out_slice(s))
    arrived = [swap_chip(grad_normed[r * count : (r + 1) * count], r) for r in range(1, chips)]
    first_gain_term = call(gain_back_kernel, shape((1, model), f32))(grad_normed, *token_parts)
    gain_sums = jnp.concatenate(
        [first_gain_term.reshape(-1), second_gain_term.reshape(-1), gain_terms.reshape(-1)]
    ).reshape(-1, LANES)
    gain_sums = gain_sums + swap_core(gain_sums)
    router_grad = (
        lax.dynamic_slice_in_dim(router_part, my_core * depth, depth, 1)
        + swap_core(lax.dynamic_slice_in_dim(router_part, (1 - my_core) * depth, depth, 1))
    ).T
    state = (front_step, out_step, arrived, gain_sums, router_grad)
    front_step, out_step, arrived, gain_sums, router_grad = fence(state)
    for s in range(3, outer):
        front_step = next_step(front_step, front_half[s])
        moved_step = next_step(moved_step, moved_own[s], moved_partner[s])
    moved[0] = spread(moving[0])
    tokens_grad = call(tokens_back_kernel, shape((count, model), f32))(
        tokens, grad_normed[:count], *arrived, grad_hidden, first_gain_row
    )
    gain_sums = sum([swap_chip(gain_sums, r) for r in range(1, chips)], gain_sums)
    out_grad = out_step.astype(f32) + out_slice(0).astype(f32)
    state = (front_step, moved_step, moved, gain_sums, tokens_grad, out_grad)
    front_step, moved_step, moved, gain_sums, tokens_grad, out_grad = fence(state)
    moved_own[0], partner = settle(picks[0], moved[0])
    moved_partner[0] = swap_core(partner)
    output = hidden + moved_own[0] + moved_partner[0].astype(f32) + moved_step.astype(f32)
    output = output.astype(bf16)
    gain_sums = sum([shift_outer(gain_sums, s) for s in range(1, outer)], gain_sums).reshape(-1)
    front = (front_step.astype(f32) + front_half[0].astype(f32)).astype(bf16)
    front = front.reshape(chips, depth, columns)
    front = by_chip([swap_chip(front[r], r) for r in range(chips)])
    out_grad = out_step.astype(f32) + out_slice(0).astype(f32)

    def lay_out(first, last):
        return jnp.concatenate([part[:, first:last] for part in front], axis=1).astype(f32)

    query_grad = lay_out(0, group_columns)
    key_grad = lay_out(group_columns, group_columns + width)
    value_grad = lay_out(group_columns + width, columns)
    return (
        output,
        tokens_grad,
        query_grad,
        key_grad,
        value_grad,
        out_grad,
        router_grad,
        gate_grad[None],
        up_grad[None],
        down_grad[None],
        gain_sums[:model],
        gain_sums[model : 2 * model],
        gain_sums[2 * model : 2 * model + width],
        gain_sums[2 * model + width :],
    )


def solution(mesh):
    rows = P("fsdp", None)
    blocks = P("fsdp", None, None)
    placed = (rows,) * 9 + (blocks,) * 3 + (P(),) * 4
    return jax.shard_map(
        body,
        mesh=mesh,
        in_specs=placed,
        out_specs=(rows,) * 7 + (blocks,) * 3 + (P(),) * 4,
        check_vma=False,
    )
```

```python
import functools

import jax
import jax.numpy as jnp
from jax import lax
from jax.experimental import pallas as pl
from jax.experimental.pallas import tpu as pltpu
from jax.sharding import PartitionSpec as P

EPS = 1e-06
THETA = 1000000.0
NEGATIVE = -1e30
CORES = 2
LANES = 128
MEBIBYTE = 1024 * 1024
FLOPS_A_MICRO = 1_000_000_000
BYTES_A_MICRO = 2_000_000
CONTRACT_ROWS = (((0,), (0,)), ((), ()))
CONTRACT_LAST = (((1,), (1,)), ((), ()))


def root_mean_square_norm(value_rows, gain):
    return (
        value_rows
        * lax.rsqrt(jnp.mean(value_rows * value_rows, axis=-1, keepdims=True) + EPS)
        * gain
    )


def sequence_layout(lengths, count_total):
    ends = jnp.cumsum(lengths)
    starts = ends - lengths
    places = jnp.arange(count_total, dtype=jnp.int32)
    member = ((places[:, None] >= starts[None, :]) & (places[:, None] < ends[None, :])).astype(
        jnp.int32
    )
    labels = jnp.arange(lengths.shape[0], dtype=jnp.int32)
    segment = jnp.sum(member * labels[None, :], axis=1)
    offset = jnp.sum(member * starts[None, :], axis=1)
    return (segment, places - offset)


def rotary_tables(position, width):
    half = width // 2
    inverse = jnp.power(THETA, -(jnp.arange(half, dtype=jnp.float32) * 2.0) / width)
    angle = position.astype(jnp.float32)[:, None] * inverse[None, :]
    angle = jnp.concatenate([angle, angle], axis=1)
    return (jnp.cos(angle), jnp.sin(angle))


def call(kernel, outs, mebibytes=32, micros=0, **specs):
    if micros:
        specs["cost_estimate"] = pl.CostEstimate(
            flops=micros * FLOPS_A_MICRO, bytes_accessed=micros * BYTES_A_MICRO, transcendentals=0
        )
    return pl.pallas_call(
        kernel,
        out_shape=outs,
        compiler_params=pltpu.CompilerParams(vmem_limit_bytes=mebibytes * MEBIBYTE),
        **specs,
    )


def turned_sine(sine_table):
    half = sine_table.shape[1] // 2
    return jnp.concatenate([-sine_table[:, :half], sine_table[:, half:]], axis=1)


def head_rotated(value, gain, cosine, sine):
    normal = (
        value * lax.rsqrt(jnp.mean(value * value, axis=-1, keepdims=True) + EPS) * gain
    )
    return normal * cosine + pltpu.roll(normal, value.shape[1] // 2, 1) * sine


def head_shares(query, key, allowed, scale):
    scores = lax.dot_general(query, key, CONTRACT_LAST, preferred_element_type=jnp.float32)
    scores = jnp.where(allowed, scores * scale, NEGATIVE)
    exponent = jnp.exp(scores - jnp.max(scores, axis=-1, keepdims=True))
    return exponent / jnp.sum(exponent, axis=-1, keepdims=True)


def norm_kernel(outer, my_outer, *refs):
    *parts, gain, order, out, normed = refs
    count = parts[0].shape[0]
    span = order.shape[0]
    half = span // CORES
    for b, part in enumerate(parts):
        normed[b * count : (b + 1) * count, :] = root_mean_square_norm(
            part[...].astype(jnp.float32), gain[...]
        ).astype(jnp.bfloat16)
    for s in range(outer):
        start = lax.rem(my_outer[0] + (outer - s), outer) * span
        block = normed[:, pl.ds(pl.multiple_of(start, LANES), span)]
        block = jnp.dot(block, order[...], preferred_element_type=jnp.float32)
        block = block.astype(jnp.bfloat16)
        for k in range(CORES):
            first = (k * outer + s) * half
            out[:, first : first + half] = block[:, k * half : (k + 1) * half]


def project_kernel(normed, *refs):
    *pieces, out = refs
    rows = pieces[0].shape[0]
    total = jnp.zeros(out.shape, jnp.float32)
    for i, piece in enumerate(pieces):
        total += jnp.dot(
            normed[:, i * rows : (i + 1) * rows], piece[...], preferred_element_type=jnp.float32
        )
    out[...] = total


def add_kernel(first, second, *outs):
    rows = outs[0].shape[0]
    for i, out in enumerate(outs):
        part = slice(i * rows, (i + 1) * rows)
        total = first[part, :].astype(jnp.float32) + second[part, :].astype(jnp.float32)
        out[...] = total.astype(out.dtype)


def choose_kernel(places, *refs):
    half = len(refs) // 2
    parts, outs = refs[:half], refs[half:]
    for i, out in enumerate(outs):
        for j, part in enumerate(parts):

            @pl.when(places[i] == j)
            def _(part=part, out=out):
                out[...] = part[...]


def project_back_kernel(outer, chips, my_outer, grad, *refs):
    *pieces, order = refs[:-chips]
    outs = refs[-chips:]
    f32, bf16 = jnp.float32, jnp.bfloat16
    count = outs[0].shape[0]
    for s in range(outer):

        @pl.when(pl.program_id(0) == s)
        def _(s=s):
            block = jnp.concatenate(
                [
                    lax.dot_general(
                        grad[...], part[...], CONTRACT_LAST, preferred_element_type=f32
                    )
                    for part in pieces[s::outer]
                ],
                axis=1,
            ).astype(bf16)
            block = lax.dot_general(
                block, order[...], CONTRACT_LAST, preferred_element_type=f32
            ).astype(bf16)
            for r, out in enumerate(outs):
                out[...] = block[r * count : (r + 1) * count, :]


def router_order_kernel(outer, experts, my_outer, *refs):
    *pieces, order, out = refs
    span = order.shape[0]
    column = lax.broadcasted_iota(jnp.int32, (span, out.shape[1]), 1)
    for s in range(outer):
        block = jnp.concatenate([part[...] for part in pieces[s::outer]], axis=0)
        block = jnp.dot(order[...], block, preferred_element_type=jnp.float32)
        start = pl.multiple_of(lax.rem(my_outer[0] + (outer - s), outer) * span, LANES)
        out[pl.ds(start, span), :] = jnp.where(column < experts, block, 0.0).astype(jnp.bfloat16)


def gain_back_kernel(*refs):
    *parts, gain_grad = refs
    half = len(parts) // 2
    total = jnp.zeros(gain_grad.shape, jnp.float32)
    for grad, part in zip(parts[:half], parts[half:]):
        value = part[...].astype(jnp.float32)
        root = lax.rsqrt(jnp.mean(value * value, axis=-1, keepdims=True) + EPS)
        total += jnp.sum(grad[...].astype(jnp.float32) * value * root, axis=0, keepdims=True)
    gain_grad[...] = total


def tokens_back_kernel(tokens, own, *refs):
    *others, hidden_grad, gain, tokens_grad = refs
    f32 = jnp.float32
    grad = own[...].astype(f32)
    for other in others:
        grad = grad + other[...].astype(f32)
    value = tokens[...].astype(f32)
    root = lax.rsqrt(jnp.mean(value * value, axis=-1, keepdims=True) + EPS)
    normal = value * root
    grad = grad * gain[...]
    tokens_grad[...] = hidden_grad[...] + root * (
        grad - normal * jnp.mean(normal * grad, axis=-1, keepdims=True)
    )


def attend_kernel(scale, front, cosine, sine, allowed, query_gain, key_gain, order, *outs):
    query_out, key_out, value_out, context_out, context = outs
    width = cosine.shape[1]
    heads = query_out.shape[1] // width
    bf16 = jnp.bfloat16
    cos, sin = cosine[...], sine[...]
    open_places = allowed[...] > 0.0
    key = head_rotated(
        front[:, heads * width : (heads + 1) * width], key_gain[...], cos, sin
    ).astype(bf16)
    value = front[:, (heads + 1) * width :].astype(bf16)
    key_out[...] = key
    value_out[...] = value
    for h in range(heads):
        part = slice(h * width, (h + 1) * width)
        query = head_rotated(front[:, part], query_gain[...], cos, sin).astype(bf16)
        query_out[:, part] = query
        shares = head_shares(query, key, open_places, scale).astype(bf16)
        context[:, part] = jnp.dot(
            shares, value, preferred_element_type=jnp.float32
        ).astype(bf16)
    context_out[...] = jnp.dot(
        context[...], order[...], preferred_element_type=jnp.float32
    ).astype(bf16)


def head_back(grad, value, gain, cosine, sine):
    grad = grad * cosine + pltpu.roll(grad * sine, value.shape[1] // 2, 1)
    root = lax.rsqrt(jnp.mean(value * value, axis=-1, keepdims=True) + EPS)
    normal = value * root
    gain_grad = jnp.sum(grad * normal, axis=0, keepdims=True)
    grad = grad * gain
    grad = root * (grad - normal * jnp.mean(normal * grad, axis=-1, keepdims=True))
    return grad, gain_grad


def attend_back_kernel(
    scale, front, query_in, key_in, value_in, grad_own, grad_other, cosine, sine, allowed, *rest
):
    query_gain, key_gain, order, front_grad, gain_grads, context_grad = rest
    half = grad_own.shape[1]
    context_grad[...] = (
        lax.dot_general(
            grad_own[...], order[:, :half], CONTRACT_LAST, preferred_element_type=jnp.float32
        )
        + lax.dot_general(
            grad_other[...], order[:, half:], CONTRACT_LAST, preferred_element_type=jnp.float32
        )
    ).astype(jnp.bfloat16)
    width = cosine.shape[1]
    heads = query_in.shape[1] // width
    f32, bf16 = jnp.float32, jnp.bfloat16
    cos, sin = cosine[...], sine[...]
    open_places = allowed[...] > 0.0
    key, value = key_in[...], value_in[...]
    key_total = jnp.zeros(key.shape, f32)
    value_total = jnp.zeros(key.shape, f32)
    gain_total = jnp.zeros((1, width), f32)
    for h in range(heads):
        part = slice(h * width, (h + 1) * width)
        query, grad = query_in[:, part], context_grad[:, part]
        shares = head_shares(query, key, open_places, scale)
        grad_shares = lax.dot_general(grad, value, CONTRACT_LAST, preferred_element_type=f32)
        grad_scores = (
            shares * (grad_shares - jnp.sum(shares * grad_shares, axis=-1, keepdims=True))
        ).astype(bf16)
        value_total += lax.dot_general(
            shares.astype(bf16), grad, CONTRACT_ROWS, preferred_element_type=f32
        )
        key_total += lax.dot_general(
            grad_scores, query, CONTRACT_ROWS, preferred_element_type=f32
        )
        grad_query = jnp.dot(grad_scores, key, preferred_element_type=f32) * scale
        grad_query, gain_grad = head_back(grad_query, front[:, part], query_gain[...], cos, sin)
        front_grad[:, part] = grad_query.astype(bf16)
        gain_total += gain_grad
    part = slice(heads * width, (heads + 1) * width)
    grad_key, key_gain_grad = head_back(
        key_total * scale, front[:, part], key_gain[...], cos, sin
    )
    front_grad[:, part] = grad_key.astype(bf16)
    front_grad[:, (heads + 1) * width :] = value_total.astype(bf16)

    @pl.when(pl.program_id(0) == 0)
    def _():
        gain_grads[...] = jnp.zeros(gain_grads.shape, f32)

    gain_grads[0:1, :] += gain_total
    gain_grads[1:2, :] += key_gain_grad


def router_kernel(experts, *refs):
    tokens, own, *others, gain, router, mask, hidden_out, wide_out, prob_out, gates_out = refs
    f32, bf16 = jnp.float32, jnp.bfloat16
    model = tokens.shape[1]
    lanes = mask.shape[1]
    hidden = tokens[...].astype(f32) + own[...]
    for other in others:
        hidden = hidden + other[...].astype(f32)
    hidden_out[...] = hidden
    second = root_mean_square_norm(hidden, gain[...]).astype(bf16)
    wide_out[:, :model] = second
    logits = jnp.dot(second, router[...], preferred_element_type=f32)
    column = lax.broadcasted_iota(jnp.int32, logits.shape, 1)
    logits = jnp.where(column < experts, logits, NEGATIVE)
    exponent = jnp.exp(logits - jnp.max(logits, axis=-1, keepdims=True))
    prob = exponent / jnp.sum(exponent, axis=-1, keepdims=True)
    chosen = prob * mask[...]
    gates = chosen / jnp.sum(chosen, axis=-1, keepdims=True)
    prob_out[...] = prob
    gates_out[...] = gates
    high = gates.astype(bf16).astype(f32)
    low = gates - high
    if 2 * experts <= lanes:
        wide_out[:, model:] = (high + pltpu.roll(low, experts, 1)).astype(bf16)
    else:
        wide_out[:, model : model + lanes] = high.astype(bf16)
        wide_out[:, model + lanes :] = low.astype(bf16)


def router_back_kernel(experts, *refs):
    own, near, came, cotangent, hidden, gain, router, mask, prob, gates, *outs = refs
    hidden_grad, attn_grad, logits_grad, gain_grad = outs
    f32, bf16 = jnp.float32, jnp.bfloat16
    model = cotangent.shape[1]
    lanes = mask.shape[1]
    pairs = own[:, model:] + near[:, model:].astype(f32) + came[:, model:].astype(f32)
    if 2 * experts <= lanes:
        grad_gates = pairs + pltpu.roll(pairs, lanes - experts, 1)
    else:
        grad_gates = pairs[:, :lanes] + pairs[:, lanes:]
    chosen_sum = jnp.sum(prob[...] * mask[...], axis=-1, keepdims=True)
    grad_gates = jnp.where(mask[...] > 0.0, grad_gates, 0.0)
    grad_chosen = (
        mask[...]
        * (grad_gates - jnp.sum(gates[...] * grad_gates, axis=-1, keepdims=True))
        / chosen_sum
    )
    grad_logits = (
        prob[...] * (grad_chosen - jnp.sum(prob[...] * grad_chosen, axis=-1, keepdims=True))
    ).astype(bf16)
    logits_grad[...] = grad_logits
    grad = (
        own[:, :model]
        + near[:, :model].astype(f32)
        + came[:, :model].astype(f32)
        + lax.dot_general(grad_logits, router[...], CONTRACT_LAST, preferred_element_type=f32)
    )
    value = hidden[...]
    root = lax.rsqrt(jnp.mean(value * value, axis=-1, keepdims=True) + EPS)
    normal = value * root
    gain_grad[...] = jnp.sum(grad * normal, axis=0, keepdims=True)
    grad = grad * gain[...]
    grad = cotangent[...].astype(f32) + root * (
        grad - normal * jnp.mean(normal * grad, axis=-1, keepdims=True)
    )
    hidden_grad[...] = grad
    attn_grad[...] = grad.astype(bf16)


def pick_kernel(capacity, own, partner, near, earlier, *outs):
    *parts, picks = outs
    f32, bf16 = jnp.float32, jnp.bfloat16
    rows, model = parts[0].shape
    count = own.shape[0]
    masks = [
        lax.dot_general(near[...], side[:, model:], CONTRACT_LAST, preferred_element_type=f32)
        for side in (own, partner)
    ]
    ranks = [jnp.dot(m.astype(bf16), earlier[...], preferred_element_type=f32) for m in masks]
    mask = jnp.concatenate(masks, axis=1)
    rank = jnp.concatenate([ranks[0], ranks[1] + capacity], axis=1)
    place = lax.broadcasted_iota(jnp.int32, (rows, CORES * count), 0).astype(f32)
    for r in range(len(parts)):
        hit = (place == rank[r : r + 1, :]) & (mask[r : r + 1, :] > 0.5)
        picks[r * rows : (r + 1) * rows, :] = jnp.where(hit, 1.0, 0.0).astype(bf16)
    both = jnp.concatenate([own[:, :model], partner[:, :model]], axis=0)
    chosen = jnp.dot(picks[...], both, preferred_element_type=f32).astype(bf16)
    for r, part in enumerate(parts):
        part[...] = chosen[r * rows : (r + 1) * rows, :]


def send_kernel(picks, own, partner, *parts):
    rows = parts[0].shape[0]
    both = jnp.concatenate([own[...], partner[...]], axis=0)
    chosen = jnp.dot(picks[...], both, preferred_element_type=jnp.float32).astype(jnp.bfloat16)
    for r, part in enumerate(parts):
        part[...] = chosen[r * rows : (r + 1) * rows, :]


def settle_kernel(picks, *refs):
    *parts, own, partner = refs
    count = own.shape[0]
    rows = jnp.concatenate([part[...] for part in parts], axis=0)
    total = lax.dot_general(
        picks[...], rows, CONTRACT_ROWS, preferred_element_type=jnp.float32
    )
    own[...] = total[:count, :]
    partner[...] = total[count:, :].astype(jnp.bfloat16)


def move_kernel(units, weight, *parts):
    rows = parts[0].shape[0]
    moved = jnp.dot(units[...], weight[...], preferred_element_type=jnp.float32)
    for r, part in enumerate(parts):
        part[...] = moved[r * rows : (r + 1) * rows, :].astype(jnp.bfloat16)


def expert_kernel(chips, experts, me, *refs):
    f32, bf16 = jnp.float32, jnp.bfloat16
    came, given = refs[:chips], refs[chips : 2 * chips]
    gate_weight, up_weight, down_weight = refs[2 * chips : 2 * chips + 3]
    back = refs[2 * chips + 3 : 3 * chips + 3]
    units_out, gate_out, up_out, rows, grads, row_gate, change, total = refs[3 * chips + 3 :]
    size, model = came[0].shape[0], rows.shape[1]
    step = pl.program_id(0)
    column = lax.broadcasted_iota(jnp.int32, (size, came[0].shape[1] - model), 1)
    high_column, low_column = column == me[0], column == me[0] + experts

    @pl.when(step == 0)
    def _():
        for r in range(chips):
            part = slice(r * size, (r + 1) * size)
            rows[part, :] = came[r][:, :model]
            grads[part, :] = given[r][...]
            side = jnp.where(high_column | low_column, came[r][:, model:].astype(f32), 0.0)
            row_gate[part, :] = jnp.sum(side, axis=1, keepdims=True)
        change[...] = jnp.zeros(change.shape, f32)
        total[...] = jnp.zeros(total.shape, f32)

    gate_part = jnp.dot(rows[...], gate_weight[...], preferred_element_type=f32)
    up_part = jnp.dot(rows[...], up_weight[...], preferred_element_type=f32)
    raw = lax.dot_general(
        grads[...], down_weight[...], CONTRACT_LAST, preferred_element_type=f32
    )
    sig = 1.0 / (1.0 + jnp.exp(-gate_part))
    silu = gate_part * sig
    units = silu * up_part
    change[...] += jnp.sum(units * raw, axis=1, keepdims=True)
    units_out[...] = (row_gate[...] * units).astype(bf16)
    grad_units = row_gate[...] * raw
    gate_grad = (grad_units * up_part * sig * (1.0 + gate_part * (1.0 - sig))).astype(bf16)
    up_grad = (grad_units * silu).astype(bf16)
    gate_out[...] = gate_grad
    up_out[...] = up_grad
    total[...] += lax.dot_general(
        gate_grad, gate_weight[...], CONTRACT_LAST, preferred_element_type=f32
    ) + lax.dot_general(up_grad, up_weight[...], CONTRACT_LAST, preferred_element_type=f32)

    @pl.when(step == pl.num_programs(0) - 1)
    def _():
        for r in range(chips):
            part = slice(r * size, (r + 1) * size)
            back[r][:, :model] = total[part, :].astype(bf16)
            high = change[part, :].astype(bf16).astype(f32)
            low = change[part, :] - high
            back[r][:, model:] = (
                jnp.where(high_column, high, 0.0) + jnp.where(low_column, low, 0.0)
            ).astype(bf16)


def expert_grad_kernel(outer, chips, *refs):
    f32 = jnp.float32
    parts = outer * chips
    rows, grads = refs[:parts], refs[parts : 2 * parts]
    units, gates, ups = (
        refs[2 * parts + i * outer : 2 * parts + (i + 1) * outer] for i in range(3)
    )
    gate_out, up_out, down_out, left, right, all_units, all_gates, all_ups = refs[
        2 * parts + 3 * outer :
    ]
    size = rows[0].shape[0]
    for i in range(parts):
        part = slice(i * size, (i + 1) * size)
        left[part, :] = rows[i][...]
        right[part, :] = grads[i][...]
    size = units[0].shape[0]

    @pl.when(pl.program_id(0) == 0)
    def _():
        for s in range(outer):
            part = slice(s * size, (s + 1) * size)
            all_units[part, :] = units[s][...]
            all_gates[part, :] = gates[s][...]
            all_ups[part, :] = ups[s][...]

    def product(a, b):
        return lax.dot_general(a[...], b[...], CONTRACT_ROWS, preferred_element_type=f32)

    gate_out[...] = product(left, all_gates)
    up_out[...] = product(left, all_ups)
    down_out[...] = product(all_units, right)


def round_up(number, step):
    return -(-number // step) * step


def after(value, *others):
    return lax.optimization_barrier((value, *others))[0]


def body(
    tokens,
    cotangent,
    lengths,
    routes,
    query_weight,
    key_matrix,
    value_matrix,
    out_weight,
    router_weight,
    expert_gate,
    expert_up,
    expert_down,
    first_gain,
    second_gain,
    query_norm_gain,
    key_gain,
):
    f32, bf16, i32 = jnp.float32, jnp.bfloat16, jnp.int32
    shape = jax.ShapeDtypeStruct
    fence = lax.optimization_barrier
    count, model = tokens.shape
    width = query_norm_gain.shape[0]
    heads = query_weight.shape[1] // width
    kv_heads = key_matrix.shape[1] // width
    head_group = heads // kv_heads
    choose = routes.shape[1]
    shards = lax.axis_size("fsdp")
    experts = shards * expert_gate.shape[0]
    capacity = max(2, count * choose * 5 // (4 * experts))
    scale = width ** (-0.5)

    chips = kv_heads
    plane = chips * CORES
    outer = shards // plane
    span = outer // chips
    me = lax.axis_index("fsdp")
    my_core = me % CORES
    my_chip = (me // CORES) % chips
    my_outer = me // plane
    me_scalar = me.reshape(1)
    outer_scalar = my_outer.reshape(1)
    smem = pl.BlockSpec(memory_space=pltpu.SMEM)
    vmem = pl.BlockSpec(memory_space=pltpu.VMEM)

    def swap_core(value):
        return lax.ppermute(value, "fsdp", [(i, i ^ 1) for i in range(shards)])

    def swap_chip(value, r):
        if r == 0:
            return value
        return lax.ppermute(value, "fsdp", [(i, i ^ (r * CORES)) for i in range(shards)])

    def shift_outer(value, s=1):
        if s == 0:
            return value
        return lax.ppermute(
            value,
            "fsdp",
            [(i, ((i // plane + s) % outer) * plane + i % plane) for i in range(shards)],
        )

    def gather_chips(value):
        return [swap_chip(value, r) for r in range(chips)]

    def spread(parts):
        return [swap_chip(part, r) for r, part in enumerate(parts)]

    def scatter_outer(take):
        total = take(my_outer)
        for s in range(1, outer):
            total = total + shift_outer(take((my_outer + s) % outer), s)
        return total

    def by_chip(parts):
        parts = jnp.stack(parts)
        return [
            lax.dynamic_index_in_dim(parts, my_chip ^ m, 0, keepdims=False) for m in range(chips)
        ]

    depth = query_weight.shape[0]
    group_columns = head_group * width
    half_columns = group_columns // CORES
    columns = group_columns + 2 * width
    rows_out = out_weight.shape[0]

    lanes = round_up(experts, LANES)
    pair_width = round_up(2 * experts, LANES)
    part_rows = round_up(CORES * capacity, 16)
    slots = chips * part_rows

    def dispatch_first(piece, partner):
        *parts, picks = call(
            functools.partial(pick_kernel, capacity),
            [shape((part_rows, model), bf16)] * chips + [shape((slots, CORES * count), bf16)],
            mebibytes=16,
        )(piece, partner, near, earlier)
        return parts, picks

    def dispatch(picks, piece, partner):
        outs = [shape((part_rows, piece.shape[1]), bf16)] * chips
        return call(send_kernel, outs, mebibytes=16)(picks, piece, partner)

    def settle(picks, parts):
        columns_of = parts[0].shape[1]
        return call(
            settle_kernel,
            (shape((count, columns_of), f32), shape((count, columns_of), bf16)),
            mebibytes=16,
        )(picks, *parts)

    together = chips * count
    first_gain_row, second_gain_row = first_gain[None, :], second_gain[None, :]
    query_gain_row, key_gain_row = query_norm_gain[None, :], key_gain[None, :]

    def norm(token_parts):
        return call(
            functools.partial(norm_kernel, outer),
            shape((together, model), bf16),
            in_specs=[smem] + [vmem] * (chips + 2),
            scratch_shapes=[pltpu.VMEM((together, model), bf16)],
        )(outer_scalar, *token_parts, first_gain_row, front_order)

    def positions(length_parts):
        layouts = [sequence_layout(part[0], count) for part in length_parts]
        segment = jnp.stack([layout[0] for layout in layouts])
        position = jnp.concatenate([layout[1] for layout in layouts])
        cosine_table, sine_table = rotary_tables(position, width)
        sine_table = turned_sine(sine_table)
        places = jnp.arange(count, dtype=i32)
        allowed = (segment[:, :, None] == segment[:, None, :]) & (
            places[None, None, :] <= places[None, :, None]
        )
        return cosine_table, sine_table, allowed.astype(f32).reshape(together, count)

    sequences = lengths.shape[1]
    side_width = round_up(experts + sequences, LANES)
    side = jnp.pad(router_weight, ((0, 0), (0, side_width - experts))) + jnp.pad(
        lengths.astype(bf16), ((0, depth - 1), (experts, side_width - experts - sequences))
    )
    cut = []
    for r in range(chips):
        target = my_chip ^ r
        part = [
            lax.dynamic_slice_in_dim(query_weight, target * group_columns, group_columns, 1),
            lax.dynamic_slice_in_dim(key_matrix, target * width, width, 1),
            lax.dynamic_slice_in_dim(value_matrix, target * width, width, 1),
            side,
        ]
        cut.append(swap_chip(jnp.concatenate(part, axis=1), r))
    out_pieces = [out_weight, shift_outer(out_weight)]
    front_pieces, front_others = [], []
    state = fence((cut, out_pieces, routes, tokens, cotangent))
    cut, out_pieces, routes, tokens, cotangent = state
    length_parts = [
        part[:1, columns + experts : columns + experts + sequences].astype(i32) for part in cut
    ]
    cut = jnp.concatenate(cut, axis=0)
    me = after(me, cut)
    my_core, my_chip, my_outer = me % CORES, (me // CORES) % chips, me // plane

    def arrival_order(length, block, inner):
        place = jnp.arange(length, dtype=i32)
        went_to = (
            (
                ((place // block % CORES) ^ my_core) * chips
                + ((place // (block * CORES) % chips) ^ my_chip)
            )
            * inner
            + place // (block * plane)
        ) * block + place % block
        return (went_to[:, None] == place[None, :]).astype(bf16)

    front_order = arrival_order(plane * depth, depth, 1)
    out_order = arrival_order(group_columns, rows_out, span)

    mask = jnp.sum(
        (routes[:, :, None] == jnp.arange(lanes, dtype=i32)[None, None, :]).astype(f32), axis=1
    )
    near = jnp.arange(2 * chips, dtype=i32)
    near = jnp.where(
        near < chips, my_outer * plane + (my_chip ^ near) * CORES + my_core, -1
    )
    near = (near[:, None] == jnp.arange(lanes, dtype=i32)[None, :]).astype(bf16)
    earlier = jnp.triu(jnp.ones((count, count), bf16), 1)
    cotangent_wide = jnp.concatenate([cotangent, mask.astype(bf16)], axis=1)
    cotangent_pieces, cotangent_parts, picks = [cotangent_wide], [], []
    cotangent_partners = []

    def send_cotangent(s):
        parts, pick = dispatch_first(cotangent_pieces[s], cotangent_partners[s])
        cotangent_parts.append(spread(parts))
        picks.append(pick)

    front_pieces.append(cut)
    for t in range(2, outer + 1):
        front_pieces.append(shift_outer(front_pieces[-1]))
        if t < outer:
            out_pieces.append(shift_outer(out_pieces[-1]))
        front_others.append(swap_core(front_pieces[-2]))
        if t == 2:
            token_parts = [swap_chip(tokens, r) for r in range(chips - 1)]
            cotangent_partners.append(swap_core(cotangent_pieces[0]))
            state = (token_parts, cotangent_partners, positions(length_parts))
            state = fence((state, front_pieces, front_others, out_pieces))
            (token_parts, cotangent_partners, tables), *state = state
            cosine_table, sine_table, allowed = tables
        elif t == 3:
            token_parts.append(swap_chip(tokens, chips - 1))
            send_cotangent(0)
            state = (cotangent_parts, picks, token_parts)
            state = fence((state, front_pieces, front_others, out_pieces))
            (cotangent_parts, picks, token_parts), *state = state
        elif t < outer:
            state = fence((front_pieces, front_others, out_pieces))
        else:
            cotangent_pieces.append(shift_outer(cotangent_pieces[0]))
            normed_low = norm(token_parts)
            stacked = jnp.stack(out_pieces)
            out_own = []
            for r in range(chips):
                part = [
                    lax.dynamic_index_in_dim(
                        stacked,
                        (my_outer + outer - ((my_chip ^ r) * span + u)) % outer,
                        0,
                        keepdims=False,
                    )
                    for u in range(span)
                ]
                out_own.append(swap_chip(jnp.concatenate(part, axis=0), r))
            state = fence((front_pieces, front_others, out_pieces))
        front_pieces, front_others, out_pieces = state
    cotangent_pieces, out_own, normed_low = fence((cotangent_pieces, out_own, normed_low))

    front_others.append(swap_core(front_pieces[-1]))
    cotangent_partners.append(swap_core(cotangent_pieces[1]))
    out_own = jnp.concatenate(out_own, axis=0)
    front_others, cotangent_partners, out_own = fence((front_others, cotangent_partners, out_own))
    out_other = swap_core(out_own)
    for s in range(2, outer - 1):
        cotangent_pieces.append(shift_outer(cotangent_pieces[-1]))
    tile = 2 * width
    projected = call(
        project_kernel,
        shape((together, columns), f32),
        grid=(columns // tile,),
        in_specs=[pl.BlockSpec((together, model), lambda n: (0, 0))]
        + [pl.BlockSpec((chips * depth, tile), lambda n: (0, n))] * (CORES * outer),
        out_specs=pl.BlockSpec((together, tile), lambda n: (0, n)),
    )(normed_low, *front_pieces, *front_others)

    cotangent_pieces[1] = after(cotangent_pieces[1], projected)
    send_cotangent(1)

    def blocks(columns_of):
        return pl.BlockSpec((count, columns_of), lambda b: (b, 0))

    once = pl.BlockSpec((1, width), lambda b: (0, 0))
    order_once = pl.BlockSpec((group_columns, group_columns), lambda b: (0, 0))
    query_low, key_low, value_low, context_low = call(
        functools.partial(attend_kernel, scale),
        (
            shape((together, group_columns), bf16),
            shape((together, width), bf16),
            shape((together, width), bf16),
            shape((together, group_columns), bf16),
        ),
        grid=(chips,),
        in_specs=[
            blocks(columns),
            blocks(width),
            blocks(width),
            blocks(count),
            once,
            once,
            order_once,
        ],
        out_specs=[blocks(group_columns), blocks(width), blocks(width), blocks(group_columns)],
        scratch_shapes=[pltpu.VMEM((count, group_columns), bf16)],
    )(projected, cosine_table, sine_table, allowed, query_gain_row, key_gain_row, out_order)
    state = (context_low, out_other, cotangent_pieces, cotangent_parts, picks)
    state = fence((state, query_low, key_low, value_low, projected))
    (context_low, out_other, cotangent_pieces, cotangent_parts, picks), *state = state
    query_low, key_low, value_low, projected = state
    context_own, context_other = context_low[:, :half_columns], context_low[:, half_columns:]

    def attended(first, last):
        return jnp.dot(
            context_own[first:last], out_own, preferred_element_type=f32
        ) + jnp.dot(context_other[first:last], out_other, preferred_element_type=f32)

    away = attended(count, together).astype(bf16)
    arrived = [swap_chip(away[(r - 1) * count : r * count], r) for r in range(1, chips)]
    home = attended(0, count)
    cotangent_pieces.append(shift_outer(cotangent_pieces[-1]))
    cotangent_partners.append(swap_core(cotangent_pieces[2]))
    router_block = pl.BlockSpec((chips * depth, lanes), lambda n: (0, columns // lanes))
    order_block = pl.BlockSpec((plane * depth, plane * depth), lambda n: (0, 0))
    router_wide = call(
        functools.partial(router_order_kernel, outer, experts),
        shape((model, lanes), bf16),
        grid=(1,),
        in_specs=[smem, *[router_block] * (CORES * outer), order_block],
        out_specs=pl.BlockSpec((model, lanes), lambda n: (0, 0)),
    )(outer_scalar, *front_pieces, *front_others, after(front_order, away))
    arrived, home, cotangent_pieces, cotangent_partners, router_wide = fence(
        (arrived, home, cotangent_pieces, cotangent_partners, router_wide)
    )
    hidden, second_wide, prob, gates = call(
        functools.partial(router_kernel, experts),
        (
            shape((count, model), f32),
            shape((count, model + pair_width), bf16),
            shape((count, lanes), f32),
            shape((count, lanes), f32),
        ),
    )(tokens, home, *arrived, second_gain_row, router_wide, mask)

    gate_weight, up_weight, down_weight = expert_gate[0], expert_up[0], expert_down[0]
    hidden_units = gate_weight.shape[1]
    unit_tile = 2 * LANES

    def expert(came, given):
        part = pl.BlockSpec((part_rows, model + pair_width), lambda f: (0, 0))
        units = pl.BlockSpec((slots, unit_tile), lambda f: (0, f))
        outs = call(
            functools.partial(expert_kernel, chips, experts),
            [shape((part_rows, model + pair_width), bf16)] * chips
            + [shape((slots, hidden_units), bf16)] * 3,
            micros=11,
            grid=(hidden_units // unit_tile,),
            in_specs=[smem]
            + [part] * chips
            + [pl.BlockSpec((part_rows, model), lambda f: (0, 0))] * chips
            + [pl.BlockSpec((model, unit_tile), lambda f: (0, f))] * 2
            + [pl.BlockSpec((unit_tile, model), lambda f: (f, 0))],
            out_specs=[part] * chips + [units] * 3,
            scratch_shapes=[
                pltpu.VMEM((slots, model), bf16),
                pltpu.VMEM((slots, model), bf16),
                pltpu.VMEM((slots, 1), f32),
                pltpu.VMEM((slots, 1), f32),
                pltpu.VMEM((slots, model), f32),
            ],
        )(me_scalar, *came, *given, gate_weight, up_weight, down_weight)
        return outs[:chips], (came, given, *outs[chips:])

    def move(s):
        return call(move_kernel, [shape((part_rows, model), bf16)] * chips, mebibytes=16)(
            kept[s][2], down_weight
        )

    second_pieces, second_partners = [second_wide], []
    came, backs, kept, returned, settled_own, settled_partner = {}, {}, {}, {}, {}, {}
    moved, moving, moved_own, moved_partner = {}, [], {}, {}
    grad_step = None
    for t in range(outer + 5):
        if 0 <= t - 1 < outer:
            sent = dispatch(picks[t - 1], second_pieces[t - 1], second_partners[t - 1])
            came[t - 1] = spread(sent)
        if 2 <= t + 2 < outer:
            send_cotangent(t + 2)
        if t + 3 < outer:
            cotangent_partners.append(swap_core(cotangent_pieces[t + 3]))
        if t + 1 < outer:
            second_pieces.append(shift_outer(second_pieces[t]))
        if t < outer:
            second_partners.append(swap_core(second_pieces[t]))
        if t - 5 >= 1:
            total = settled_own[t - 5] + settled_partner[t - 5].astype(f32)
            if grad_step is not None:
                total = total + grad_step.astype(f32)
            grad_step = shift_outer(total.astype(bf16))
        if 0 <= t - 4 < outer:
            settled_own[t - 4], partner = settle(picks[t - 4], returned[t - 4])
            settled_partner[t - 4] = swap_core(partner)
        if 0 <= t - 3 < outer:
            returned[t - 3] = spread(backs[t - 3])
        if t == outer + 2:
            moving = [move(i) for i in range(outer)]
        if t >= outer + 3:
            moved[t - outer - 2] = spread(moving[t - outer - 2])
        if t == outer + 4:
            moved_own[1], partner = settle(picks[1], moved[1])
            moved_partner[1] = swap_core(partner)
        if 0 <= t - 2 < outer:
            backs[t - 2], kept[t - 2] = expert(came[t - 2], cotangent_parts[t - 2])
        state = (second_pieces, second_partners, cotangent_partners, cotangent_parts, picks)
        state = (state, came, backs, returned, settled_own, settled_partner)
        state = fence((state, moved, moving, moved_own, moved_partner, grad_step, kept))
        state, moved, moving, moved_own, moved_partner, grad_step, kept = state
        state, came, backs, returned, settled_own, settled_partner = state
        second_pieces, second_partners, cotangent_partners, cotangent_parts, picks = state

    grad_hidden, grad_hidden_low, grad_logits_low, second_gain_term = call(
        functools.partial(router_back_kernel, experts),
        (
            shape((count, model), f32),
            shape((count, model), bf16),
            shape((count, lanes), bf16),
            shape((1, model), f32),
        ),
        mebibytes=60,
    )(
        settled_own[0],
        settled_partner[0],
        grad_step,
        cotangent,
        hidden,
        second_gain_row,
        router_wide,
        mask,
        prob,
        gates,
    )
    grad_attn_low = jnp.concatenate(gather_chips(grad_hidden_low), axis=0)
    moved_step = shift_outer((moved_own[1] + moved_partner[1].astype(f32)).astype(bf16))
    kept_late = [fence((kept[s], grad_hidden_low))[0] for s in range(outer)]
    total_slots = outer * slots
    row_tile = pl.BlockSpec((part_rows, unit_tile), lambda i: (0, i))
    unit_once = pl.BlockSpec((slots, hidden_units), lambda i: (0, 0))
    gate_grad, up_grad, down_grad = call(
        functools.partial(expert_grad_kernel, outer, chips),
        (
            shape((model, hidden_units), f32),
            shape((model, hidden_units), f32),
            shape((hidden_units, model), f32),
        ),
        mebibytes=60,
        micros=20,
        grid=(model // unit_tile,),
        in_specs=[row_tile] * (2 * outer * chips) + [unit_once] * (3 * outer),
        out_specs=[
            pl.BlockSpec((unit_tile, hidden_units), lambda i: (i, 0)),
            pl.BlockSpec((unit_tile, hidden_units), lambda i: (i, 0)),
            pl.BlockSpec((hidden_units, unit_tile), lambda i: (0, i)),
        ],
        scratch_shapes=[pltpu.VMEM((total_slots, unit_tile), bf16)] * 2
        + [pltpu.VMEM((total_slots, hidden_units), bf16)] * 3,
    )(
        *[part for i in range(2) for keep in kept_late for part in keep[i]],
        *[keep[i] for i in range(2, 5) for keep in kept_late],
    )


    state = (grad_attn_low, gate_grad, up_grad, down_grad, moved_step, grad_logits_low)
    grad_attn_low, gate_grad, up_grad, down_grad, moved_step, grad_logits_low = fence(state)

    def next_step(step, *parts):
        total = step.astype(f32)
        for part in parts:
            total = total + part.astype(f32)
        return shift_outer(total.astype(bf16))

    out_send, out_keep = (
        lax.dot_general(
            context, grad_attn_low, CONTRACT_ROWS, preferred_element_type=f32
        ).astype(bf16)
        for context in (context_other, context_own)
    )
    out_swapped = swap_core(out_send)
    grad_context_own, grad_context_other = (
        lax.dot_general(
            grad_attn_low, weight, CONTRACT_LAST, preferred_element_type=f32
        ).astype(bf16)
        for weight in (out_own, out_other)
    )
    moved_own[2], partner = settle(picks[2], after(moved[2], out_send))
    moved_partner[2] = swap_core(partner)
    state = (out_keep, out_swapped, grad_context_own, grad_context_other)
    state, moved_own, moved_partner = fence((state, moved_own, moved_partner))
    out_keep, out_swapped, grad_context_own, grad_context_other = state
    out_half = (out_keep.astype(f32) + out_swapped.astype(f32)).astype(bf16)
    out_half = out_half.reshape(chips, span * rows_out, model)
    out_came = [swap_chip(out_half[r], r) for r in range(chips)]
    moved_step = next_step(moved_step, moved_own[2], moved_partner[2])
    grad_front_low, gain_terms = call(
        functools.partial(attend_back_kernel, scale),
        (shape((together, columns), bf16), shape((2, width), f32)),
        micros=18,
        grid=(chips,),
        in_specs=[
            blocks(columns),
            blocks(group_columns),
            blocks(width),
            blocks(width),
            blocks(half_columns),
            blocks(half_columns),
            blocks(width),
            blocks(width),
            blocks(count),
            once,
            once,
            order_once,
        ],
        out_specs=[blocks(columns), pl.BlockSpec((2, width), lambda b: (0, 0))],
        scratch_shapes=[pltpu.VMEM((count, group_columns), bf16)],
    )(
        projected,
        query_low,
        key_low,
        value_low,
        grad_context_own,
        grad_context_other,
        cosine_table,
        sine_table,
        allowed,
        query_gain_row,
        key_gain_row,
        out_order,
    )

    grad_front_low, gain_terms, out_came, moved_step, grad_logits_low = fence(
        (grad_front_low, gain_terms, out_came, moved_step, grad_logits_low)
    )

    half_model = model // CORES
    front_send, front_keep = (
        lax.dot_general(
            normed_low[:, k * half_model : (k + 1) * half_model],
            grad_front_low,
            CONTRACT_ROWS,
            preferred_element_type=f32,
        ).astype(bf16)
        for k in (1, 0)
    )
    front_swapped = swap_core(front_send)
    out_parts = [
        part[u * rows_out : (u + 1) * rows_out]
        for part in after(out_came, front_send)
        for u in range(span)
    ]
    target = (my_outer - jnp.arange(outer, dtype=i32)) % outer
    out_places = ((target // span) ^ my_chip) * span + target % span
    out_home, *out_away = call(
        choose_kernel,
        [shape((rows_out, model), bf16)] * outer,
        in_specs=[smem] + [vmem] * outer,
    )(out_places, *out_parts)
    out_step = shift_outer(out_away[0])
    for s in range(3, outer):
        moved[s] = spread(moving[s])
    state = (front_keep, front_swapped, moved, out_step, out_home, out_away)
    front_keep, front_swapped, moved, out_step, out_home, out_away = fence(state)
    front_half = call(add_kernel, [shape((chips * depth, columns), bf16)] * outer)(
        front_keep, front_swapped
    )

    def next_sum(step, part):
        return shift_outer(call(add_kernel, [shape(part.shape, bf16)])(step, part)[0])

    front_step = shift_outer(front_half[1])
    out_step = next_sum(out_step, out_away[1])
    piece_block = pl.BlockSpec((chips * depth, columns), lambda s, o: (0, 0))
    grad_normed = pl.pallas_call(
        functools.partial(project_back_kernel, outer, chips),
        out_shape=[shape((count, model), bf16)] * chips,
        grid_spec=pltpu.PrefetchScalarGridSpec(
            num_scalar_prefetch=1,
            grid=(outer,),
            in_specs=[
                pl.BlockSpec((together, columns), lambda s, o: (0, 0)),
                *[piece_block] * (CORES * outer),
                pl.BlockSpec((plane * depth, plane * depth), lambda s, o: (0, 0)),
            ],
            out_specs=[
                pl.BlockSpec(
                    (count, plane * depth), lambda s, o: (0, lax.rem(o[0] + outer - s, outer))
                )
            ]
            * chips,
        ),
        compiler_params=pltpu.CompilerParams(vmem_limit_bytes=32 * MEBIBYTE),
    )(
        outer_scalar,
        after(grad_front_low, *front_half),
        *front_pieces,
        *front_others,
        front_order,
    )
    first_gain_term = call(gain_back_kernel, shape((1, model), f32))(*grad_normed, *token_parts)
    gain_sums = jnp.concatenate(
        [first_gain_term.reshape(-1), second_gain_term.reshape(-1), gain_terms.reshape(-1)]
    ).reshape(-1, LANES)
    gain_sums = gain_sums + swap_core(gain_sums)
    for s in range(3, outer):
        moved_own[s], partner = settle(picks[s], moved[s])
        moved_partner[s] = swap_core(partner)
    state = (front_half, front_step, out_step, grad_normed, moved_own, moved_partner)
    state, gain_sums = fence((state, gain_sums))
    front_half, front_step, out_step, grad_normed, moved_own, moved_partner = state
    front_step = next_sum(front_step, front_half[2])
    for s in range(3, outer):
        out_step = next_sum(out_step, out_away[s - 1])
    arrived = [swap_chip(grad_normed[r], r) for r in range(1, chips)]
    router_part = lax.dot_general(
        after(grad_logits_low, *grad_normed)[:, :experts],
        second_wide[:, :model],
        CONTRACT_ROWS,
        preferred_element_type=f32,
    )
    router_part = scatter_outer(
        lambda o: lax.dynamic_slice_in_dim(router_part, o * (plane * depth), plane * depth, 1)
    )
    state = (front_step, out_step, arrived, router_part)
    front_step, out_step, arrived, router_part = fence(state)
    for s in range(3, outer):
        front_step = next_sum(front_step, front_half[s])
        moved_step = next_step(moved_step, moved_own[s], moved_partner[s])
    moved[0] = spread(moving[0])
    tokens_grad = call(tokens_back_kernel, shape((count, model), f32))(
        tokens, grad_normed[0], *arrived, grad_hidden, first_gain_row
    )
    gain_sums = sum([swap_chip(gain_sums, r) for r in range(1, chips)], gain_sums)
    router_part = sum(
        [
            swap_chip(
                lax.dynamic_slice_in_dim(
                    router_part, (my_chip ^ r) * (CORES * depth), CORES * depth, 1
                ),
                r,
            )
            for r in range(chips)
        ]
    )
    out_grad = out_step.astype(f32) + out_home.astype(f32)
    state = (front_step, moved_step, moved, gain_sums, router_part, tokens_grad, out_grad)
    front_step, moved_step, moved, gain_sums, router_part, tokens_grad, out_grad = fence(state)
    moved_own[0], partner = settle(picks[0], moved[0])
    moved_partner[0] = swap_core(partner)
    output = hidden + moved_own[0] + moved_partner[0].astype(f32) + moved_step.astype(f32)
    output = output.astype(bf16)
    front = (front_step.astype(f32) + front_half[0].astype(f32)).astype(bf16)
    front = front.reshape(chips, depth, columns)
    front = [swap_chip(front[r], r) for r in range(chips)]
    front, gain_sums, router_part = fence((front, gain_sums, router_part))
    gain_sums = sum([shift_outer(gain_sums, s) for s in range(1, outer)], gain_sums).reshape(-1)
    router_grad = (
        lax.dynamic_slice_in_dim(router_part, my_core * depth, depth, 1)
        + swap_core(lax.dynamic_slice_in_dim(router_part, (1 - my_core) * depth, depth, 1))
    ).T
    front = by_chip(front)

    def lay_out(first, last):
        return jnp.concatenate([part[:, first:last] for part in front], axis=1).astype(f32)

    query_grad = lay_out(0, group_columns)
    key_grad = lay_out(group_columns, group_columns + width)
    value_grad = lay_out(group_columns + width, columns)
    return (
        output,
        tokens_grad,
        query_grad,
        key_grad,
        value_grad,
        out_grad,
        router_grad,
        gate_grad[None],
        up_grad[None],
        down_grad[None],
        gain_sums[:model],
        gain_sums[model : 2 * model],
        gain_sums[2 * model : 2 * model + width],
        gain_sums[2 * model + width :],
    )


def solution(mesh):
    rows = P("fsdp", None)
    blocks = P("fsdp", None, None)
    placed = (rows,) * 9 + (blocks,) * 3 + (P(),) * 4
    return jax.shard_map(
        body,
        mesh=mesh,
        in_specs=placed,
        out_specs=(rows,) * 7 + (blocks,) * 3 + (P(),) * 4,
        check_vma=False,
    )
```

```python
import functools

import jax
import jax.numpy as jnp
from jax import lax
from jax.experimental import pallas as pl
from jax.experimental.pallas import tpu as pltpu
from jax.sharding import PartitionSpec as P

EPS = 1e-06
THETA = 1000000.0
NEGATIVE = -1e30
CORES = 2
LANES = 128
MEBIBYTE = 1024 * 1024
FLOPS_A_MICRO = 1_000_000_000
BYTES_A_MICRO = 2_000_000
CONTRACT_ROWS = (((0,), (0,)), ((), ()))
CONTRACT_LAST = (((1,), (1,)), ((), ()))


def root_mean_square_norm(value_rows, gain):
    return (
        value_rows
        * lax.rsqrt(jnp.mean(value_rows * value_rows, axis=-1, keepdims=True) + EPS)
        * gain
    )


def sequence_layout(lengths, count_total):
    ends = jnp.cumsum(lengths)
    starts = ends - lengths
    places = jnp.arange(count_total, dtype=jnp.int32)
    member = ((places[:, None] >= starts[None, :]) & (places[:, None] < ends[None, :])).astype(
        jnp.int32
    )
    labels = jnp.arange(lengths.shape[0], dtype=jnp.int32)
    segment = jnp.sum(member * labels[None, :], axis=1)
    offset = jnp.sum(member * starts[None, :], axis=1)
    return (segment, places - offset)


def rotary_tables(position, width):
    half = width // 2
    inverse = jnp.power(THETA, -(jnp.arange(half, dtype=jnp.float32) * 2.0) / width)
    angle = position.astype(jnp.float32)[:, None] * inverse[None, :]
    angle = jnp.concatenate([angle, angle], axis=1)
    return (jnp.cos(angle), jnp.sin(angle))


def call(kernel, outs, mebibytes=32, micros=0, **specs):
    if micros:
        specs["cost_estimate"] = pl.CostEstimate(
            flops=micros * FLOPS_A_MICRO, bytes_accessed=micros * BYTES_A_MICRO, transcendentals=0
        )
    return pl.pallas_call(
        kernel,
        out_shape=outs,
        compiler_params=pltpu.CompilerParams(vmem_limit_bytes=mebibytes * MEBIBYTE),
        **specs,
    )


def turned_sine(sine_table):
    half = sine_table.shape[1] // 2
    return jnp.concatenate([-sine_table[:, :half], sine_table[:, half:]], axis=1)


def head_rotated(value, gain, cosine, sine):
    normal = (
        value * lax.rsqrt(jnp.mean(value * value, axis=-1, keepdims=True) + EPS) * gain
    )
    return normal * cosine + pltpu.roll(normal, value.shape[1] // 2, 1) * sine


def head_shares(query, key, allowed, scale):
    scores = lax.dot_general(query, key, CONTRACT_LAST, preferred_element_type=jnp.float32)
    scores = jnp.where(allowed, scores * scale, NEGATIVE)
    exponent = jnp.exp(scores - jnp.max(scores, axis=-1, keepdims=True))
    return exponent * (1.0 / jnp.sum(exponent, axis=-1, keepdims=True))


def stacked(source, heads, width):
    return jnp.concatenate(
        [source[:, h * width : (h + 1) * width] for h in range(heads)], axis=0
    )


def norm_kernel(outer, my_outer, *refs):
    *parts, gain, order, out, normed = refs
    count = parts[0].shape[0]
    span = order.shape[0]
    half = span // CORES
    for b, part in enumerate(parts):
        normed[b * count : (b + 1) * count, :] = root_mean_square_norm(
            part[...].astype(jnp.float32), gain[...]
        ).astype(jnp.bfloat16)
    for s in range(outer):
        start = lax.rem(my_outer[0] + (outer - s), outer) * span
        block = normed[:, pl.ds(pl.multiple_of(start, LANES), span)]
        block = jnp.dot(block, order[...], preferred_element_type=jnp.float32)
        block = block.astype(jnp.bfloat16)
        for k in range(CORES):
            first = (k * outer + s) * half
            out[:, first : first + half] = block[:, k * half : (k + 1) * half]


def project_kernel(normed, *refs):
    *pieces, out = refs
    rows = pieces[0].shape[0]
    total = jnp.zeros(out.shape, jnp.float32)
    for i, piece in enumerate(pieces):
        total += jnp.dot(
            normed[:, i * rows : (i + 1) * rows], piece[...], preferred_element_type=jnp.float32
        )
    out[...] = total


def add_kernel(first, second, *outs):
    rows = outs[0].shape[0]
    for i, out in enumerate(outs):
        part = slice(i * rows, (i + 1) * rows)
        total = first[part, :].astype(jnp.float32) + second[part, :].astype(jnp.float32)
        out[...] = total.astype(out.dtype)


def choose_kernel(places, *refs):
    half = len(refs) // 2
    parts, outs = refs[:half], refs[half:]
    for i, out in enumerate(outs):
        for j, part in enumerate(parts):

            @pl.when(places[i] == j)
            def _(part=part, out=out):
                out[...] = part[...]


def project_back_kernel(outer, chips, my_outer, grad, *refs):
    *pieces, order = refs[:-chips]
    outs = refs[-chips:]
    f32, bf16 = jnp.float32, jnp.bfloat16
    count = outs[0].shape[0]
    for s in range(outer):

        @pl.when(pl.program_id(0) == s)
        def _(s=s):
            block = jnp.concatenate(
                [
                    lax.dot_general(
                        grad[...], part[...], CONTRACT_LAST, preferred_element_type=f32
                    )
                    for part in pieces[s::outer]
                ],
                axis=1,
            ).astype(bf16)
            block = lax.dot_general(
                block, order[...], CONTRACT_LAST, preferred_element_type=f32
            ).astype(bf16)
            for r, out in enumerate(outs):
                out[...] = block[r * count : (r + 1) * count, :]


def router_order_kernel(outer, experts, my_outer, *refs):
    *pieces, order, out = refs
    span = order.shape[0]
    column = lax.broadcasted_iota(jnp.int32, (span, out.shape[1]), 1)
    for s in range(outer):
        block = jnp.concatenate([part[...] for part in pieces[s::outer]], axis=0)
        block = jnp.dot(order[...], block, preferred_element_type=jnp.float32)
        start = pl.multiple_of(lax.rem(my_outer[0] + (outer - s), outer) * span, LANES)
        out[pl.ds(start, span), :] = jnp.where(column < experts, block, 0.0).astype(jnp.bfloat16)


def gain_back_kernel(*refs):
    *parts, gain_grad = refs
    half = len(parts) // 2
    total = jnp.zeros(gain_grad.shape, jnp.float32)
    for grad, part in zip(parts[:half], parts[half:]):
        value = part[...].astype(jnp.float32)
        root = lax.rsqrt(jnp.mean(value * value, axis=-1, keepdims=True) + EPS)
        total += jnp.sum(grad[...].astype(jnp.float32) * value * root, axis=0, keepdims=True)
    gain_grad[...] = total


def tokens_back_kernel(tokens, own, *refs):
    *others, hidden_grad, gain, tokens_grad = refs
    f32 = jnp.float32
    grad = own[...].astype(f32)
    for other in others:
        grad = grad + other[...].astype(f32)
    value = tokens[...].astype(f32)
    root = lax.rsqrt(jnp.mean(value * value, axis=-1, keepdims=True) + EPS)
    normal = value * root
    grad = grad * gain[...]
    tokens_grad[...] = hidden_grad[...] + root * (
        grad - normal * jnp.mean(normal * grad, axis=-1, keepdims=True)
    )


def attend_kernel(scale, front, cosine, sine, allowed, query_gain, key_gain, order, *outs):
    query_out, key_out, value_out, context_out, context = outs
    width = cosine.shape[1]
    heads = query_out.shape[1] // width
    bf16 = jnp.bfloat16
    cos, sin = cosine[...], sine[...]
    key = head_rotated(
        front[:, heads * width : (heads + 1) * width], key_gain[...], cos, sin
    ).astype(bf16)
    value = front[:, (heads + 1) * width :].astype(bf16)
    key_out[...] = key
    value_out[...] = value
    count = cos.shape[0]
    all_cos, all_sin = (jnp.concatenate([table] * heads, axis=0) for table in (cos, sin))
    all_places = jnp.concatenate([allowed[...]] * heads, axis=0) > 0.0
    query = head_rotated(stacked(front, heads, width), query_gain[...], all_cos, all_sin)
    query = query.astype(bf16)
    shares = head_shares(query, key, all_places, scale).astype(bf16)
    mixed = jnp.dot(shares, value, preferred_element_type=jnp.float32).astype(bf16)
    for h in range(heads):
        part, rows = slice(h * width, (h + 1) * width), slice(h * count, (h + 1) * count)
        query_out[:, part] = query[rows, :]
        context[:, part] = mixed[rows, :]
    context_out[...] = jnp.dot(
        context[...], order[...], preferred_element_type=jnp.float32
    ).astype(bf16)


def head_back(grad, value, gain, cosine, sine):
    grad = grad * cosine + pltpu.roll(grad * sine, value.shape[1] // 2, 1)
    root = lax.rsqrt(jnp.mean(value * value, axis=-1, keepdims=True) + EPS)
    normal = value * root
    gain_grad = jnp.sum(grad * normal, axis=0, keepdims=True)
    grad = grad * gain
    grad = root * (grad - normal * jnp.mean(normal * grad, axis=-1, keepdims=True))
    return grad, gain_grad


def attend_back_kernel(
    scale, front, query_in, key_in, value_in, grad_own, grad_other, cosine, sine, allowed, *rest
):
    query_gain, key_gain, order, front_grad, gain_grads, context_grad = rest
    half = grad_own.shape[1]
    context_grad[...] = (
        lax.dot_general(
            grad_own[...], order[:, :half], CONTRACT_LAST, preferred_element_type=jnp.float32
        )
        + lax.dot_general(
            grad_other[...], order[:, half:], CONTRACT_LAST, preferred_element_type=jnp.float32
        )
    ).astype(jnp.bfloat16)
    width = cosine.shape[1]
    heads = query_in.shape[1] // width
    f32, bf16 = jnp.float32, jnp.bfloat16
    cos, sin = cosine[...], sine[...]
    count = cos.shape[0]
    all_cos, all_sin = (jnp.concatenate([table] * heads, axis=0) for table in (cos, sin))
    all_places = jnp.concatenate([allowed[...]] * heads, axis=0) > 0.0
    key, value = key_in[...], value_in[...]
    query, grad = stacked(query_in, heads, width), stacked(context_grad, heads, width)
    shares = head_shares(query, key, all_places, scale)
    grad_shares = lax.dot_general(grad, value, CONTRACT_LAST, preferred_element_type=f32)
    grad_scores = (
        shares * (grad_shares - jnp.sum(shares * grad_shares, axis=-1, keepdims=True))
    ).astype(bf16)
    value_total = lax.dot_general(
        shares.astype(bf16), grad, CONTRACT_ROWS, preferred_element_type=f32
    )
    key_total = lax.dot_general(grad_scores, query, CONTRACT_ROWS, preferred_element_type=f32)
    grad_query = jnp.dot(grad_scores, key, preferred_element_type=f32) * scale
    grad_query, gain_total = head_back(
        grad_query, stacked(front, heads, width), query_gain[...], all_cos, all_sin
    )
    grad_query = grad_query.astype(bf16)
    for h in range(heads):
        front_grad[:, h * width : (h + 1) * width] = grad_query[h * count : (h + 1) * count, :]
    part = slice(heads * width, (heads + 1) * width)
    grad_key, key_gain_grad = head_back(
        key_total * scale, front[:, part], key_gain[...], cos, sin
    )
    front_grad[:, part] = grad_key.astype(bf16)
    front_grad[:, (heads + 1) * width :] = value_total.astype(bf16)

    @pl.when(pl.program_id(0) == 0)
    def _():
        gain_grads[...] = jnp.zeros(gain_grads.shape, f32)

    gain_grads[0:1, :] += gain_total
    gain_grads[1:2, :] += key_gain_grad


def router_kernel(experts, *refs):
    tokens, own, *others, gain, router, mask, hidden_out, wide_out, prob_out, gates_out = refs
    f32, bf16 = jnp.float32, jnp.bfloat16
    model = tokens.shape[1]
    lanes = mask.shape[1]
    hidden = tokens[...].astype(f32) + own[...]
    for other in others:
        hidden = hidden + other[...].astype(f32)
    hidden_out[...] = hidden
    second = root_mean_square_norm(hidden, gain[...]).astype(bf16)
    wide_out[:, :model] = second
    logits = jnp.dot(second, router[...], preferred_element_type=f32)
    column = lax.broadcasted_iota(jnp.int32, logits.shape, 1)
    logits = jnp.where(column < experts, logits, NEGATIVE)
    exponent = jnp.exp(logits - jnp.max(logits, axis=-1, keepdims=True))
    prob = exponent / jnp.sum(exponent, axis=-1, keepdims=True)
    chosen = prob * mask[...]
    gates = chosen / jnp.sum(chosen, axis=-1, keepdims=True)
    prob_out[...] = prob
    gates_out[...] = gates
    high = gates.astype(bf16).astype(f32)
    low = gates - high
    if 2 * experts <= lanes:
        wide_out[:, model:] = (high + pltpu.roll(low, experts, 1)).astype(bf16)
    else:
        wide_out[:, model : model + lanes] = high.astype(bf16)
        wide_out[:, model + lanes :] = low.astype(bf16)


def router_back_kernel(experts, *refs):
    own, near, came, cotangent, hidden, gain, router, mask, prob, gates, *outs = refs
    hidden_grad, attn_grad, logits_grad, gain_grad = outs
    f32, bf16 = jnp.float32, jnp.bfloat16
    model = cotangent.shape[1]
    lanes = mask.shape[1]
    pairs = own[:, model:] + near[:, model:].astype(f32) + came[:, model:].astype(f32)
    if 2 * experts <= lanes:
        grad_gates = pairs + pltpu.roll(pairs, lanes - experts, 1)
    else:
        grad_gates = pairs[:, :lanes] + pairs[:, lanes:]
    chosen_sum = jnp.sum(prob[...] * mask[...], axis=-1, keepdims=True)
    grad_gates = jnp.where(mask[...] > 0.0, grad_gates, 0.0)
    grad_chosen = (
        mask[...]
        * (grad_gates - jnp.sum(gates[...] * grad_gates, axis=-1, keepdims=True))
        / chosen_sum
    )
    grad_logits = (
        prob[...] * (grad_chosen - jnp.sum(prob[...] * grad_chosen, axis=-1, keepdims=True))
    ).astype(bf16)
    logits_grad[...] = grad_logits
    grad = (
        own[:, :model]
        + near[:, :model].astype(f32)
        + came[:, :model].astype(f32)
        + lax.dot_general(grad_logits, router[...], CONTRACT_LAST, preferred_element_type=f32)
    )
    value = hidden[...]
    root = lax.rsqrt(jnp.mean(value * value, axis=-1, keepdims=True) + EPS)
    normal = value * root
    gain_grad[...] = jnp.sum(grad * normal, axis=0, keepdims=True)
    grad = grad * gain[...]
    grad = cotangent[...].astype(f32) + root * (
        grad - normal * jnp.mean(normal * grad, axis=-1, keepdims=True)
    )
    hidden_grad[...] = grad
    attn_grad[...] = grad.astype(bf16)


def pick_kernel(capacity, own, partner, near, earlier, *outs):
    *parts, picks = outs
    f32, bf16 = jnp.float32, jnp.bfloat16
    rows, model = parts[0].shape
    count = own.shape[0]
    masks = [
        lax.dot_general(near[...], side[:, model:], CONTRACT_LAST, preferred_element_type=f32)
        for side in (own, partner)
    ]
    ranks = [jnp.dot(m.astype(bf16), earlier[...], preferred_element_type=f32) for m in masks]
    mask = jnp.concatenate(masks, axis=1)
    rank = jnp.concatenate([ranks[0], ranks[1] + capacity], axis=1)
    place = lax.broadcasted_iota(jnp.int32, (rows, CORES * count), 0).astype(f32)
    for r in range(len(parts)):
        hit = (place == rank[r : r + 1, :]) & (mask[r : r + 1, :] > 0.5)
        picks[r * rows : (r + 1) * rows, :] = jnp.where(hit, 1.0, 0.0).astype(bf16)
    both = jnp.concatenate([own[:, :model], partner[:, :model]], axis=0)
    chosen = jnp.dot(picks[...], both, preferred_element_type=f32).astype(bf16)
    for r, part in enumerate(parts):
        part[...] = chosen[r * rows : (r + 1) * rows, :]


def send_kernel(picks, own, partner, *parts):
    rows = parts[0].shape[0]
    both = jnp.concatenate([own[...], partner[...]], axis=0)
    chosen = jnp.dot(picks[...], both, preferred_element_type=jnp.float32).astype(jnp.bfloat16)
    for r, part in enumerate(parts):
        part[...] = chosen[r * rows : (r + 1) * rows, :]


def settle_kernel(picks, *refs):
    *parts, own, partner = refs
    count = own.shape[0]
    rows = jnp.concatenate([part[...] for part in parts], axis=0)
    total = lax.dot_general(
        picks[...], rows, CONTRACT_ROWS, preferred_element_type=jnp.float32
    )
    own[...] = total[:count, :]
    partner[...] = total[count:, :].astype(jnp.bfloat16)


def move_kernel(units, weight, *parts):
    rows = parts[0].shape[0]
    moved = jnp.dot(units[...], weight[...], preferred_element_type=jnp.float32)
    for r, part in enumerate(parts):
        part[...] = moved[r * rows : (r + 1) * rows, :].astype(jnp.bfloat16)


def expert_kernel(chips, experts, me, *refs):
    f32, bf16 = jnp.float32, jnp.bfloat16
    came, given = refs[:chips], refs[chips : 2 * chips]
    gate_weight, up_weight, down_weight = refs[2 * chips : 2 * chips + 3]
    back = refs[2 * chips + 3 : 3 * chips + 3]
    units_out, gate_out, up_out, rows, grads, row_gate, change, total = refs[3 * chips + 3 :]
    size, model = came[0].shape[0], rows.shape[1]
    step = pl.program_id(0)
    column = lax.broadcasted_iota(jnp.int32, (size, came[0].shape[1] - model), 1)
    high_column, low_column = column == me[0], column == me[0] + experts

    @pl.when(step == 0)
    def _():
        for r in range(chips):
            part = slice(r * size, (r + 1) * size)
            rows[part, :] = came[r][:, :model]
            grads[part, :] = given[r][...]
            side = jnp.where(high_column | low_column, came[r][:, model:].astype(f32), 0.0)
            row_gate[part, :] = jnp.sum(side, axis=1, keepdims=True)
        change[...] = jnp.zeros(change.shape, f32)
        total[...] = jnp.zeros(total.shape, f32)

    gate_part = jnp.dot(rows[...], gate_weight[...], preferred_element_type=f32)
    up_part = jnp.dot(rows[...], up_weight[...], preferred_element_type=f32)
    raw = lax.dot_general(
        grads[...], down_weight[...], CONTRACT_LAST, preferred_element_type=f32
    )
    sig = 1.0 / (1.0 + jnp.exp(-gate_part))
    silu = gate_part * sig
    units = silu * up_part
    change[...] += jnp.sum(units * raw, axis=1, keepdims=True)
    units_out[...] = (row_gate[...] * units).astype(bf16)
    grad_units = row_gate[...] * raw
    gate_grad = (grad_units * up_part * sig * (1.0 + gate_part * (1.0 - sig))).astype(bf16)
    up_grad = (grad_units * silu).astype(bf16)
    gate_out[...] = gate_grad
    up_out[...] = up_grad
    total[...] += lax.dot_general(
        gate_grad, gate_weight[...], CONTRACT_LAST, preferred_element_type=f32
    ) + lax.dot_general(up_grad, up_weight[...], CONTRACT_LAST, preferred_element_type=f32)

    @pl.when(step == pl.num_programs(0) - 1)
    def _():
        for r in range(chips):
            part = slice(r * size, (r + 1) * size)
            back[r][:, :model] = total[part, :].astype(bf16)
            high = change[part, :].astype(bf16).astype(f32)
            low = change[part, :] - high
            back[r][:, model:] = (
                jnp.where(high_column, high, 0.0) + jnp.where(low_column, low, 0.0)
            ).astype(bf16)


def expert_grad_kernel(outer, chips, *refs):
    f32 = jnp.float32
    parts = outer * chips
    rows, grads = refs[:parts], refs[parts : 2 * parts]
    units, gates, ups = (
        refs[2 * parts + i * outer : 2 * parts + (i + 1) * outer] for i in range(3)
    )
    gate_out, up_out, down_out, left, right, all_units, all_gates, all_ups = refs[
        2 * parts + 3 * outer :
    ]
    size = rows[0].shape[0]
    for i in range(parts):
        part = slice(i * size, (i + 1) * size)
        left[part, :] = rows[i][...]
        right[part, :] = grads[i][...]
    size = units[0].shape[0]

    @pl.when(pl.program_id(0) == 0)
    def _():
        for s in range(outer):
            part = slice(s * size, (s + 1) * size)
            all_units[part, :] = units[s][...]
            all_gates[part, :] = gates[s][...]
            all_ups[part, :] = ups[s][...]

    def product(a, b):
        return lax.dot_general(a[...], b[...], CONTRACT_ROWS, preferred_element_type=f32)

    gate_out[...] = product(left, all_gates)
    up_out[...] = product(left, all_ups)
    down_out[...] = product(all_units, right)


def round_up(number, step):
    return -(-number // step) * step


def after(value, *others):
    return lax.optimization_barrier((value, *others))[0]


def body(
    tokens,
    cotangent,
    lengths,
    routes,
    query_weight,
    key_matrix,
    value_matrix,
    out_weight,
    router_weight,
    expert_gate,
    expert_up,
    expert_down,
    first_gain,
    second_gain,
    query_norm_gain,
    key_gain,
):
    f32, bf16, i32 = jnp.float32, jnp.bfloat16, jnp.int32
    shape = jax.ShapeDtypeStruct
    fence = lax.optimization_barrier
    count, model = tokens.shape
    width = query_norm_gain.shape[0]
    heads = query_weight.shape[1] // width
    kv_heads = key_matrix.shape[1] // width
    head_group = heads // kv_heads
    choose = routes.shape[1]
    shards = lax.axis_size("fsdp")
    experts = shards * expert_gate.shape[0]
    capacity = max(2, count * choose * 5 // (4 * experts))
    scale = width ** (-0.5)

    chips = kv_heads
    plane = chips * CORES
    outer = shards // plane
    span = outer // chips
    me = lax.axis_index("fsdp")
    my_core = me % CORES
    my_chip = (me // CORES) % chips
    my_outer = me // plane
    me_scalar = me.reshape(1)
    outer_scalar = my_outer.reshape(1)
    smem = pl.BlockSpec(memory_space=pltpu.SMEM)
    vmem = pl.BlockSpec(memory_space=pltpu.VMEM)

    def swap_core(value):
        return lax.ppermute(value, "fsdp", [(i, i ^ 1) for i in range(shards)])

    def swap_chip(value, r):
        if r == 0:
            return value
        return lax.ppermute(value, "fsdp", [(i, i ^ (r * CORES)) for i in range(shards)])

    def shift_outer(value, s=1):
        if s == 0:
            return value
        return lax.ppermute(
            value,
            "fsdp",
            [(i, ((i // plane + s) % outer) * plane + i % plane) for i in range(shards)],
        )

    def gather_chips(value):
        return [swap_chip(value, r) for r in range(chips)]

    def spread(parts):
        return [swap_chip(part, r) for r, part in enumerate(parts)]

    def scatter_outer(take):
        total = take(my_outer)
        for s in range(1, outer):
            total = total + shift_outer(take((my_outer + s) % outer), s)
        return total

    def by_chip(parts):
        parts = jnp.stack(parts)
        return [
            lax.dynamic_index_in_dim(parts, my_chip ^ m, 0, keepdims=False) for m in range(chips)
        ]

    depth = query_weight.shape[0]
    group_columns = head_group * width
    half_columns = group_columns // CORES
    columns = group_columns + 2 * width
    rows_out = out_weight.shape[0]

    lanes = round_up(experts, LANES)
    pair_width = round_up(2 * experts, LANES)
    part_rows = round_up(CORES * capacity, 16)
    slots = chips * part_rows

    def dispatch_first(piece, partner):
        *parts, picks = call(
            functools.partial(pick_kernel, capacity),
            [shape((part_rows, model), bf16)] * chips + [shape((slots, CORES * count), bf16)],
            mebibytes=16,
        )(piece, partner, near, earlier)
        return parts, picks

    def dispatch(picks, piece, partner):
        outs = [shape((part_rows, piece.shape[1]), bf16)] * chips
        return call(send_kernel, outs, mebibytes=16)(picks, piece, partner)

    def settle(picks, parts):
        columns_of = parts[0].shape[1]
        return call(
            settle_kernel,
            (shape((count, columns_of), f32), shape((count, columns_of), bf16)),
            mebibytes=16,
        )(picks, *parts)

    together = chips * count
    first_gain_row, second_gain_row = first_gain[None, :], second_gain[None, :]
    query_gain_row, key_gain_row = query_norm_gain[None, :], key_gain[None, :]

    def norm(token_parts):
        return call(
            functools.partial(norm_kernel, outer),
            shape((together, model), bf16),
            in_specs=[smem] + [vmem] * (chips + 2),
            scratch_shapes=[pltpu.VMEM((together, model), bf16)],
        )(outer_scalar, *token_parts, first_gain_row, front_order)

    def positions(length_parts):
        layouts = [sequence_layout(part[0], count) for part in length_parts]
        segment = jnp.stack([layout[0] for layout in layouts])
        position = jnp.concatenate([layout[1] for layout in layouts])
        cosine_table, sine_table = rotary_tables(position, width)
        sine_table = turned_sine(sine_table)
        places = jnp.arange(count, dtype=i32)
        allowed = (segment[:, :, None] == segment[:, None, :]) & (
            places[None, None, :] <= places[None, :, None]
        )
        return cosine_table, sine_table, allowed.astype(f32).reshape(together, count)

    sequences = lengths.shape[1]
    side_width = round_up(experts + sequences, LANES)
    side = jnp.pad(router_weight, ((0, 0), (0, side_width - experts))) + jnp.pad(
        lengths.astype(bf16), ((0, depth - 1), (experts, side_width - experts - sequences))
    )
    cut = []
    for r in range(chips):
        target = my_chip ^ r
        part = [
            lax.dynamic_slice_in_dim(query_weight, target * group_columns, group_columns, 1),
            lax.dynamic_slice_in_dim(key_matrix, target * width, width, 1),
            lax.dynamic_slice_in_dim(value_matrix, target * width, width, 1),
            side,
        ]
        cut.append(swap_chip(jnp.concatenate(part, axis=1), r))
    out_pieces = [out_weight, shift_outer(out_weight)]
    front_pieces, front_others = [], []
    state = fence((cut, out_pieces, routes, tokens, cotangent))
    cut, out_pieces, routes, tokens, cotangent = state
    length_parts = [
        part[:1, columns + experts : columns + experts + sequences].astype(i32) for part in cut
    ]
    cut = jnp.concatenate(cut, axis=0)
    me = after(me, cut)
    my_core, my_chip, my_outer = me % CORES, (me // CORES) % chips, me // plane

    def arrival_order(length, block, inner):
        place = jnp.arange(length, dtype=i32)
        went_to = (
            (
                ((place // block % CORES) ^ my_core) * chips
                + ((place // (block * CORES) % chips) ^ my_chip)
            )
            * inner
            + place // (block * plane)
        ) * block + place % block
        return (went_to[:, None] == place[None, :]).astype(bf16)

    front_order = arrival_order(plane * depth, depth, 1)
    out_order = arrival_order(group_columns, rows_out, span)

    mask = jnp.sum(
        (routes[:, :, None] == jnp.arange(lanes, dtype=i32)[None, None, :]).astype(f32), axis=1
    )
    near = jnp.arange(2 * chips, dtype=i32)
    near = jnp.where(
        near < chips, my_outer * plane + (my_chip ^ near) * CORES + my_core, -1
    )
    near = (near[:, None] == jnp.arange(lanes, dtype=i32)[None, :]).astype(bf16)
    earlier = jnp.triu(jnp.ones((count, count), bf16), 1)
    cotangent_wide = jnp.concatenate([cotangent, mask.astype(bf16)], axis=1)
    cotangent_pieces, cotangent_parts, picks = [cotangent_wide], [], []
    cotangent_partners = []

    def send_cotangent(s):
        parts, pick = dispatch_first(cotangent_pieces[s], cotangent_partners[s])
        cotangent_parts.append(spread(parts))
        picks.append(pick)

    front_pieces.append(cut)
    for t in range(2, outer + 1):
        front_pieces.append(shift_outer(front_pieces[-1]))
        if t < outer:
            out_pieces.append(shift_outer(out_pieces[-1]))
        front_others.append(swap_core(front_pieces[-2]))
        if t == 2:
            token_parts = [swap_chip(tokens, r) for r in range(chips - 1)]
            cotangent_partners.append(swap_core(cotangent_pieces[0]))
            state = (token_parts, cotangent_partners, positions(length_parts))
            state = fence((state, front_pieces, front_others, out_pieces))
            (token_parts, cotangent_partners, tables), *state = state
            cosine_table, sine_table, allowed = tables
        elif t == 3:
            token_parts.append(swap_chip(tokens, chips - 1))
            send_cotangent(0)
            state = (cotangent_parts, picks, token_parts)
            state = fence((state, front_pieces, front_others, out_pieces))
            (cotangent_parts, picks, token_parts), *state = state
        elif t < outer:
            state = fence((front_pieces, front_others, out_pieces))
        else:
            cotangent_pieces.append(shift_outer(cotangent_pieces[0]))
            normed_low = norm(token_parts)
            stacked = jnp.stack(out_pieces)
            out_own = []
            for r in range(chips):
                part = [
                    lax.dynamic_index_in_dim(
                        stacked,
                        (my_outer + outer - ((my_chip ^ r) * span + u)) % outer,
                        0,
                        keepdims=False,
                    )
                    for u in range(span)
                ]
                out_own.append(swap_chip(jnp.concatenate(part, axis=0), r))
            state = fence((front_pieces, front_others, out_pieces))
        front_pieces, front_others, out_pieces = state
    cotangent_pieces, out_own, normed_low = fence((cotangent_pieces, out_own, normed_low))

    front_others.append(swap_core(front_pieces[-1]))
    cotangent_partners.append(swap_core(cotangent_pieces[1]))
    out_own = jnp.concatenate(out_own, axis=0)
    front_others, cotangent_partners, out_own = fence((front_others, cotangent_partners, out_own))
    out_other = swap_core(out_own)
    for s in range(2, outer - 1):
        cotangent_pieces.append(shift_outer(cotangent_pieces[-1]))
    tile = 2 * width
    projected = call(
        project_kernel,
        shape((together, columns), f32),
        grid=(columns // tile,),
        in_specs=[pl.BlockSpec((together, model), lambda n: (0, 0))]
        + [pl.BlockSpec((chips * depth, tile), lambda n: (0, n))] * (CORES * outer),
        out_specs=pl.BlockSpec((together, tile), lambda n: (0, n)),
    )(normed_low, *front_pieces, *front_others)

    cotangent_pieces[1] = after(cotangent_pieces[1], projected)
    send_cotangent(1)

    def blocks(columns_of):
        return pl.BlockSpec((count, columns_of), lambda b: (b, 0))

    once = pl.BlockSpec((1, width), lambda b: (0, 0))
    order_once = pl.BlockSpec((group_columns, group_columns), lambda b: (0, 0))
    query_low, key_low, value_low, context_low = call(
        functools.partial(attend_kernel, scale),
        (
            shape((together, group_columns), bf16),
            shape((together, width), bf16),
            shape((together, width), bf16),
            shape((together, group_columns), bf16),
        ),
        grid=(chips,),
        in_specs=[
            blocks(columns),
            blocks(width),
            blocks(width),
            blocks(count),
            once,
            once,
            order_once,
        ],
        out_specs=[blocks(group_columns), blocks(width), blocks(width), blocks(group_columns)],
        scratch_shapes=[pltpu.VMEM((count, group_columns), bf16)],
    )(projected, cosine_table, sine_table, allowed, query_gain_row, key_gain_row, out_order)
    state = (context_low, out_other, cotangent_pieces, cotangent_parts, picks)
    state = fence((state, query_low, key_low, value_low, projected))
    (context_low, out_other, cotangent_pieces, cotangent_parts, picks), *state = state
    query_low, key_low, value_low, projected = state
    context_own, context_other = context_low[:, :half_columns], context_low[:, half_columns:]

    def attended(first, last):
        return jnp.dot(
            context_own[first:last], out_own, preferred_element_type=f32
        ) + jnp.dot(context_other[first:last], out_other, preferred_element_type=f32)

    away = attended(count, together).astype(bf16)
    arrived = [swap_chip(away[(r - 1) * count : r * count], r) for r in range(1, chips)]
    home = attended(0, count)
    cotangent_pieces.append(shift_outer(cotangent_pieces[-1]))
    cotangent_partners.append(swap_core(cotangent_pieces[2]))
    router_block = pl.BlockSpec((chips * depth, lanes), lambda n: (0, columns // lanes))
    order_block = pl.BlockSpec((plane * depth, plane * depth), lambda n: (0, 0))
    router_wide = call(
        functools.partial(router_order_kernel, outer, experts),
        shape((model, lanes), bf16),
        grid=(1,),
        in_specs=[smem, *[router_block] * (CORES * outer), order_block],
        out_specs=pl.BlockSpec((model, lanes), lambda n: (0, 0)),
    )(outer_scalar, *front_pieces, *front_others, after(front_order, away))
    arrived, home, cotangent_pieces, cotangent_partners, router_wide = fence(
        (arrived, home, cotangent_pieces, cotangent_partners, router_wide)
    )
    hidden, second_wide, prob, gates = call(
        functools.partial(router_kernel, experts),
        (
            shape((count, model), f32),
            shape((count, model + pair_width), bf16),
            shape((count, lanes), f32),
            shape((count, lanes), f32),
        ),
    )(tokens, home, *arrived, second_gain_row, router_wide, mask)

    gate_weight, up_weight, down_weight = expert_gate[0], expert_up[0], expert_down[0]
    hidden_units = gate_weight.shape[1]
    unit_tile = 2 * LANES

    def expert(came, given):
        part = pl.BlockSpec((part_rows, model + pair_width), lambda f: (0, 0))
        units = pl.BlockSpec((slots, unit_tile), lambda f: (0, f))
        outs = call(
            functools.partial(expert_kernel, chips, experts),
            [shape((part_rows, model + pair_width), bf16)] * chips
            + [shape((slots, hidden_units), bf16)] * 3,
            micros=11,
            grid=(hidden_units // unit_tile,),
            in_specs=[smem]
            + [part] * chips
            + [pl.BlockSpec((part_rows, model), lambda f: (0, 0))] * chips
            + [pl.BlockSpec((model, unit_tile), lambda f: (0, f))] * 2
            + [pl.BlockSpec((unit_tile, model), lambda f: (f, 0))],
            out_specs=[part] * chips + [units] * 3,
            scratch_shapes=[
                pltpu.VMEM((slots, model), bf16),
                pltpu.VMEM((slots, model), bf16),
                pltpu.VMEM((slots, 1), f32),
                pltpu.VMEM((slots, 1), f32),
                pltpu.VMEM((slots, model), f32),
            ],
        )(me_scalar, *came, *given, gate_weight, up_weight, down_weight)
        return outs[:chips], (came, given, *outs[chips:])

    def move(s):
        return call(move_kernel, [shape((part_rows, model), bf16)] * chips, mebibytes=16)(
            kept[s][2], down_weight
        )

    second_pieces, second_partners = [second_wide], []
    came, backs, kept, returned, settled_own, settled_partner = {}, {}, {}, {}, {}, {}
    moved, moving, moved_own, moved_partner = {}, [], {}, {}
    grad_step = None
    for t in range(outer + 5):
        if 0 <= t - 1 < outer:
            sent = dispatch(picks[t - 1], second_pieces[t - 1], second_partners[t - 1])
            came[t - 1] = spread(sent)
        if 2 <= t + 2 < outer:
            send_cotangent(t + 2)
        if t + 3 < outer:
            cotangent_partners.append(swap_core(cotangent_pieces[t + 3]))
        if t + 1 < outer:
            second_pieces.append(shift_outer(second_pieces[t]))
        if t < outer:
            second_partners.append(swap_core(second_pieces[t]))
        if t - 5 >= 1:
            total = settled_own[t - 5] + settled_partner[t - 5].astype(f32)
            if grad_step is not None:
                total = total + grad_step.astype(f32)
            grad_step = shift_outer(total.astype(bf16))
        if 0 <= t - 4 < outer:
            settled_own[t - 4], partner = settle(picks[t - 4], returned[t - 4])
            settled_partner[t - 4] = swap_core(partner)
        if 0 <= t - 3 < outer:
            returned[t - 3] = spread(backs[t - 3])
        if t == outer + 2:
            moving = [move(i) for i in range(outer)]
        if t >= outer + 3:
            moved[t - outer - 2] = spread(moving[t - outer - 2])
        if t == outer + 4:
            moved_own[1], partner = settle(picks[1], moved[1])
            moved_partner[1] = swap_core(partner)
        if 0 <= t - 2 < outer:
            backs[t - 2], kept[t - 2] = expert(came[t - 2], cotangent_parts[t - 2])
        state = (second_pieces, second_partners, cotangent_partners, cotangent_parts, picks)
        state = (state, came, backs, returned, settled_own, settled_partner)
        state = fence((state, moved, moving, moved_own, moved_partner, grad_step, kept))
        state, moved, moving, moved_own, moved_partner, grad_step, kept = state
        state, came, backs, returned, settled_own, settled_partner = state
        second_pieces, second_partners, cotangent_partners, cotangent_parts, picks = state

    grad_hidden, grad_hidden_low, grad_logits_low, second_gain_term = call(
        functools.partial(router_back_kernel, experts),
        (
            shape((count, model), f32),
            shape((count, model), bf16),
            shape((count, lanes), bf16),
            shape((1, model), f32),
        ),
        mebibytes=60,
    )(
        settled_own[0],
        settled_partner[0],
        grad_step,
        cotangent,
        hidden,
        second_gain_row,
        router_wide,
        mask,
        prob,
        gates,
    )
    grad_attn_low = jnp.concatenate(gather_chips(grad_hidden_low), axis=0)
    moved_step = shift_outer((moved_own[1] + moved_partner[1].astype(f32)).astype(bf16))
    kept_late = [fence((kept[s], grad_hidden_low))[0] for s in range(outer)]
    total_slots = outer * slots
    row_tile = pl.BlockSpec((part_rows, unit_tile), lambda i: (0, i))
    unit_once = pl.BlockSpec((slots, hidden_units), lambda i: (0, 0))
    gate_grad, up_grad, down_grad = call(
        functools.partial(expert_grad_kernel, outer, chips),
        (
            shape((model, hidden_units), f32),
            shape((model, hidden_units), f32),
            shape((hidden_units, model), f32),
        ),
        mebibytes=60,
        micros=20,
        grid=(model // unit_tile,),
        in_specs=[row_tile] * (2 * outer * chips) + [unit_once] * (3 * outer),
        out_specs=[
            pl.BlockSpec((unit_tile, hidden_units), lambda i: (i, 0)),
            pl.BlockSpec((unit_tile, hidden_units), lambda i: (i, 0)),
            pl.BlockSpec((hidden_units, unit_tile), lambda i: (0, i)),
        ],
        scratch_shapes=[pltpu.VMEM((total_slots, unit_tile), bf16)] * 2
        + [pltpu.VMEM((total_slots, hidden_units), bf16)] * 3,
    )(
        *[part for i in range(2) for keep in kept_late for part in keep[i]],
        *[keep[i] for i in range(2, 5) for keep in kept_late],
    )


    state = (grad_attn_low, gate_grad, up_grad, down_grad, moved_step, grad_logits_low)
    grad_attn_low, gate_grad, up_grad, down_grad, moved_step, grad_logits_low = fence(state)

    def next_step(step, *parts):
        total = step.astype(f32)
        for part in parts:
            total = total + part.astype(f32)
        return shift_outer(total.astype(bf16))

    out_send, out_keep = (
        lax.dot_general(
            context, grad_attn_low, CONTRACT_ROWS, preferred_element_type=f32
        ).astype(bf16)
        for context in (context_other, context_own)
    )
    out_swapped = swap_core(out_send)
    grad_context_own, grad_context_other = (
        lax.dot_general(
            grad_attn_low, weight, CONTRACT_LAST, preferred_element_type=f32
        ).astype(bf16)
        for weight in (out_own, out_other)
    )
    moved_own[2], partner = settle(picks[2], after(moved[2], out_send))
    moved_partner[2] = swap_core(partner)
    state = (out_keep, out_swapped, grad_context_own, grad_context_other)
    state, moved_own, moved_partner = fence((state, moved_own, moved_partner))
    out_keep, out_swapped, grad_context_own, grad_context_other = state
    out_half = (out_keep.astype(f32) + out_swapped.astype(f32)).astype(bf16)
    out_half = out_half.reshape(chips, span * rows_out, model)
    out_came = [swap_chip(out_half[r], r) for r in range(chips)]
    moved_step = next_step(moved_step, moved_own[2], moved_partner[2])
    grad_front_low, gain_terms = call(
        functools.partial(attend_back_kernel, scale),
        (shape((together, columns), bf16), shape((2, width), f32)),
        micros=18,
        grid=(chips,),
        in_specs=[
            blocks(columns),
            blocks(group_columns),
            blocks(width),
            blocks(width),
            blocks(half_columns),
            blocks(half_columns),
            blocks(width),
            blocks(width),
            blocks(count),
            once,
            once,
            order_once,
        ],
        out_specs=[blocks(columns), pl.BlockSpec((2, width), lambda b: (0, 0))],
        scratch_shapes=[pltpu.VMEM((count, group_columns), bf16)],
    )(
        projected,
        query_low,
        key_low,
        value_low,
        grad_context_own,
        grad_context_other,
        cosine_table,
        sine_table,
        allowed,
        query_gain_row,
        key_gain_row,
        out_order,
    )

    grad_front_low, gain_terms, out_came, moved_step, grad_logits_low = fence(
        (grad_front_low, gain_terms, out_came, moved_step, grad_logits_low)
    )

    half_model = model // CORES
    front_send, front_keep = (
        lax.dot_general(
            normed_low[:, k * half_model : (k + 1) * half_model],
            grad_front_low,
            CONTRACT_ROWS,
            preferred_element_type=f32,
        ).astype(bf16)
        for k in (1, 0)
    )
    front_swapped = swap_core(front_send)
    out_parts = [
        part[u * rows_out : (u + 1) * rows_out]
        for part in after(out_came, front_send)
        for u in range(span)
    ]
    target = (my_outer - jnp.arange(outer, dtype=i32)) % outer
    out_places = ((target // span) ^ my_chip) * span + target % span
    out_home, *out_away = call(
        choose_kernel,
        [shape((rows_out, model), bf16)] * outer,
        in_specs=[smem] + [vmem] * outer,
    )(out_places, *out_parts)
    out_step = shift_outer(out_away[0])
    for s in range(3, outer):
        moved[s] = spread(moving[s])
    state = (front_keep, front_swapped, moved, out_step, out_home, out_away)
    front_keep, front_swapped, moved, out_step, out_home, out_away = fence(state)
    front_half = call(add_kernel, [shape((chips * depth, columns), bf16)] * outer)(
        front_keep, front_swapped
    )

    def next_sum(step, part):
        return shift_outer(call(add_kernel, [shape(part.shape, bf16)])(step, part)[0])

    front_step = shift_outer(front_half[1])
    out_step = next_sum(out_step, out_away[1])
    piece_block = pl.BlockSpec((chips * depth, columns), lambda s, o: (0, 0))
    grad_normed = pl.pallas_call(
        functools.partial(project_back_kernel, outer, chips),
        out_shape=[shape((count, model), bf16)] * chips,
        grid_spec=pltpu.PrefetchScalarGridSpec(
            num_scalar_prefetch=1,
            grid=(outer,),
            in_specs=[
                pl.BlockSpec((together, columns), lambda s, o: (0, 0)),
                *[piece_block] * (CORES * outer),
                pl.BlockSpec((plane * depth, plane * depth), lambda s, o: (0, 0)),
            ],
            out_specs=[
                pl.BlockSpec(
                    (count, plane * depth), lambda s, o: (0, lax.rem(o[0] + outer - s, outer))
                )
            ]
            * chips,
        ),
        compiler_params=pltpu.CompilerParams(vmem_limit_bytes=32 * MEBIBYTE),
    )(
        outer_scalar,
        after(grad_front_low, *front_half),
        *front_pieces,
        *front_others,
        front_order,
    )
    first_gain_term = call(gain_back_kernel, shape((1, model), f32))(*grad_normed, *token_parts)
    gain_sums = jnp.concatenate(
        [first_gain_term.reshape(-1), second_gain_term.reshape(-1), gain_terms.reshape(-1)]
    ).reshape(-1, LANES)
    gain_sums = gain_sums + swap_core(gain_sums)
    for s in range(3, outer):
        moved_own[s], partner = settle(picks[s], moved[s])
        moved_partner[s] = swap_core(partner)
    state = (front_half, front_step, out_step, grad_normed, moved_own, moved_partner)
    state, gain_sums = fence((state, gain_sums))
    front_half, front_step, out_step, grad_normed, moved_own, moved_partner = state
    front_step = next_sum(front_step, front_half[2])
    for s in range(3, outer):
        out_step = next_sum(out_step, out_away[s - 1])
    arrived = [swap_chip(grad_normed[r], r) for r in range(1, chips)]
    router_part = lax.dot_general(
        after(grad_logits_low, *grad_normed)[:, :experts],
        second_wide[:, :model],
        CONTRACT_ROWS,
        preferred_element_type=f32,
    )
    router_part = scatter_outer(
        lambda o: lax.dynamic_slice_in_dim(router_part, o * (plane * depth), plane * depth, 1)
    )
    state = (front_step, out_step, arrived, router_part)
    front_step, out_step, arrived, router_part = fence(state)
    for s in range(3, outer):
        front_step = next_sum(front_step, front_half[s])
        moved_step = next_step(moved_step, moved_own[s], moved_partner[s])
    moved[0] = spread(moving[0])
    tokens_grad = call(tokens_back_kernel, shape((count, model), f32))(
        tokens, grad_normed[0], *arrived, grad_hidden, first_gain_row
    )
    gain_sums = sum([swap_chip(gain_sums, r) for r in range(1, chips)], gain_sums)
    router_part = sum(
        [
            swap_chip(
                lax.dynamic_slice_in_dim(
                    router_part, (my_chip ^ r) * (CORES * depth), CORES * depth, 1
                ),
                r,
            )
            for r in range(chips)
        ]
    )
    out_grad = out_step.astype(f32) + out_home.astype(f32)
    state = (front_step, moved_step, moved, gain_sums, router_part, tokens_grad, out_grad)
    front_step, moved_step, moved, gain_sums, router_part, tokens_grad, out_grad = fence(state)
    moved_own[0], partner = settle(picks[0], moved[0])
    moved_partner[0] = swap_core(partner)
    output = hidden + moved_own[0] + moved_partner[0].astype(f32) + moved_step.astype(f32)
    output = output.astype(bf16)
    front = (front_step.astype(f32) + front_half[0].astype(f32)).astype(bf16)
    front = front.reshape(chips, depth, columns)
    front = [swap_chip(front[r], r) for r in range(chips)]
    front, gain_sums, router_part = fence((front, gain_sums, router_part))
    gain_sums = sum([shift_outer(gain_sums, s) for s in range(1, outer)], gain_sums).reshape(-1)
    router_grad = (
        lax.dynamic_slice_in_dim(router_part, my_core * depth, depth, 1)
        + swap_core(lax.dynamic_slice_in_dim(router_part, (1 - my_core) * depth, depth, 1))
    ).T
    front = by_chip(front)

    def lay_out(first, last):
        return jnp.concatenate([part[:, first:last] for part in front], axis=1).astype(f32)

    query_grad = lay_out(0, group_columns)
    key_grad = lay_out(group_columns, group_columns + width)
    value_grad = lay_out(group_columns + width, columns)
    return (
        output,
        tokens_grad,
        query_grad,
        key_grad,
        value_grad,
        out_grad,
        router_grad,
        gate_grad[None],
        up_grad[None],
        down_grad[None],
        gain_sums[:model],
        gain_sums[model : 2 * model],
        gain_sums[2 * model : 2 * model + width],
        gain_sums[2 * model + width :],
    )


def solution(mesh):
    rows = P("fsdp", None)
    blocks = P("fsdp", None, None)
    placed = (rows,) * 9 + (blocks,) * 3 + (P(),) * 4
    return jax.shard_map(
        body,
        mesh=mesh,
        in_specs=placed,
        out_specs=(rows,) * 7 + (blocks,) * 3 + (P(),) * 4,
        check_vma=False,
    )
```
